128 devices in a mesh: lat: 4 (over x), lon: 32 (over z, y, core).
Axes of the slice: x: 4, y: 4, z: 4, core: 2. Of those that a mesh axis runs over, the one named last changes fastest.
Arguments:
- grid_field: bfloat16 [128, 4096, 192], P('lat', 'lon'), may hold values from -6 to 6
- conv_weight: bfloat16 [9, 192, 192], replicated, may hold values from -0.15625 to 0.15625
- observed: float32 [32768, 128], P(('lat', 'lon')), may hold values from -6 to 6
- hidden_mask: int32 [32768, 128], P(('lat', 'lon')), may hold values 0 or 1
- tile_route: int32 [32768, 1], P(('lat', 'lon')), may hold values from 0 to 127; in each aligned block of 256 rows (0 to 255, 256 to 511, ...) at most 4 rows name the same one
- station_spot: int32 [32768], P(('lat', 'lon')), may hold values from 0 to 62991
- neighbours: int32 [32768, 16], P(('lat', 'lon')), may hold values from 0 to 255
- neighbour_count: int32 [32768], P(('lat', 'lon')), may hold values from 2 to 16
- edge_bias: float32 [32768, 16], P(('lat', 'lon')), may hold values from -9 to 300
- live_count: int32 [128], P(('lat', 'lon')), may hold values from 32 to 256, as said below
- in_weight: bfloat16 [448, 192], replicated, may hold values from -0.25 to 0.25
- norm_gain: float32 [192], replicated, may hold values from 0.1 to 1.9
- qkv_weight: bfloat16 [192, 576], replicated, may hold values from -0.4375 to 0.4375
- out_weight: bfloat16 [192, 192], replicated, may hold values from -0.4375 to 0.4375
- final_gain: float32 [192], replicated, may hold values from 0.1 to 1.9
- head_weight: bfloat16 [192, 128], replicated, may hold values from -0.4375 to 0.4375
Outputs:
- predicted: float32 [32768, 128], P(('lat', 'lon'))
- grid_gradient: float32 [128, 4096, 192], P('lat', 'lon')
The draws below stay inside these ranges and needn't reach their ends.
Inputs may be any that keep to these rules, and one draw needn't show every extreme that they name: `tile_route`: within the stations of one region no tile is named by more than 4 stations, and some tile reaches 4 in every draw. `neighbours`: entries at positions j >= neighbour_count are padding. Stations 0 to live_count - 1 of a region are present; some region has all 256 in every draw.
All inputs are finite; a program needn't handle non-finite values. No bound on the sum of `hidden_mask` on one device may be relied on, other than what follows from the above.
Results may differ from the reference program's by a relative error of at most 0.02.
Values may be sent and summed in bfloat16 or wider, within the bound.
A program may use at most 192 MiB of HBM per device.

```python
import math
import jax
import jax.numpy as jnp
import numpy as np
from jax import lax

CHANNELS = 192
FEATURES = 128
HEADS = 3
NEIGHBOURS = 16
TILE_LAT = 32
TILE_LON = 128
SLOTS = 256
HEAD_DIM = 64
REGIONS = 128
STATIONS = 32768
GRID_LAT = 128
GRID_LON = 4096
CAPACITY = 4
N_LON = 32


def draw_live_count(key, part):
    first_key, second_key = jax.random.split(jax.random.fold_in(key, 7))
    halvings = jax.random.randint(first_key, (REGIONS,), 0, 4).astype(jnp.int32)
    counts = jnp.right_shift(jnp.full((REGIONS,), SLOTS, jnp.int32), halvings)
    fullest = jax.random.randint(second_key, (), 0, REGIONS)
    return jnp.where(jnp.arange(REGIONS) == fullest, SLOTS, counts).astype(jnp.int32)


def draw_edge_bias(key, part):
    keys = jax.random.split(jax.random.fold_in(key, 13), 1)
    return 1.5 * jnp.clip(jax.random.normal(keys[0], (STATIONS, NEIGHBOURS), jnp.float32), -6.0, 6.0)


def set_ends(entries, key, smallest, high):
    longest = entries.shape.index(max(entries.shape))
    spots = []
    for shift in (0, 1):
        where = [jax.random.randint(jax.random.fold_in(key, axis), (), 0, length) for axis, length in enumerate(entries.shape)]
        where[longest] = (where[longest] + shift) % entries.shape[longest]
        spots.append(tuple(where))
    return entries.at[spots[0]].set(smallest).at[spots[1]].set(high)


def block_levels(own_key, shape, cuts, smallest, largest):
    factor_of, own = 1.0, jax.random.fold_in(own_key, 6)
    for axis_at, parts in cuts:
        draws = jnp.exp(jax.random.uniform(jax.random.fold_in(own, axis_at), (parts,), jnp.float32, smallest / len(cuts), largest / len(cuts)))
        factor_of = factor_of * jnp.repeat(draws, shape[axis_at] // parts).reshape([-1 if axis == axis_at else 1 for axis in range(len(shape))])
    return factor_of


def shared_out(rng, own, number, rows, amount, top, most, lean):
    order = jax.random.permutation(rng, amount)
    packed, usual = shares(amount, rows * top, most, lean, True), shares(amount, rows * top, most, lean, False)
    places = jnp.arange(amount)

    def named(tallies, turn):
        used = int((tallies > 0).sum())
        fixed = max(1, used // 4)
        moved = fixed + (places - fixed + turn * (used - fixed)) % max(1, amount - fixed)
        return jnp.zeros((amount,), jnp.int32).at[order[jnp.where(places < fixed, places, moved)]].set(jnp.asarray(tallies, jnp.int32))

    tallies = jnp.where(number % 4 == 0, named(packed, number // 4), named(usual, number - number // 4 - 1))
    mixed = jax.random.permutation(jax.random.fold_in(own, 3), amount)
    donor, sink = mixed[0:amount // 2 * 2:2], mixed[1:amount // 2 * 2:2]
    margin = jnp.minimum(tallies[donor] - 1, most - tallies[sink]) // 2
    margin = jnp.where((donor == order[0]) | (sink == order[0]) | (tallies[sink] == 0), 0, jnp.maximum(margin, 0))
    moved = jax.random.randint(jax.random.fold_in(own, 4), (amount // 2,), 0, 1 << 20) % (margin + 1)
    tallies = tallies.at[donor].add(-moved).at[sink].add(moved)
    items = jnp.searchsorted(jnp.cumsum(tallies), jnp.arange(rows * top), side="right").astype(jnp.int32)
    listing = items.reshape(top, rows).T
    listing = listing[jax.random.permutation(jax.random.fold_in(own, 1), rows)]
    turn = jax.random.randint(jax.random.fold_in(own, 2), (rows, 1), 0, top)
    return jnp.take_along_axis(listing, (jnp.arange(top)[None, :] + turn) % top, axis=1)


def shares(amount, total, most, lean, full):
    weights = [(1 << 20) // math.isqrt(rank ** lean) + 1 for rank in range(1, amount + 1)]
    largest = most if full else min(most, max(-(-total // amount), total * weights[0] // sum(weights)))
    least = 1 if total - largest >= amount - 1 else 0
    holding, spare = [largest] + [least] * (amount - 1), total - largest - least * (amount - 1)
    while spare > 0:
        movable = [i for i in range(1, amount) if holding[i] < largest] or [i for i in range(1, amount) if holding[i] < most]
        whole, budget = sum([weights[i] for i in movable]), spare
        for i in movable:
            more = min(most - holding[i], max(1, budget * weights[i] // whole), spare)
            holding[i] = holding[i] + more
            spare = spare - more
    return np.array(holding)


def scatter_about(key, extent, deviation, limit, shards=(), kind=jnp.bfloat16):
    values = deviation * jax.random.normal(key, extent, jnp.float32)
    if shards:
        values = values * block_levels(key, extent, shards, -0.22, 0.18)
    return jnp.clip(values, -limit, limit).astype(kind)


def setup_inputs(seed: int = 0) -> dict:
    arg_keys = jax.random.split(jax.random.key(seed), 17)
    grid_field = scatter_about(arg_keys[0], (GRID_LAT, GRID_LON, CHANNELS), 1.0, 6.0, ((0, 4), (1, 32)))
    conv_weight = scatter_about(arg_keys[1], (9, CHANNELS, CHANNELS), (9 * CHANNELS) ** -0.5, 0.15625)
    observed = scatter_about(arg_keys[2], (STATIONS, FEATURES), 1.0, 6.0, ((0, 128),), jnp.float32)
    hidden_mask = set_ends((jax.random.randint(arg_keys[3], (STATIONS, FEATURES), 0, 4) < 1).astype(jnp.int32), jax.random.fold_in(arg_keys[3], 1), 0, 1)
    tile_route_keys = jax.random.split(jax.random.fold_in(arg_keys[4], 1), STATIONS // SLOTS)
    tile_route_turns = jax.random.permutation(jax.random.fold_in(arg_keys[4], 3), STATIONS // SLOTS)
    tile_route = jax.vmap(lambda own, number: shared_out(jax.random.fold_in(arg_keys[4], 2), own, number, SLOTS, REGIONS, 1, CAPACITY, 2))(tile_route_keys, tile_route_turns).reshape((STATIONS, 1))
    station_spot = set_ends(jax.random.randint(arg_keys[5], (STATIONS,), 0, 16 * (TILE_LAT - 1) * (TILE_LON - 1)), jax.random.fold_in(arg_keys[5], 1), 0, (16 * (TILE_LAT - 1) * (TILE_LON - 1)) - 1).astype(jnp.int32)
    neighbours = set_ends(jax.random.randint(arg_keys[6], (STATIONS, NEIGHBOURS), 0, SLOTS), jax.random.fold_in(arg_keys[6], 1), 0, SLOTS - 1).astype(jnp.int32)
    neighbour_count = set_ends(jax.random.randint(arg_keys[7], (STATIONS,), 2, NEIGHBOURS + 1), jax.random.fold_in(arg_keys[7], 1), 2, NEIGHBOURS).astype(jnp.int32)
    edge_bias = draw_edge_bias(jax.random.fold_in(arg_keys[16], 71), 0)
    live_count = draw_live_count(jax.random.fold_in(arg_keys[16], 71), 0)
    in_weight = scatter_about(arg_keys[10], (2 * FEATURES + CHANNELS, CHANNELS), (2 * FEATURES + CHANNELS) ** -0.5, 0.25)
    norm_gain = jnp.clip(1.0 + 0.18 * jax.random.normal(arg_keys[11], (CHANNELS,), jnp.float32), 0.1, 1.9)
    qkv_weight = scatter_about(arg_keys[12], (CHANNELS, 3 * CHANNELS), CHANNELS ** -0.5, 0.4375)
    out_weight = scatter_about(arg_keys[13], (CHANNELS, CHANNELS), CHANNELS ** -0.5, 0.4375)
    final_gain = jnp.clip(1.0 + 0.18 * jax.random.normal(arg_keys[14], (CHANNELS,), jnp.float32), 0.1, 1.9)
    head_weight = scatter_about(arg_keys[15], (CHANNELS, FEATURES), CHANNELS ** -0.5, 0.4375)
    return dict(grid_field=grid_field, conv_weight=conv_weight, observed=observed, hidden_mask=hidden_mask, tile_route=tile_route, station_spot=station_spot, neighbours=neighbours, neighbour_count=neighbour_count, edge_bias=edge_bias, live_count=live_count, in_weight=in_weight, norm_gain=norm_gain, qkv_weight=qkv_weight, out_weight=out_weight, final_gain=final_gain, head_weight=head_weight)


EPS = 1e-06

def extend(field):
    wrapped = jnp.concatenate([field[:, -1:], field, field[:, :1]], axis=1)
    return jnp.pad(wrapped, ((1, 1), (0, 0), (0, 0)))

def convolve(extended, taps, tile_rows, tile_cols):
    accumulated = jnp.zeros((tile_rows * tile_cols, taps.shape[2]), jnp.float32)
    for offset in range(9):
        shifted = extended[offset // 3:offset // 3 + tile_rows, offset % 3:offset % 3 + tile_cols]
        accumulated = accumulated + jnp.dot(shifted.reshape(tile_rows * tile_cols, -1), taps[offset], preferred_element_type=jnp.float32)
    return accumulated.reshape(tile_rows, tile_cols, -1)

def locate(spots, tile_cols):
    fine_width = 4 * (tile_cols - 1)
    fine_row = spots // fine_width
    fine_col = spots % fine_width
    frac_row = ((fine_row % 4).astype(jnp.float32) + 0.5) / 4.0
    frac_col = ((fine_col % 4).astype(jnp.float32) + 0.5) / 4.0
    return (fine_row // 4, fine_col // 4, frac_row, frac_col)

def rms_scale(values, gain):
    return values * lax.rsqrt(lax.optimization_barrier(jnp.mean(values * values, axis=1, keepdims=True)) + EPS) * gain

def station_forward(interp_rows, observed, hidden_mask, neighbours, valid, edge_bias, alive, in_weight, norm_gain, qkv_weight, out_weight, final_gain, head_weight):
    station_rows = observed.shape[0]
    mask_float = hidden_mask.astype(jnp.float32)
    joined = jnp.concatenate([observed * (1.0 - mask_float), mask_float, interp_rows], axis=1).astype(jnp.bfloat16)
    embedded = jnp.dot(joined, in_weight, preferred_element_type=jnp.float32)
    normed = rms_scale(embedded, norm_gain).astype(jnp.bfloat16)
    projected = jnp.dot(normed, qkv_weight, preferred_element_type=jnp.float32).astype(jnp.bfloat16)
    query_rows = projected[:, :CHANNELS].reshape(station_rows, HEADS, HEAD_DIM).astype(jnp.float32)
    key_rows = projected[:, CHANNELS:2 * CHANNELS]
    value_rows = projected[:, 2 * CHANNELS:]
    near_keys = key_rows[neighbours].reshape(station_rows, -1, HEADS, HEAD_DIM).astype(jnp.float32)
    near_values = value_rows[neighbours].reshape(station_rows, -1, HEADS, HEAD_DIM).astype(jnp.float32)
    own_keys = key_rows.reshape(station_rows, HEADS, HEAD_DIM).astype(jnp.float32)
    own_values = value_rows.reshape(station_rows, HEADS, HEAD_DIM).astype(jnp.float32)
    score_scale = 1.0 / jnp.sqrt(jnp.float32(HEAD_DIM))
    near_score = jnp.einsum('shd,skhd->shk', query_rows, near_keys) * score_scale + edge_bias[:, None, :]
    near_score = jnp.where(valid[:, None, :], near_score, -1e+30)
    own_score = jnp.einsum('shd,shd->sh', query_rows, own_keys) * score_scale
    top_score = jnp.maximum(lax.optimization_barrier(jnp.max(near_score, axis=2)), own_score)
    near_weight = jnp.exp(near_score - top_score[:, :, None])
    own_weight = jnp.exp(own_score - top_score)
    weight_sum = lax.optimization_barrier(jnp.sum(near_weight, axis=2)) + own_weight
    near_prob = (near_weight / weight_sum[:, :, None]).astype(jnp.bfloat16).astype(jnp.float32)
    own_prob = (own_weight / weight_sum).astype(jnp.bfloat16).astype(jnp.float32)
    mixed_rows = jnp.einsum('shk,skhd->shd', near_prob, near_values) + own_prob[:, :, None] * own_values
    mixed_rows = mixed_rows.reshape(station_rows, CHANNELS).astype(jnp.bfloat16)
    residual = embedded + jnp.dot(mixed_rows, out_weight, preferred_element_type=jnp.float32)
    final_rows = rms_scale(residual, final_gain).astype(jnp.bfloat16)
    return jnp.dot(final_rows, head_weight, preferred_element_type=jnp.float32) * alive[:, None]

def reference(grid_field, conv_weight, observed, hidden_mask, tile_route, station_spot, neighbours, neighbour_count, edge_bias, live_count, in_weight, norm_gain, qkv_weight, out_weight, final_gain, head_weight):
    pre_act = convolve(extend(grid_field), conv_weight, GRID_LAT, GRID_LON)
    field = (grid_field.astype(jnp.float32) + jax.nn.silu(pre_act)).astype(jnp.bfloat16)
    tiles = tile_route[:, 0]
    cell_row, cell_col, frac_row, frac_col = locate(station_spot, TILE_LON)
    grid_row = tiles // N_LON * TILE_LAT + cell_row
    grid_col = tiles % N_LON * TILE_LON + cell_col
    corner_weights = [(1.0 - frac_row) * (1.0 - frac_col), (1.0 - frac_row) * frac_col, frac_row * (1.0 - frac_col), frac_row * frac_col]
    corner_rows = [grid_row, grid_row, grid_row + 1, grid_row + 1]
    corner_cols = [grid_col, grid_col + 1, grid_col, grid_col + 1]
    blended = corner_weights[0][:, None] * field[corner_rows[0], corner_cols[0]].astype(jnp.float32)
    for corner in range(1, 4):
        blended = blended + corner_weights[corner][:, None] * field[corner_rows[corner], corner_cols[corner]].astype(jnp.float32)
    interp = blended.astype(jnp.bfloat16)

    def region_pass(region_items):
        interp_r, observed_r, mask_r, neighbours_r, counts_r, bias_r, live_r = region_items
        local_index = jnp.arange(SLOTS, dtype=jnp.int32)
        alive = (local_index < live_r).astype(jnp.float32)
        valid = (jnp.arange(NEIGHBOURS, dtype=jnp.int32)[None, :] < counts_r[:, None]) & (neighbours_r < live_r)

        def forward(interp_rows):
            return station_forward(interp_rows, observed_r, mask_r, neighbours_r, valid, bias_r, alive, in_weight, norm_gain, qkv_weight, out_weight, final_gain, head_weight)
        predicted_r, pullback = jax.vjp(forward, interp_r.astype(jnp.float32))
        d_pred = 2.0 * alive[:, None] * mask_r.astype(jnp.float32) * (predicted_r - observed_r)
        return (predicted_r, pullback(d_pred)[0])
    predicted, d_interp = lax.map(region_pass, (interp.reshape(REGIONS, SLOTS, CHANNELS), observed.reshape(REGIONS, SLOTS, FEATURES), hidden_mask.reshape(REGIONS, SLOTS, FEATURES), neighbours.reshape(REGIONS, SLOTS, NEIGHBOURS), neighbour_count.reshape(REGIONS, SLOTS), edge_bias.reshape(REGIONS, SLOTS, NEIGHBOURS), live_count))
    d_interp = d_interp.reshape(STATIONS, CHANNELS)
    d_field = jnp.zeros((GRID_LAT, GRID_LON, CHANNELS), jnp.float32)
    for corner in range(4):
        d_field = d_field.at[corner_rows[corner], corner_cols[corner]].add(corner_weights[corner][:, None] * d_interp)
    gate_sigmoid = jax.nn.sigmoid(pre_act)
    d_pre = (d_field * gate_sigmoid * (1.0 + pre_act * (1.0 - gate_sigmoid))).astype(jnp.bfloat16)
    flipped = jnp.transpose(conv_weight, (0, 2, 1))[::-1]
    grid_gradient = d_field + convolve(extend(d_pre), flipped, GRID_LAT, GRID_LON)
    return (predicted.reshape(STATIONS, FEATURES), grid_gradient)
```

```python
import math

import jax
import jax.numpy as jnp
from jax import lax
from jax.experimental import pallas as pl
from jax.experimental.pallas import tpu as pltpu
from jax.sharding import Mesh
from jax.sharding import PartitionSpec as P

CHANNELS = 192
HEADS = 3
HEAD_DIM = 64
LON = ("lon_0", "lon_1", "lon_2")
LAT_LON = ("lat", "lon_0", "lon_1", "lon_2")


EPS = 1e-06


def direct_exchange(pieces, number):
    peers, rows, lanes = pieces.shape
    sizes = [lax.axis_size(a) for a in LAT_LON]

    def kernel(x_ref, o_ref, held, send_sem, recv_sem):
        me = lax.axis_index("lat")
        for axis in LAT_LON[1:]:
            me = me * lax.axis_size(axis) + lax.axis_index(axis)

        def coords(p):
            found = []
            for size in reversed(sizes):
                found.append(lax.rem(p, size))
                p = p // size
            return tuple(reversed(found))

        barrier = pltpu.get_barrier_semaphore()

        def greet(i, carry):
            peer = lax.rem(me + i, peers)
            pl.semaphore_signal(
                barrier, inc=1, device_id=coords(peer), device_id_type=pl.DeviceIdType.MESH
            )
            return carry

        lax.fori_loop(1, peers, greet, 0)
        pl.semaphore_wait(barrier, peers - 1)

        def send(i, carry):
            peer = lax.rem(me + i, peers)
            pltpu.make_async_remote_copy(
                src_ref=x_ref.at[peer],
                dst_ref=held.at[me],
                send_sem=send_sem,
                recv_sem=recv_sem,
                device_id=coords(peer),
                device_id_type=pl.DeviceIdType.MESH,
            ).start()
            return carry

        lax.fori_loop(1, peers, send, 0)
        held[me] = x_ref[me]
        rest = held.at[pl.ds(0, peers - 1)]
        pltpu.make_async_copy(rest, rest, recv_sem).wait()
        pltpu.make_async_copy(rest, rest, send_sem).wait()
        o_ref[...] = held[...]

    return pl.pallas_call(
        kernel,
        out_shape=jax.ShapeDtypeStruct(pieces.shape, pieces.dtype),
        in_specs=[pl.BlockSpec(memory_space=pltpu.VMEM)],
        out_specs=pl.BlockSpec(memory_space=pltpu.VMEM),
        scratch_shapes=[
            pltpu.VMEM(pieces.shape, pieces.dtype),
            pltpu.SemaphoreType.DMA,
            pltpu.SemaphoreType.DMA,
        ],
        compiler_params=pltpu.CompilerParams(
            collective_id=number, has_side_effects=True, vmem_limit_bytes=16 << 20
        ),
        name=f"exchange_{number}",
    )(pieces)


def send_rows(rows, number):
    regions, capacity, channels = rows.shape
    wide = jnp.pad(rows, ((0, 0), (0, 0), (0, 256 - channels)))
    pieces = wide.reshape(regions, capacity * 2, 128)
    back = direct_exchange(pieces, number)
    return back.reshape(regions, capacity, 256)[:, :, :channels]


def padded(cells, sides, width):
    for axis, dim in sides:
        count = lax.axis_size(axis)
        head = lax.slice_in_dim(cells, 0, width, axis=dim)
        tail = lax.slice_in_dim(cells, cells.shape[dim] - width, cells.shape[dim], axis=dim)
        cells = jnp.concatenate(
            [
                lax.ppermute(tail, axis, [(i, (i + 1) % count) for i in range(count)]),
                cells,
                lax.ppermute(head, axis, [((i + 1) % count, i) for i in range(count)]),
            ],
            axis=dim,
        )
    return cells


def split_up(value, dim, peers):
    before, after = (value.shape[:dim], value.shape[dim + 1 :])
    return jnp.moveaxis(value.reshape(*before, peers, -1, *after), dim, 0)


def in_order(pieces, dim):
    shape = list(pieces.shape[1:])
    shape[dim] *= pieces.shape[0]
    return jnp.moveaxis(pieces, 0, dim).reshape(shape)


def turned_blocks(pieces, axes, sequence):
    inside = pieces.shape[1:]
    whole = pieces.reshape(*(lax.axis_size(a) for a in axes), *inside)
    for k in sequence:
        whole = lax.all_to_all(whole, axes[k], k, k, tiled=True)
    return whole.reshape(-1, *inside)


def exchange_by_chip(value, groups, sequence, split_dim, concat_dim):
    peers = lax.axis_size(groups[0]) * lax.axis_size(groups[1])
    pieces = split_up(value, split_dim, peers)
    return in_order(turned_blocks(pieces, groups, sequence), concat_dim)


def seal_poles(extended):
    position = lax.axis_index("lat")
    last_index = lax.axis_size("lat") - 1
    keep = jnp.ones((extended.shape[0],), extended.dtype)
    keep = keep.at[0].set(jnp.where(position > 0, 1.0, 0.0).astype(extended.dtype))
    keep = keep.at[extended.shape[0] - 1].set(
        jnp.where(position < last_index, 1.0, 0.0).astype(extended.dtype)
    )
    return extended * keep[:, None, None]


def convolve(extended, taps, tile_rows, tile_cols, contract, reverse_taps):
    ext_rows, ext_cols, channels = extended.shape
    flat = extended.reshape(ext_rows * ext_cols, channels)
    products = lax.dot_general(
        flat, taps, (((1,), (contract,)), ((), ())), preferred_element_type=jnp.float32
    )
    products = products.reshape(ext_rows, ext_cols, 9, -1)
    total = None
    for offset in range(9):
        tap_index = 8 - offset if reverse_taps else offset
        term = products[
            offset // 3 : offset // 3 + tile_rows, offset % 3 : offset % 3 + tile_cols, tap_index
        ]
        total = term if total is None else total + term
    return total


def locate(spots, tile_cols):
    fine_width = 4 * (tile_cols - 1)
    fine_row = spots // fine_width
    fine_col = spots % fine_width
    base_cell = fine_row // 4 * tile_cols + fine_col // 4
    frac_row = ((fine_row % 4).astype(jnp.float32) + 0.5) / 4.0
    frac_col = ((fine_col % 4).astype(jnp.float32) + 0.5) / 4.0
    cells = jnp.stack(
        [base_cell, base_cell + 1, base_cell + tile_cols, base_cell + tile_cols + 1], axis=-1
    )
    weights = jnp.stack(
        [
            (1.0 - frac_row) * (1.0 - frac_col),
            (1.0 - frac_row) * frac_col,
            frac_row * (1.0 - frac_col),
            frac_row * frac_col,
        ],
        axis=-1,
    )
    return (cells, weights)


def blend(parts, weights):
    blended = weights[..., 0:1] * parts[..., 0, :]
    for corner in range(1, 4):
        blended = blended + weights[..., corner : corner + 1] * parts[..., corner, :]
    return blended


def rms_scale(values, gain):
    return values * lax.rsqrt(jnp.mean(values * values, axis=1, keepdims=True) + EPS) * gain


def station_forward(
    interp_rows,
    observed,
    hidden_mask,
    neighbours,
    valid,
    edge_bias,
    alive,
    in_weight,
    norm_gain,
    qkv_weight,
    out_weight,
    final_gain,
    head_weight,
):
    station_rows = observed.shape[0]
    mask_float = hidden_mask.astype(jnp.float32)
    joined = jnp.concatenate(
        [observed * (1.0 - mask_float), mask_float, interp_rows], axis=1
    ).astype(jnp.bfloat16)
    embedded = jnp.dot(joined, in_weight, preferred_element_type=jnp.float32)
    normed = rms_scale(embedded, norm_gain).astype(jnp.bfloat16)
    projected = jnp.dot(normed, qkv_weight, preferred_element_type=jnp.float32).astype(jnp.bfloat16)
    query_rows = projected[:, :CHANNELS].reshape(station_rows, HEADS, HEAD_DIM)
    key_rows = projected[:, CHANNELS : 2 * CHANNELS]
    value_rows = projected[:, 2 * CHANNELS :]
    near_keys = key_rows[neighbours].reshape(station_rows, -1, HEADS, HEAD_DIM)
    near_values = value_rows[neighbours].reshape(station_rows, -1, HEADS, HEAD_DIM)
    own_keys = key_rows.reshape(station_rows, HEADS, HEAD_DIM)
    own_values = value_rows.reshape(station_rows, HEADS, HEAD_DIM)
    score_scale = 1.0 / math.sqrt(HEAD_DIM)
    near_score = (
        jnp.einsum("shd,skhd->shk", query_rows, near_keys, preferred_element_type=jnp.float32)
        * score_scale
        + edge_bias[:, None, :]
    )
    near_score = jnp.where(valid[:, None, :], near_score, -1e30)
    own_score = (
        jnp.einsum("shd,shd->sh", query_rows, own_keys, preferred_element_type=jnp.float32)
        * score_scale
    )
    top_score = jnp.maximum(jnp.max(near_score, axis=2), own_score)
    near_weight = jnp.exp(near_score - top_score[:, :, None])
    own_weight = jnp.exp(own_score - top_score)
    weight_sum = jnp.sum(near_weight, axis=2) + own_weight
    near_prob = (near_weight / weight_sum[:, :, None]).astype(jnp.bfloat16)
    own_prob = (own_weight / weight_sum).astype(jnp.bfloat16)
    mixed_rows = jnp.einsum(
        "shk,skhd->shd", near_prob, near_values, preferred_element_type=jnp.float32
    )
    mixed_rows = mixed_rows + own_prob.astype(jnp.float32)[:, :, None] * own_values.astype(
        jnp.float32
    )
    mixed_rows = mixed_rows.reshape(station_rows, CHANNELS).astype(jnp.bfloat16)
    residual = embedded + jnp.dot(mixed_rows, out_weight, preferred_element_type=jnp.float32)
    final_rows = rms_scale(residual, final_gain).astype(jnp.bfloat16)
    return jnp.dot(final_rows, head_weight, preferred_element_type=jnp.float32) * alive[:, None]


def on_device(
    grid_field,
    conv_weight,
    observed,
    hidden_mask,
    tile_route,
    station_spot,
    neighbours,
    neighbour_count,
    edge_bias,
    live_count,
    in_weight,
    norm_gain,
    qkv_weight,
    out_weight,
    final_gain,
    head_weight,
):
    tile_rows, tile_cols, channels = grid_field.shape
    station_rows = observed.shape[0]
    regions = lax.axis_size("lat") * lax.axis_size(LON)
    capacity = max(2, 2 * station_rows // regions)
    extended = seal_poles(padded(grid_field, (("lat", 0), (LON, 1)), 1))
    pre_act = convolve(extended, conv_weight, tile_rows, tile_cols, 1, False)
    field = (grid_field.astype(jnp.float32) + jax.nn.silu(pre_act)).astype(jnp.bfloat16)
    flat_field = field.reshape(tile_rows * tile_cols, channels)
    target = tile_route[:, 0]
    member = (target[:, None] == jnp.arange(regions, dtype=jnp.int32)[None, :]).astype(jnp.bfloat16)
    station_index = jnp.arange(station_rows, dtype=jnp.int32)
    earlier = (station_index[:, None] > station_index[None, :]).astype(jnp.bfloat16)
    before = jnp.dot(earlier, member, preferred_element_type=jnp.float32)
    rank = jnp.sum(before * member.astype(jnp.float32), axis=1).astype(jnp.int32)
    slot = target * capacity + rank
    requests = (
        jnp.zeros((regions * capacity,), jnp.int32)
        .at[slot]
        .set(station_spot)
        .reshape(regions, capacity)
    )
    wide_requests = jnp.pad(requests, ((0, 0), (0, 128 - capacity))).reshape(regions, 1, 128)
    asked = direct_exchange(wide_requests, 0).reshape(regions, 128)[:, :capacity]
    cells, weights = locate(asked, tile_cols)
    picked = flat_field[cells]
    blended = blend(picked.astype(jnp.float32), weights).astype(jnp.bfloat16)
    answer = send_rows(blended, 1)
    interp = answer.reshape(regions * capacity, channels)[slot]
    live_here = live_count[0]
    alive = (station_index < live_here).astype(jnp.float32)
    valid = (
        jnp.arange(neighbours.shape[1], dtype=jnp.int32)[None, :] < neighbour_count[:, None]
    ) & (neighbours < live_here)

    def forward(interp_rows):
        return station_forward(
            interp_rows,
            observed,
            hidden_mask,
            neighbours,
            valid,
            edge_bias,
            alive,
            in_weight,
            norm_gain,
            qkv_weight,
            out_weight,
            final_gain,
            head_weight,
        )

    predicted, pullback = jax.vjp(forward, interp.astype(jnp.float32))
    d_pred = 2.0 * alive[:, None] * hidden_mask.astype(jnp.float32) * (predicted - observed)
    d_interp = pullback(d_pred)[0]
    received_cells, received_weights = locate(asked, tile_cols)
    outgoing = (
        jnp.zeros((regions * capacity, channels), jnp.float32)
        .at[slot]
        .set(d_interp)
        .reshape(regions, capacity, channels)
    )
    incoming = send_rows(outgoing.astype(jnp.bfloat16), 2).astype(outgoing.dtype)
    spread = received_weights[..., None] * incoming[:, :, None, :]
    d_field = jnp.zeros((tile_rows * tile_cols, channels), jnp.float32)
    d_field = (
        d_field.at[received_cells.reshape(-1)]
        .add(spread.reshape(-1, channels))
        .reshape(tile_rows, tile_cols, channels)
    )
    gate_sigmoid = jax.nn.sigmoid(pre_act)
    d_pre = (d_field * gate_sigmoid * (1.0 + pre_act * (1.0 - gate_sigmoid))).astype(jnp.bfloat16)
    d_ext = seal_poles(padded(d_pre, (("lat", 0), (LON, 1)), 1))
    grid_gradient = d_field + convolve(d_ext, conv_weight, tile_rows, tile_cols, 2, True)
    return (predicted, grid_gradient)


def solution(mesh):
    split = Mesh(
        mesh.devices.reshape(mesh.shape["lat"], 4, 4, 2), ("lat", "lon_0", "lon_1", "lon_2")
    )
    return jax.shard_map(
        on_device,
        mesh=split,
        in_specs=(
            P("lat", LON, None),
            P(),
            P(LAT_LON, None),
            P(LAT_LON, None),
            P(LAT_LON, None),
            P(LAT_LON),
            P(LAT_LON, None),
            P(LAT_LON),
            P(LAT_LON, None),
            P(LAT_LON),
            P(),
            P(),
            P(),
            P(),
            P(),
            P(),
        ),
        out_specs=(P(LAT_LON, None), P("lat", LON, None)),
        check_vma=False,
    )
```

```python
import jax
import jax.numpy as jnp
from jax import lax
from jax.experimental import pallas as pl
from jax.experimental.pallas import tpu as pltpu
from jax.sharding import PartitionSpec as P

CH = 192
HEADS = 3
HEAD_DIM = 64
ROWS = 32
COLS = 128
FINE = 4 * (COLS - 1)
CAP = 4
N = 128
N_LAT = 4
N_LON = 32
SLOTS = N * CAP
STATIONS = 256
TAPS = 9 * CH
DEPTH = TAPS + 2 * ROWS
EPS = 1e-06
F32 = jnp.float32
BF16 = jnp.bfloat16
LAT_LON = ("lat", "lon")


def nn(a, b):
    return lax.dot_general(a, b, (((1,), (0,)), ((), ())), preferred_element_type=F32)


def nt(a, b):
    return lax.dot_general(a, b, (((1,), (1,)), ((), ())), preferred_element_type=F32)


def lane_iota(shape):
    return lax.broadcasted_iota(jnp.int32, shape, len(shape) - 1)


def row_iota(shape):
    return lax.broadcasted_iota(jnp.int32, shape, len(shape) - 2)


def as_columns(row):
    return jnp.transpose(jnp.broadcast_to(row, (128, row.shape[1])))


def kernel(
    x_ref,
    conv_ref,
    observed_ref,
    mask_ref,
    tile_ref,
    spot_ref,
    neighbours_ref,
    count_ref,
    bias_ref,
    live_ref,
    in_ref,
    gain1_ref,
    qkv_ref,
    out_ref,
    gain2_ref,
    head_ref,
    predicted_ref,
    grad_ref,
    shifted,
    taps_f,
    taps_b,
    field,
    slope,
    spread,
    answer_out,
    answer_in,
    grads_out,
    grads_in,
    ask_out,
    ask_in,
    wide,
    row_in,
    side_out,
    side_in,
    corner_in,
    select,
    select_t,
    scores_bias,
    grads_t,
    embedded0,
    gain1,
    gain2,
    in_low,
    in_low_t,
    qkv_t,
    out_t,
    head_t,
    mask_t,
    observed_t,
    halo_send,
    halo_recv,
    a2a_send,
    a2a_recv,
):
    lat = lax.axis_index("lat")
    lon = lax.axis_index("lon")
    me = lat * N_LON + lon
    barrier = pltpu.get_barrier_semaphore()

    def coords(peer):
        return (peer // N_LON, lax.rem(peer, N_LON))

    def greet(i, carry):
        pl.semaphore_signal(
            barrier, inc=1, device_id=coords(lax.rem(me + i, N)), device_id_type=pl.DeviceIdType.MESH
        )
        return carry

    lax.fori_loop(1, N, greet, 0)

    tile_row = tile_ref[...].astype(F32)
    tile_cols = as_columns(tile_row)
    tile_cols = jnp.concatenate([tile_cols, tile_cols], axis=1)
    square = (STATIONS, STATIONS)
    same = (tile_cols == tile_row) & (row_iota(square) < lane_iota(square))
    rank = jnp.sum(same.astype(F32), axis=0, keepdims=True)
    slot = tile_row * CAP + rank
    spot = spot_ref[...].astype(F32)
    spot_high = jnp.floor(spot * (1.0 / 256.0))
    spot_low = spot - 256.0 * spot_high
    part = row_iota((128, STATIONS))
    wanted = jnp.where(part < CAP, spot_high, spot_low)
    wanted = jnp.where((part & (CAP - 1)).astype(F32) == rank, wanted, 0.0)
    wanted = jnp.where(part < 2 * CAP, wanted, 0.0).astype(BF16)
    is_tile = (row_iota((N, STATIONS)).astype(F32) == tile_row).astype(BF16)
    ask_out[...] = nt(is_tile, wanted).reshape(N, 1, 128)

    def fill_shifted(y, value):
        lane = lane_iota((CH, COLS))
        shifted[y, 1] = value.astype(BF16)
        shifted[y, 0] = jnp.where(lane == 0, 0.0, pltpu.roll(value, 1, 1)).astype(BF16)
        shifted[y, 2] = jnp.where(lane == COLS - 1, 0.0, pltpu.roll(value, COLS - 1, 1)).astype(BF16)

    def gather_ends(y, value, ends):
        lane = lane_iota((CH, COLS))
        ends = jnp.where(lane == y, value[:, 0:1], ends)
        return jnp.where(lane == y + ROWS, value[:, COLS - 1 : COLS], ends)

    def put_ends(turn, ends):
        sides = jnp.transpose(ends)[0 : 2 * ROWS].astype(BF16)
        side_out[turn, :, 0:CH] = sides
        side_out[turn, :, CH:] = jnp.zeros((2 * ROWS, 256 - CH), BF16)

    def fill_row(y, ends):
        value = x_ref[y].astype(F32)
        fill_shifted(y + 1, value)
        return gather_ends(y, value, ends)

    ends = lax.fori_loop(0, ROWS, fill_row, jnp.zeros((CH, COLS), F32))
    put_ends(0, ends)

    up, down = lax.rem(lat + N_LAT - 1, N_LAT), lax.rem(lat + 1, N_LAT)
    left, right = lax.rem(lon + N_LON - 1, N_LON), lax.rem(lon + 1, N_LON)

    def halo_copies(turn):
        first, last = shifted.at[1, 1], shifted.at[ROWS, 1]
        mine = side_out.at[turn]
        plan = [
            (first, row_in.at[turn, 1], (up, lon)),
            (last, row_in.at[turn, 0], (down, lon)),
            (mine.at[pl.ds(0, ROWS)], side_in.at[turn, 1], (lat, left)),
            (mine.at[pl.ds(ROWS, ROWS)], side_in.at[turn, 0], (lat, right)),
            (mine.at[pl.ds(0, 16)], corner_in.at[turn, 3], (up, left)),
            (mine.at[pl.ds(ROWS, 16)], corner_in.at[turn, 2], (up, right)),
            (mine.at[pl.ds(16, 16)], corner_in.at[turn, 1], (down, left)),
            (mine.at[pl.ds(ROWS + 16, 16)], corner_in.at[turn, 0], (down, right)),
        ]
        return [
            pltpu.make_async_remote_copy(
                src_ref=source,
                dst_ref=target,
                send_sem=halo_send.at[turn, k],
                recv_sem=halo_recv.at[turn, k],
                device_id=where,
                device_id_type=pl.DeviceIdType.MESH,
            )
            for k, (source, target, where) in enumerate(plan)
        ]

    def start_exchange(turn, source, target):
        def send(i, carry):
            peer = lax.rem(me + i, N)
            pltpu.make_async_remote_copy(
                src_ref=source.at[peer],
                dst_ref=target.at[me],
                send_sem=a2a_send.at[turn],
                recv_sem=a2a_recv.at[turn],
                device_id=coords(peer),
                device_id_type=pl.DeviceIdType.MESH,
            ).start()
            return carry

        lax.fori_loop(1, N, send, 0)
        target[me] = source[me]

    def wait_received(turn, target):
        rest = target.at[pl.ds(0, N - 1)]
        pltpu.make_async_copy(rest, rest, a2a_recv.at[turn]).wait()

    def wait_sent(turn, source):
        rest = source.at[pl.ds(0, N - 1)]
        pltpu.make_async_copy(rest, rest, a2a_send.at[turn]).wait()

    pl.semaphore_wait(barrier, N - 1)
    first_halo = halo_copies(0)
    for copy in first_halo:
        copy.start()
    start_exchange(0, ask_out, ask_in)

    for tap in range(9):
        taps_f[:, CH * tap : CH * (tap + 1)] = jnp.transpose(conv_ref[tap].astype(F32)).astype(BF16)
        taps_b[:, CH * tap : CH * (tap + 1)] = conv_ref[8 - tap]
    select_t[...] = (row_iota((SLOTS, STATIONS)).astype(F32) == slot).astype(BF16)
    slot_cols = as_columns(slot)
    slot_cols = jnp.concatenate([slot_cols] * (SLOTS // 128), axis=1)
    select[...] = (lane_iota((STATIONS, SLOTS)).astype(F32) == slot_cols).astype(BF16)
    for wide_gain, gain in ((gain1, gain1_ref), (gain2, gain2_ref)):
        cols = as_columns(gain[...])
        wide_gain[...] = jnp.concatenate([cols, cols], axis=1)
    observed_t[...] = jnp.transpose(observed_ref[...])
    mask_t[...] = jnp.transpose(mask_ref[...].astype(F32))
    shown = (observed_t[...] * (1.0 - mask_t[...])).astype(BF16)
    embedded0[...] = nn(in_ref[:, 0:128], shown) + nn(in_ref[:, 128:256], mask_t[...].astype(BF16))
    low = in_ref[:, 256:448].astype(F32)
    in_low[...] = jnp.concatenate([low, jnp.zeros((CH, 64), F32)], axis=1).astype(BF16)
    in_low_t[...] = jnp.transpose(low).astype(BF16)
    qkv_t[...] = jnp.transpose(qkv_ref[...].astype(F32)).astype(BF16)
    out_t[...] = jnp.transpose(out_ref[...].astype(F32)).astype(BF16)
    head_t[...] = jnp.transpose(head_ref[...].astype(F32)).astype(BF16)

    live = live_ref[...].astype(F32)
    station = lane_iota((1, STATIONS)).astype(F32)
    near = neighbours_ref[...].astype(F32)
    used = (row_iota((16, STATIONS)).astype(F32) < count_ref[...].astype(F32)) & (near < live)
    near = jnp.where(used, near, -1.0)
    near = jnp.concatenate([near, station, jnp.full((7, STATIONS), -1.0, F32)], axis=0)
    bias = jnp.concatenate([bias_ref[...], jnp.zeros((8, STATIONS), F32)], axis=0)
    top = jnp.full((24, STATIONS), -1e30, F32)
    for j in range(17):
        top = jnp.where(near == near[j : j + 1], jnp.maximum(top, bias[j : j + 1]), top)
    together = jnp.zeros((24, STATIONS), F32)
    for j in range(17):
        together = together + jnp.where(near == near[j : j + 1], jnp.exp(bias[j : j + 1] - top), 0.0)
    level = top + jnp.log(together)
    other = row_iota(square).astype(F32)
    dense = jnp.full(square, -1e30, F32)
    for j in range(17):
        dense = jnp.where(other == near[j : j + 1], level[j : j + 1], dense)
    scores_bias[...] = dense

    wait_received(0, ask_in)
    asked = ask_in[...].reshape(N, 128).astype(BF16)
    repeat = (row_iota((SLOTS, N)) // CAP == lane_iota((SLOTS, N))).astype(BF16)
    asked = nn(repeat, asked)
    place = lane_iota((SLOTS, 128))
    turn_of = row_iota((SLOTS, 128)) & (CAP - 1)
    spots = jnp.where(place == turn_of, asked * 256.0, 0.0) + jnp.where(place == turn_of + CAP, asked, 0.0)
    spots = jnp.sum(spots, axis=1, keepdims=True)
    fine_row = jnp.floor((spots + 0.5) * (1.0 / FINE))
    fine_col = spots - FINE * fine_row
    at_row = jnp.broadcast_to((fine_row + 0.5) * 0.25, (SLOTS, COLS))
    at_col = jnp.broadcast_to((fine_col + 0.5) * 0.25, (SLOTS, COLS))
    along = jnp.maximum(1.0 - jnp.abs(at_col - place.astype(F32)), 0.0).astype(BF16)
    at_row = at_row.astype(BF16)

    def fill_spread(y, carry):
        away = jnp.abs(at_row - y.astype(BF16))
        spread[y] = jnp.maximum(1.0 - away, 0.0).astype(BF16) * along
        return carry

    lax.fori_loop(0, ROWS, fill_spread, 0)

    keep_up = jnp.where(lat > 0, 1.0, 0.0)
    keep_down = jnp.where(lat < N_LAT - 1, 1.0, 0.0)

    def take_halo(turn, copies, taps, backward):
        for copy in copies:
            copy.wait_recv()
        fill_shifted(0, row_in[turn, 0].astype(F32) * keep_up)
        fill_shifted(ROWS + 1, row_in[turn, 1].astype(F32) * keep_down)
        total = []
        for side in range(2):
            above = corner_in[turn, side].astype(F32)[15:16, 0:CH] * keep_up
            below = corner_in[turn, 2 + side].astype(F32)[0:1, 0:CH] * keep_down
            column = jnp.concatenate([above, side_in[turn, side].astype(F32)[:, 0:CH], below], axis=0)
            sums = None
            for i in range(3):
                part = column[i : i + ROWS].astype(BF16)
                if backward:
                    term = nt(part, conv_ref[8 - (3 * i + 2 * side)])
                else:
                    term = nn(part, conv_ref[3 * i + 2 * side])
                sums = term if sums is None else sums + term
            total.append(sums)
        total = jnp.concatenate(total + [jnp.zeros((64, CH), F32)], axis=0)
        taps[:, TAPS:] = jnp.transpose(total)[:, 0 : 2 * ROWS].astype(BF16)

    def around(y):
        ends_at = row_iota((2 * ROWS, COLS))
        lane = lane_iota((2 * ROWS, COLS))
        hit = ((ends_at == y) & (lane == 0)) | ((ends_at == y + ROWS) & (lane == COLS - 1))
        return jnp.concatenate(
            [shifted[pl.ds(y, 3)].reshape(TAPS, COLS), hit.astype(F32).astype(BF16)], axis=0
        )

    take_halo(0, first_halo, taps_f, False)

    def forward_rows(pair, carry):
        y = pair * 2
        pre = nn(taps_f[...], jnp.concatenate([around(y), around(y + 1)], axis=1))
        gate = 1.0 / (1.0 + jnp.exp(-pre))
        moved = pre * gate
        tilt = gate * (1.0 + pre * (1.0 - gate))
        for k in range(2):
            cut = slice(COLS * k, COLS * (k + 1))
            field[y + k] = (x_ref[y + k].astype(F32) + moved[:, cut]).astype(BF16)
            slope[y + k] = tilt[:, cut].astype(BF16)
        return carry

    lax.fori_loop(0, ROWS // 2, forward_rows, 0)

    def send_wide(rows, out):
        wide[pl.ds(0, SLOTS, 2)] = rows[:, 0:128]
        wide[pl.ds(1, SLOTS, 2)] = jnp.concatenate([rows[:, 128:CH], jnp.zeros((SLOTS, 256 - CH), F32)], axis=1)
        out[...] = wide[...].reshape(N, 2 * CAP, 128).astype(BF16)

    def read_wide(held):
        wide[...] = held[...].astype(F32).reshape(2 * SLOTS, 128)
        return wide[pl.ds(0, SLOTS, 2)], wide[pl.ds(1, SLOTS, 2)]

    sampled = jnp.zeros((SLOTS, CH), F32)
    for eighth in range(4):
        rows = [8 * eighth + k for k in range(8)]
        sampled = sampled + nt(
            jnp.concatenate([spread[y] for y in rows], axis=1), jnp.concatenate([field[y] for y in rows], axis=1)
        )
    send_wide(sampled, answer_out)
    start_exchange(1, answer_out, answer_in)
    wait_received(1, answer_in)

    low_part, high_part = read_wide(answer_in)
    answers = jnp.concatenate([low_part, high_part], axis=1).astype(BF16)
    interp = nn(select[...], answers).astype(BF16)
    embedded = embedded0[...] + nt(in_low[...], interp)
    scale1 = lax.rsqrt(jnp.mean(embedded * embedded, axis=0, keepdims=True) + EPS)
    unit1 = embedded * scale1
    projected = nn(qkv_t[...], (unit1 * gain1[...]).astype(BF16)).astype(BF16)
    probs, mixed = [], []
    score_scale = 1.0 / 8.0

    def part_of(kind, head):
        at = kind * CH + head * HEAD_DIM
        return projected[at : at + HEAD_DIM]

    def turned(value):
        return jnp.transpose(value.astype(F32)).astype(BF16)

    for head in range(HEADS):
        score = nn(turned(part_of(1, head)), part_of(0, head)) * score_scale + scores_bias[...]
        weight = jnp.exp(score - jnp.max(score, axis=0, keepdims=True))
        prob = (weight * (1.0 / jnp.sum(weight, axis=0, keepdims=True))).astype(BF16)
        probs.append(prob)
        mixed.append(nn(part_of(2, head), prob))
    mixed = jnp.concatenate(mixed, axis=0).astype(BF16)
    residual = embedded + nn(out_t[...], mixed)
    scale2 = lax.rsqrt(jnp.mean(residual * residual, axis=0, keepdims=True) + EPS)
    unit2 = residual * scale2
    final = (unit2 * gain2[...]).astype(BF16)
    alive = (station < live).astype(F32)
    predicted = nn(head_t[...], final) * alive
    d_pred = (2.0 * alive * mask_t[...] * (predicted - observed_t[...])).astype(BF16)

    d_unit2 = nn(head_ref[...], d_pred) * gain2[...]
    d_residual = scale2 * (d_unit2 - unit2 * jnp.mean(d_unit2 * unit2, axis=0, keepdims=True))
    d_mixed = nn(out_ref[...], d_residual.astype(BF16)).astype(BF16)
    d_query, d_key, d_value = [], [], []
    for head in range(HEADS):
        d_here = d_mixed[head * HEAD_DIM : (head + 1) * HEAD_DIM]
        prob = probs[head]
        d_prob = nn(turned(part_of(2, head)), d_here)
        wide_prob = prob.astype(F32)
        d_score = d_prob - jnp.sum(d_prob * wide_prob, axis=0, keepdims=True)
        d_score = (wide_prob * d_score * score_scale).astype(BF16)
        d_query.append(nn(part_of(1, head), d_score))
        d_key.append(nt(part_of(0, head), d_score))
        d_value.append(nt(d_here, prob))
    d_projected = jnp.concatenate(d_query + d_key + d_value, axis=0).astype(BF16)
    d_unit1 = nn(qkv_ref[...], d_projected) * gain1[...]
    d_embedded = d_residual + scale1 * (d_unit1 - unit1 * jnp.mean(d_unit1 * unit1, axis=0, keepdims=True))
    d_interp = nn(in_low_t[...], d_embedded.astype(BF16)).astype(BF16)
    send_wide(nt(select_t[...], d_interp), grads_out)
    start_exchange(2, grads_out, grads_in)
    predicted_ref[...] = jnp.transpose(predicted)
    for copy in first_halo:
        copy.wait_send()
    wait_received(2, grads_in)

    low_part, high_part = read_wide(grads_in)
    grads_t[0:128] = jnp.transpose(low_part).astype(BF16)
    grads_t[128:CH] = jnp.transpose(high_part)[0 : CH - 128].astype(BF16)

    def scatter_rows(pair, ends):
        y = pair * 2
        both = nn(grads_t[...], jnp.concatenate([spread[y], spread[y + 1]], axis=1))
        for k in range(2):
            value = both[:, COLS * k : COLS * (k + 1)]
            grad_ref[y + k] = value
            value = value * slope[y + k].astype(F32)
            fill_shifted(y + k + 1, value)
            ends = gather_ends(y + k, value, ends)
        return ends

    ends = lax.fori_loop(0, ROWS // 2, scatter_rows, jnp.zeros((CH, COLS), F32))
    put_ends(1, ends)
    second_halo = halo_copies(1)
    for copy in second_halo:
        copy.start()
    take_halo(1, second_halo, taps_b, True)

    def backward_rows(pair, carry):
        y = pair * 2
        back = nn(taps_b[...], jnp.concatenate([around(y), around(y + 1)], axis=1))
        for k in range(2):
            grad_ref[y + k] = grad_ref[y + k] + back[:, COLS * k : COLS * (k + 1)]
        return carry

    lax.fori_loop(0, ROWS // 2, backward_rows, 0)
    for copy in second_halo:
        copy.wait_send()
    wait_sent(0, ask_out)
    wait_sent(1, answer_out)
    wait_sent(2, grads_out)


def on_device(
    grid_field,
    conv_weight,
    observed,
    hidden_mask,
    tile_route,
    station_spot,
    neighbours,
    neighbour_count,
    edge_bias,
    live_count,
    in_weight,
    norm_gain,
    qkv_weight,
    out_weight,
    final_gain,
    head_weight,
):
    vmem = pl.BlockSpec(memory_space=pltpu.VMEM)
    operands = (
        jnp.transpose(grid_field, (0, 2, 1)),
        conv_weight,
        observed,
        hidden_mask,
        tile_route.reshape(1, STATIONS),
        station_spot.reshape(1, STATIONS),
        neighbours.T,
        neighbour_count.reshape(1, STATIONS),
        edge_bias.T,
        live_count.reshape(1, 1),
        in_weight.T,
        norm_gain.reshape(1, CH),
        qkv_weight,
        out_weight,
        final_gain.reshape(1, CH),
        head_weight,
    )
    predicted, gradient = pl.pallas_call(
        kernel,
        out_shape=(
            jax.ShapeDtypeStruct((STATIONS, 128), F32),
            jax.ShapeDtypeStruct((ROWS, CH, COLS), F32),
        ),
        in_specs=[vmem] * len(operands),
        out_specs=(vmem, vmem),
        scratch_shapes=[
            pltpu.VMEM((ROWS + 2, 3, CH, COLS), BF16),
            pltpu.VMEM((CH, DEPTH), BF16),
            pltpu.VMEM((CH, DEPTH), BF16),
            pltpu.VMEM((ROWS, CH, COLS), BF16),
            pltpu.VMEM((ROWS, CH, COLS), BF16),
            pltpu.VMEM((ROWS, SLOTS, COLS), BF16),
            pltpu.VMEM((N, 2 * CAP, 128), BF16),
            pltpu.VMEM((N, 2 * CAP, 128), BF16),
            pltpu.VMEM((N, 2 * CAP, 128), BF16),
            pltpu.VMEM((N, 2 * CAP, 128), BF16),
            pltpu.VMEM((N, 1, 128), F32),
            pltpu.VMEM((N, 1, 128), F32),
            pltpu.VMEM((2 * SLOTS, 128), F32),
            pltpu.VMEM((2, 2, CH, COLS), BF16),
            pltpu.VMEM((2, 2 * ROWS, 256), BF16),
            pltpu.VMEM((2, 2, ROWS, 256), BF16),
            pltpu.VMEM((2, 4, 16, 256), BF16),
            pltpu.VMEM((STATIONS, SLOTS), BF16),
            pltpu.VMEM((SLOTS, STATIONS), BF16),
            pltpu.VMEM((STATIONS, STATIONS), F32),
            pltpu.VMEM((CH, SLOTS), BF16),
            pltpu.VMEM((CH, STATIONS), F32),
            pltpu.VMEM((CH, STATIONS), F32),
            pltpu.VMEM((CH, STATIONS), F32),
            pltpu.VMEM((CH, 256), BF16),
            pltpu.VMEM((CH, CH), BF16),
            pltpu.VMEM((3 * CH, CH), BF16),
            pltpu.VMEM((CH, CH), BF16),
            pltpu.VMEM((128, CH), BF16),
            pltpu.VMEM((128, STATIONS), F32),
            pltpu.VMEM((128, STATIONS), F32),
            pltpu.SemaphoreType.DMA((2, 8)),
            pltpu.SemaphoreType.DMA((2, 8)),
            pltpu.SemaphoreType.DMA((3,)),
            pltpu.SemaphoreType.DMA((3,)),
        ],
        compiler_params=pltpu.CompilerParams(
            collective_id=0, has_side_effects=True, vmem_limit_bytes=56 << 20
        ),
        name="whole",
    )(*operands)
    return predicted, jnp.transpose(gradient, (0, 2, 1))


def solution(mesh):
    return jax.shard_map(
        on_device,
        mesh=mesh,
        in_specs=(
            P("lat", "lon", None),
            P(),
            P(LAT_LON, None),
            P(LAT_LON, None),
            P(LAT_LON, None),
            P(LAT_LON),
            P(LAT_LON, None),
            P(LAT_LON),
            P(LAT_LON, None),
            P(LAT_LON),
            P(),
            P(),
            P(),
            P(),
            P(),
            P(),
        ),
        out_specs=(P(LAT_LON, None), P("lat", "lon", None)),
        check_vma=False,
    )
```

```python
import jax
import jax.numpy as jnp
from jax import lax
from jax.experimental import pallas as pl
from jax.experimental.pallas import tpu as pltpu
from jax.sharding import PartitionSpec as P

CH = 192
HEADS = 3
HEAD_DIM = 64
ROWS = 32
COLS = 128
FINE = 4 * (COLS - 1)
CAP = 4
N = 128
N_LAT = 4
N_LON = 32
SLOTS = N * CAP
STATIONS = 256
TAPS = 9 * CH
DEPTH = TAPS + 2 * ROWS
EPS = 1e-06
F32 = jnp.float32
BF16 = jnp.bfloat16
LAT_LON = ("lat", "lon")


def nn(a, b):
    return lax.dot_general(a, b, (((1,), (0,)), ((), ())), preferred_element_type=F32)


def nt(a, b):
    return lax.dot_general(a, b, (((1,), (1,)), ((), ())), preferred_element_type=F32)


def lane_iota(shape):
    return lax.broadcasted_iota(jnp.int32, shape, len(shape) - 1)


def row_iota(shape):
    return lax.broadcasted_iota(jnp.int32, shape, len(shape) - 2)


def as_columns(row):
    return jnp.transpose(jnp.broadcast_to(row, (128, row.shape[1])))


def flipped(value):
    return jnp.transpose(value.astype(F32)).astype(BF16)


def sigmoid(v):
    return 0.5 * (1.0 + jnp.tanh(0.5 * v))


def fill_shifted(shifted, y, value):
    lane = lane_iota((CH, COLS))
    shifted[y, 1] = value.astype(BF16)
    shifted[y, 0] = jnp.where(lane == 0, 0.0, pltpu.roll(value, 1, 1)).astype(BF16)
    shifted[y, 2] = jnp.where(lane == COLS - 1, 0.0, pltpu.roll(value, COLS - 1, 1)).astype(BF16)


def around(shifted, y):
    ends_at = row_iota((2 * ROWS, COLS))
    lane = lane_iota((2 * ROWS, COLS))
    hit = ((ends_at == y) & (lane == 0)) | ((ends_at == y + ROWS) & (lane == COLS - 1))
    return jnp.concatenate([shifted[pl.ds(y, 3)].reshape(TAPS, COLS), hit.astype(F32).astype(BF16)], axis=0)


def kernel(*refs):
    (x_hbm, conv_hbm, observed_hbm, mask_hbm, tile_hbm, spot_hbm, neighbours_hbm, count_hbm) = refs[0:8]
    (bias_hbm, live_hbm, in_hbm, gain1_hbm, qkv_hbm, out_hbm, gain2_hbm, head_hbm) = refs[8:16]
    (predicted_hbm, dpre_hbm, dfield_hbm, taps_hbm) = refs[16:20]
    (x_ref, conv_ref, observed_ref, mask_ref, tile_ref, spot_ref, neighbours_ref, count_ref) = refs[20:28]
    (bias_ref, live_ref, in_ref, gain1_ref, qkv_ref, out_ref, gain2_ref, head_ref) = refs[28:36]
    (shifted, taps_f, taps_b, field, slope, spread, dpre, dfield, pick) = refs[36:45]
    (answer_out, answer_in, grads_out, grads_in, ask_out, ask_in, wide) = refs[45:52]
    (row_in, side_out, side_in, corner_in, select, select_t, scores_bias, grads_t) = refs[52:60]
    (embedded0, gain1, gain2, in_low, in_low_t, qkv_t, out_t, head_t, mask_t, observed_t) = refs[60:70]
    (ends_spread, slope_ends, predicted_out) = refs[70:73]
    (halo_send, halo_recv, a2a_send, a2a_recv, load_sem, store_sem) = refs[73:79]

    loads = [pltpu.make_async_copy(refs[k], refs[20 + k], load_sem.at[k]) for k in range(16)]
    for k in (4, 5, 0, 1, 2, 3, 6, 7, 8, 9, 10, 11, 12, 13, 14, 15):
        loads[k].start()
    lat = lax.axis_index("lat")
    lon = lax.axis_index("lon")
    me = lat * N_LON + lon
    barrier = pltpu.get_barrier_semaphore()

    def coords(peer):
        return (peer // N_LON, lax.rem(peer, N_LON))

    def greet(i, carry):
        pl.semaphore_signal(
            barrier, inc=1, device_id=coords(lax.rem(me + i, N)), device_id_type=pl.DeviceIdType.MESH
        )
        return carry

    lax.fori_loop(1, N, greet, 0)

    loads[4].wait()
    loads[5].wait()
    tile_row = tile_ref[...].astype(F32)
    tile_cols = as_columns(tile_row)
    tile_cols = jnp.concatenate([tile_cols, tile_cols], axis=1)
    square = (STATIONS, STATIONS)
    same = (tile_cols == tile_row) & (row_iota(square) < lane_iota(square))
    rank = jnp.sum(same.astype(F32), axis=0, keepdims=True)
    slot = tile_row * CAP + rank
    spot = spot_ref[...].astype(F32)
    spot_high = jnp.floor(spot * (1.0 / 256.0))
    spot_low = spot - 256.0 * spot_high
    part = row_iota((128, STATIONS))
    wanted = jnp.where(part < CAP, spot_high, spot_low)
    wanted = jnp.where((part & (CAP - 1)).astype(F32) == rank, wanted, 0.0)
    wanted = jnp.where(part < 2 * CAP, wanted, 0.0).astype(BF16)
    is_tile = (row_iota((N, STATIONS)).astype(F32) == tile_row).astype(BF16)
    ask_out[...] = nt(is_tile, wanted).reshape(N, 1, 128)

    end = row_iota((2 * ROWS, ROWS * COLS))
    end_cell = jnp.where(end < ROWS, end * COLS, (end - ROWS) * COLS + COLS - 1)
    pick[...] = (lane_iota((2 * ROWS, ROWS * COLS)) == end_cell).astype(F32).astype(BF16)
    side_out[...] = jnp.zeros((2, 2 * ROWS, 256), BF16)
    loads[0].wait()
    side_out[0, :, 0:CH] = nt(pick[...], jnp.concatenate([x_ref[y] for y in range(ROWS)], axis=1)).astype(BF16)

    up, down = lax.rem(lat + N_LAT - 1, N_LAT), lax.rem(lat + 1, N_LAT)
    left, right = lax.rem(lon + N_LON - 1, N_LON), lax.rem(lon + 1, N_LON)

    def halo_copies(turn, first, last):
        mine = side_out.at[turn]
        plan = [
            (mine.at[pl.ds(0, ROWS)], side_in.at[turn, 1], (lat, left)),
            (mine.at[pl.ds(ROWS, ROWS)], side_in.at[turn, 0], (lat, right)),
            (mine.at[pl.ds(0, 16)], corner_in.at[turn, 3], (up, left)),
            (mine.at[pl.ds(ROWS, 16)], corner_in.at[turn, 2], (up, right)),
            (mine.at[pl.ds(16, 16)], corner_in.at[turn, 1], (down, left)),
            (mine.at[pl.ds(ROWS + 16, 16)], corner_in.at[turn, 0], (down, right)),
            (first, row_in.at[turn, 1], (up, lon)),
            (last, row_in.at[turn, 0], (down, lon)),
        ]
        return [
            pltpu.make_async_remote_copy(
                src_ref=source,
                dst_ref=target,
                send_sem=halo_send.at[turn, k],
                recv_sem=halo_recv.at[turn, k],
                device_id=where,
                device_id_type=pl.DeviceIdType.MESH,
            )
            for k, (source, target, where) in enumerate(plan)
        ]

    def start_exchange(turn, source, target):
        def send(i, carry):
            peer = lax.rem(me + i, N)
            pltpu.make_async_remote_copy(
                src_ref=source.at[peer],
                dst_ref=target.at[me],
                send_sem=a2a_send.at[turn],
                recv_sem=a2a_recv.at[turn],
                device_id=coords(peer),
                device_id_type=pl.DeviceIdType.MESH,
            ).start()
            return carry

        lax.fori_loop(1, N, send, 0)
        target[me] = source[me]

    def wait_received(turn, target):
        rest = target.at[pl.ds(0, N - 1)]
        pltpu.make_async_copy(rest, rest, a2a_recv.at[turn]).wait()

    def wait_sent(turn, source):
        rest = source.at[pl.ds(0, N - 1)]
        pltpu.make_async_copy(rest, rest, a2a_send.at[turn]).wait()

    pl.semaphore_wait(barrier, N - 1)
    first_halo = halo_copies(0, x_ref.at[0], x_ref.at[ROWS - 1])
    for copy in first_halo:
        copy.start()
    start_exchange(0, ask_out, ask_in)

    def fill_row(y, carry):
        fill_shifted(shifted, y + 1, x_ref[y].astype(F32))
        return carry

    lax.fori_loop(0, ROWS, fill_row, 0, unroll=2)
    loads[1].wait()
    for tap in range(9):
        taps_f[:, CH * tap : CH * (tap + 1)] = flipped(conv_ref[tap])

    keep_up = jnp.where(lat > 0, 1.0, 0.0)
    keep_down = jnp.where(lat < N_LAT - 1, 1.0, 0.0)

    def side_terms(turn, taps, backward):
        total = []
        for side in range(2):
            above = corner_in[turn, side].astype(F32)[15:16, 0:CH] * keep_up
            below = corner_in[turn, 2 + side].astype(F32)[0:1, 0:CH] * keep_down
            column = jnp.concatenate([above, side_in[turn, side].astype(F32)[:, 0:CH], below], axis=0)
            sums = None
            for i in range(3):
                piece = column[i : i + ROWS].astype(BF16)
                if backward:
                    term = nt(piece, conv_ref[8 - (3 * i + 2 * side)])
                else:
                    term = nn(piece, conv_ref[3 * i + 2 * side])
                sums = term if sums is None else sums + term
            total.append(sums)
        total = jnp.concatenate(total + [jnp.zeros((64, CH), F32)], axis=0)
        taps[:, TAPS:] = jnp.transpose(total)[:, 0 : 2 * ROWS].astype(BF16)

    for copy in first_halo:
        copy.wait_recv()
    fill_shifted(shifted, 0, row_in[0, 0].astype(F32) * keep_up)
    fill_shifted(shifted, ROWS + 1, row_in[0, 1].astype(F32) * keep_down)
    side_terms(0, taps_f, False)

    def forward_rows(pair, carry):
        y = pair * 2
        pre = nn(taps_f[...], jnp.concatenate([around(shifted, y), around(shifted, y + 1)], axis=1))
        gate = sigmoid(pre)
        moved = pre * gate
        tilt = gate * (1.0 + pre * (1.0 - gate))
        for k in range(2):
            cut = slice(COLS * k, COLS * (k + 1))
            field[y + k] = (x_ref[y + k].astype(F32) + moved[:, cut]).astype(BF16)
            slope[y + k] = tilt[:, cut].astype(BF16)
        return carry

    lax.fori_loop(0, ROWS // 2, forward_rows, 0, unroll=4)

    wait_received(0, ask_in)
    asked = ask_in[...].reshape(N, 128).astype(BF16)
    repeat = (row_iota((SLOTS, N)) // CAP == lane_iota((SLOTS, N))).astype(BF16)
    asked = nn(repeat, asked)
    place = lane_iota((SLOTS, 128))
    turn_of = row_iota((SLOTS, 128)) & (CAP - 1)
    spots = jnp.where(place == turn_of, asked * 256.0, 0.0) + jnp.where(place == turn_of + CAP, asked, 0.0)
    spots = jnp.sum(spots, axis=1, keepdims=True)
    fine_row = jnp.floor((spots + 0.5) * (1.0 / FINE))
    fine_col = spots - FINE * fine_row
    at_row = jnp.broadcast_to((fine_row + 0.5) * 0.25, (SLOTS, COLS))
    at_col = jnp.broadcast_to((fine_col + 0.5) * 0.25, (SLOTS, COLS))
    along = jnp.maximum(1.0 - jnp.abs(at_col - place.astype(F32)), 0.0).astype(BF16)
    at_row16 = at_row.astype(BF16)

    def fill_spread(y, carry):
        away = jnp.abs(at_row16 - y.astype(BF16))
        spread[y] = jnp.maximum(1.0 - away, 0.0).astype(BF16) * along
        return carry

    lax.fori_loop(0, ROWS, fill_spread, 0, unroll=4)

    def send_wide(rows, out):
        wide[pl.ds(0, SLOTS, 2)] = rows[:, 0:128]
        wide[pl.ds(1, SLOTS, 2)] = jnp.concatenate([rows[:, 128:CH], jnp.zeros((SLOTS, 256 - CH), F32)], axis=1)
        out[...] = wide[...].reshape(N, 2 * CAP, 128).astype(BF16)

    def read_wide(held):
        wide[...] = held[...].astype(F32).reshape(2 * SLOTS, 128)
        return wide[pl.ds(0, SLOTS, 2)], wide[pl.ds(1, SLOTS, 2)]

    sampled = jnp.zeros((SLOTS, CH), F32)
    for eighth in range(4):
        rows = [8 * eighth + k for k in range(8)]
        sampled = sampled + nt(
            jnp.concatenate([spread[y] for y in rows], axis=1), jnp.concatenate([field[y] for y in rows], axis=1)
        )
    send_wide(sampled, answer_out)
    start_exchange(1, answer_out, answer_in)

    for k in (2, 3, 6, 7, 8, 9, 10, 11, 12, 13, 14, 15):
        loads[k].wait()
    select_t[...] = (row_iota((SLOTS, STATIONS)).astype(F32) == slot).astype(BF16)
    slot_cols = as_columns(slot)
    slot_cols = jnp.concatenate([slot_cols] * (SLOTS // 128), axis=1)
    select[...] = (lane_iota((STATIONS, SLOTS)).astype(F32) == slot_cols).astype(BF16)
    for wide_gain, gain in ((gain1, gain1_ref), (gain2, gain2_ref)):
        cols = as_columns(gain[...])
        wide_gain[...] = jnp.concatenate([cols, cols], axis=1)
    observed_t[...] = jnp.transpose(observed_ref[...])
    mask_t[...] = jnp.transpose(mask_ref[...].astype(F32))
    shown = (observed_t[...] * (1.0 - mask_t[...])).astype(BF16)
    embedded0[...] = nn(in_ref[:, 0:128], shown) + nn(in_ref[:, 128:256], mask_t[...].astype(BF16))
    low = in_ref[:, 256:448].astype(F32)
    in_low[...] = jnp.concatenate([low, jnp.zeros((CH, 64), F32)], axis=1).astype(BF16)
    in_low_t[...] = jnp.transpose(low).astype(BF16)
    qkv_t[...] = flipped(qkv_ref[...])
    out_t[...] = flipped(out_ref[...])
    head_t[...] = flipped(head_ref[...])

    live = live_ref[...].astype(F32)
    station = lane_iota((1, STATIONS)).astype(F32)
    near = neighbours_ref[...].astype(F32)
    used = (row_iota((16, STATIONS)).astype(F32) < count_ref[...].astype(F32)) & (near < live)
    near = jnp.where(used, near, -1.0)
    near = jnp.concatenate([near, station, jnp.full((7, STATIONS), -1.0, F32)], axis=0)
    bias = jnp.concatenate([bias_ref[...], jnp.zeros((8, STATIONS), F32)], axis=0)
    top = jnp.full((24, STATIONS), -1e30, F32)
    for j in range(17):
        top = jnp.where(near == near[j : j + 1], jnp.maximum(top, bias[j : j + 1]), top)
    together = jnp.zeros((24, STATIONS), F32)
    for j in range(17):
        together = together + jnp.where(near == near[j : j + 1], jnp.exp(bias[j : j + 1] - top), 0.0)
    level = top + jnp.log(together)
    other = row_iota(square).astype(F32)
    dense = jnp.full(square, -1e30, F32)
    for j in range(17):
        dense = jnp.where(other == near[j : j + 1], level[j : j + 1], dense)
    scores_bias[...] = dense

    wait_received(1, answer_in)

    low_part, high_part = read_wide(answer_in)
    answers = jnp.concatenate([low_part, high_part], axis=1).astype(BF16)
    interp = nn(select[...], answers).astype(BF16)
    embedded = embedded0[...] + nt(in_low[...], interp)
    scale1 = lax.rsqrt(jnp.mean(embedded * embedded, axis=0, keepdims=True) + EPS)
    unit1 = embedded * scale1
    projected = nn(qkv_t[...], (unit1 * gain1[...]).astype(BF16)).astype(BF16)
    probs, mixed = [], []
    score_scale = 1.0 / 8.0

    def part_of(kind, head):
        at = kind * CH + head * HEAD_DIM
        return projected[at : at + HEAD_DIM]

    for head in range(HEADS):
        score = nn(flipped(part_of(1, head)), part_of(0, head)) * score_scale + scores_bias[...]
        weight = jnp.exp(score - jnp.max(score, axis=0, keepdims=True))
        prob = (weight * (1.0 / jnp.sum(weight, axis=0, keepdims=True))).astype(BF16)
        probs.append(prob)
        mixed.append(nn(part_of(2, head), prob))
    mixed = jnp.concatenate(mixed, axis=0).astype(BF16)
    residual = embedded + nn(out_t[...], mixed)
    scale2 = lax.rsqrt(jnp.mean(residual * residual, axis=0, keepdims=True) + EPS)
    unit2 = residual * scale2
    final = (unit2 * gain2[...]).astype(BF16)
    alive = (station < live).astype(F32)
    predicted = nn(head_t[...], final) * alive
    d_pred = (2.0 * alive * mask_t[...] * (predicted - observed_t[...])).astype(BF16)

    d_unit2 = nn(head_ref[...], d_pred) * gain2[...]
    d_residual = scale2 * (d_unit2 - unit2 * jnp.mean(d_unit2 * unit2, axis=0, keepdims=True))
    d_mixed = nn(out_ref[...], d_residual.astype(BF16)).astype(BF16)
    d_query, d_key, d_value = [], [], []
    for head in range(HEADS):
        d_here = d_mixed[head * HEAD_DIM : (head + 1) * HEAD_DIM]
        prob = probs[head]
        d_prob = nn(flipped(part_of(2, head)), d_here)
        wide_prob = prob.astype(F32)
        d_score = d_prob - jnp.sum(d_prob * wide_prob, axis=0, keepdims=True)
        d_score = (wide_prob * d_score * score_scale).astype(BF16)
        d_query.append(nn(part_of(1, head), d_score))
        d_key.append(nt(part_of(0, head), d_score))
        d_value.append(nt(d_here, prob))
    d_projected = jnp.concatenate(d_query + d_key + d_value, axis=0).astype(BF16)
    d_unit1 = nn(qkv_ref[...], d_projected) * gain1[...]
    d_embedded = d_residual + scale1 * (d_unit1 - unit1 * jnp.mean(d_unit1 * unit1, axis=0, keepdims=True))
    d_interp = nn(in_low_t[...], d_embedded.astype(BF16)).astype(BF16)
    send_wide(nt(select_t[...], d_interp), grads_out)
    start_exchange(2, grads_out, grads_in)

    predicted_out[...] = jnp.transpose(predicted)
    stores = [pltpu.make_async_copy(predicted_out, predicted_hbm, store_sem.at[0])]
    stores[0].start()
    for tap in range(9):
        taps_b[:, CH * tap : CH * (tap + 1)] = conv_ref[8 - tap]
    slope_ends[...] = nt(pick[...], jnp.concatenate([slope[y] for y in range(ROWS)], axis=1))
    end_row = (place & (ROWS - 1)).astype(F32)
    end_col = jnp.where(place < ROWS, 0.0, COLS - 1.0)
    on_end = jnp.maximum(1.0 - jnp.abs(at_row - end_row), 0.0) * jnp.maximum(1.0 - jnp.abs(at_col - end_col), 0.0)
    ends_spread[...] = jnp.transpose(on_end)[0 : 2 * ROWS].astype(BF16)
    for copy in first_halo:
        copy.wait_send()
    wait_received(2, grads_in)

    low_part, high_part = read_wide(grads_in)
    arrived = jnp.concatenate([low_part, high_part], axis=1)
    at_ends = nn(ends_spread[...], arrived.astype(BF16))[:, 0:CH] * slope_ends[...]
    side_out[1, :, 0:CH] = at_ends.astype(BF16)
    grads_t[...] = jnp.transpose(arrived)[0:CH].astype(BF16)

    def scatter_pair(y0, y1):
        both = nn(grads_t[...], jnp.concatenate([spread[y0], spread[y1]], axis=1))
        for k, y in enumerate((y0, y1)):
            value = both[:, COLS * k : COLS * (k + 1)]
            dfield[y] = value
            dpre[y + 1] = (value * slope[y].astype(F32)).astype(BF16)

    scatter_pair(0, ROWS - 1)
    second_halo = halo_copies(1, dpre.at[1], dpre.at[ROWS])
    for copy in second_halo:
        copy.start()

    def store(source, target):
        copy = pltpu.make_async_copy(source, target, store_sem.at[len(stores)])
        copy.start()
        stores.append(copy)

    store(dfield.at[pl.ds(0, 1)], dfield_hbm.at[pl.ds(0, 1)])
    store(dfield.at[pl.ds(ROWS - 1, 1)], dfield_hbm.at[pl.ds(ROWS - 1, 1)])
    for third in range(3):

        def scatter_rows(pair, carry):
            y = 1 + 10 * third + 2 * pair
            scatter_pair(y, y + 1)
            return carry

        lax.fori_loop(0, 5, scatter_rows, 0, unroll=True)
        at = pl.ds(1 + 10 * third, 10)
        store(dfield.at[at], dfield_hbm.at[at])
        at = pl.ds(2 + 10 * third, 10)
        store(dpre.at[at], dpre_hbm.at[at])
    for copy in second_halo:
        copy.wait_recv()
    dpre[0] = (row_in[1, 0].astype(F32) * keep_up).astype(BF16)
    dpre[ROWS + 1] = (row_in[1, 1].astype(F32) * keep_down).astype(BF16)
    store(dpre.at[pl.ds(0, 2)], dpre_hbm.at[pl.ds(0, 2)])
    store(dpre.at[pl.ds(ROWS, 2)], dpre_hbm.at[pl.ds(ROWS, 2)])
    side_terms(1, taps_b, True)
    store(taps_b, taps_hbm)
    for copy in second_halo:
        copy.wait_send()
    wait_sent(0, ask_out)
    wait_sent(1, answer_out)
    wait_sent(2, grads_out)
    for copy in stores:
        copy.wait()


def back_kernel(*refs):
    (dpre_hbm, dfield_hbm, taps_hbm, predicted_hbm, grad_hbm, predicted_to) = refs[0:6]
    (dpre, dfield, taps, shifted, grad, sem) = refs[6:12]
    through = pltpu.make_async_copy(predicted_hbm, predicted_to, sem.at[0])
    load_taps = pltpu.make_async_copy(taps_hbm, taps, sem.at[1])

    def load(part):
        at = pl.ds(0, 10) if part == 0 else pl.ds(8 * part + 2, 8)
        fields = pl.ds(8 * part, 8)
        return (
            pltpu.make_async_copy(dpre_hbm.at[at], dpre.at[at], sem.at[2 + part]),
            pltpu.make_async_copy(dfield_hbm.at[fields], dfield.at[fields], sem.at[6 + part]),
        )

    def store(part):
        fields = pl.ds(8 * part, 8)
        return pltpu.make_async_copy(grad.at[fields], grad_hbm.at[fields], sem.at[10 + part])

    loads = [load(part) for part in range(4)]
    loads[0][0].start()
    load_taps.start()
    loads[0][1].start()
    for part in range(1, 4):
        for copy in loads[part]:
            copy.start()
    through.start()

    def shift_part(part):
        loads[part][0].wait()

        def shift_row(k, carry):
            fill_shifted(shifted, k, dpre[k].astype(F32))
            return carry

        first = 0 if part == 0 else 8 * part + 2
        lax.fori_loop(first, 8 * part + 10, shift_row, 0, unroll=True)

    shift_part(0)
    load_taps.wait()
    for part in range(4):
        loads[part][1].wait()

        def backward_rows(pair, carry):
            y = 8 * part + pair * 2
            back = nn(taps[...], jnp.concatenate([around(shifted, y), around(shifted, y + 1)], axis=1))
            for k in range(2):
                grad[y + k] = dfield[y + k] + back[:, COLS * k : COLS * (k + 1)]
            return carry

        lax.fori_loop(0, 4, backward_rows, 0, unroll=True)
        store(part).start()
        if part < 3:
            shift_part(part + 1)
    for part in range(4):
        store(part).wait()
    through.wait()


def on_device(
    grid_field,
    conv_weight,
    observed,
    hidden_mask,
    tile_route,
    station_spot,
    neighbours,
    neighbour_count,
    edge_bias,
    live_count,
    in_weight,
    norm_gain,
    qkv_weight,
    out_weight,
    final_gain,
    head_weight,
):
    operands = (
        jnp.transpose(grid_field, (0, 2, 1)),
        conv_weight,
        observed,
        hidden_mask,
        tile_route.reshape(1, STATIONS),
        station_spot.reshape(1, STATIONS),
        neighbours.T,
        neighbour_count.reshape(1, STATIONS),
        edge_bias.T,
        live_count.reshape(1, 1),
        in_weight.T,
        norm_gain.reshape(1, CH),
        qkv_weight,
        out_weight,
        final_gain.reshape(1, CH),
        head_weight,
    )
    anywhere = pl.BlockSpec(memory_space=pl.ANY)

    def vmem(*shape, kind=BF16):
        return pltpu.VMEM(shape, kind)

    predicted, dpre, dfield, taps = pl.pallas_call(
        kernel,
        out_shape=(
            jax.ShapeDtypeStruct((STATIONS, 128), F32),
            jax.ShapeDtypeStruct((ROWS + 2, CH, COLS), BF16),
            jax.ShapeDtypeStruct((ROWS, CH, COLS), F32),
            jax.ShapeDtypeStruct((CH, DEPTH), BF16),
        ),
        in_specs=[anywhere] * len(operands),
        out_specs=(anywhere,) * 4,
        scratch_shapes=[pltpu.VMEM(o.shape, o.dtype) for o in operands]
        + [
            vmem(ROWS + 2, 3, CH, COLS),
            vmem(CH, DEPTH),
            vmem(CH, DEPTH),
            vmem(ROWS, CH, COLS),
            vmem(ROWS, CH, COLS),
            vmem(ROWS, SLOTS, COLS),
            vmem(ROWS + 2, CH, COLS),
            vmem(ROWS, CH, COLS, kind=F32),
            vmem(2 * ROWS, ROWS * COLS),
            vmem(N, 2 * CAP, 128),
            vmem(N, 2 * CAP, 128),
            vmem(N, 2 * CAP, 128),
            vmem(N, 2 * CAP, 128),
            vmem(N, 1, 128, kind=F32),
            vmem(N, 1, 128, kind=F32),
            vmem(2 * SLOTS, 128, kind=F32),
            vmem(2, 2, CH, COLS),
            vmem(2, 2 * ROWS, 256),
            vmem(2, 2, ROWS, 256),
            vmem(2, 4, 16, 256),
            vmem(STATIONS, SLOTS),
            vmem(SLOTS, STATIONS),
            vmem(STATIONS, STATIONS, kind=F32),
            vmem(CH, SLOTS),
            vmem(CH, STATIONS, kind=F32),
            vmem(CH, STATIONS, kind=F32),
            vmem(CH, STATIONS, kind=F32),
            vmem(CH, 256),
            vmem(CH, CH),
            vmem(3 * CH, CH),
            vmem(CH, CH),
            vmem(128, CH),
            vmem(128, STATIONS, kind=F32),
            vmem(128, STATIONS, kind=F32),
            vmem(2 * ROWS, SLOTS),
            vmem(2 * ROWS, CH, kind=F32),
            vmem(STATIONS, 128, kind=F32),
            pltpu.SemaphoreType.DMA((2, 8)),
            pltpu.SemaphoreType.DMA((2, 8)),
            pltpu.SemaphoreType.DMA((3,)),
            pltpu.SemaphoreType.DMA((3,)),
            pltpu.SemaphoreType.DMA((16,)),
            pltpu.SemaphoreType.DMA((16,)),
        ],
        compiler_params=pltpu.CompilerParams(
            collective_id=0, has_side_effects=True, vmem_limit_bytes=56 << 20
        ),
        name="whole",
    )(*operands)
    gradient, predicted = pl.pallas_call(
        back_kernel,
        out_shape=(
            jax.ShapeDtypeStruct((ROWS, CH, COLS), F32),
            jax.ShapeDtypeStruct((STATIONS, 128), F32),
        ),
        in_specs=[anywhere] * 4,
        out_specs=(anywhere,) * 2,
        scratch_shapes=[
            vmem(ROWS + 2, CH, COLS),
            vmem(ROWS, CH, COLS, kind=F32),
            vmem(CH, DEPTH),
            vmem(ROWS + 2, 3, CH, COLS),
            vmem(ROWS, CH, COLS, kind=F32),
            pltpu.SemaphoreType.DMA((14,)),
        ],
        compiler_params=pltpu.CompilerParams(vmem_limit_bytes=60 << 20),
        name="back",
    )(dpre, dfield, taps, predicted)
    return predicted, jnp.transpose(gradient, (0, 2, 1))


def solution(mesh):
    return jax.shard_map(
        on_device,
        mesh=mesh,
        in_specs=(
            P("lat", "lon", None),
            P(),
            P(LAT_LON, None),
            P(LAT_LON, None),
            P(LAT_LON, None),
            P(LAT_LON),
            P(LAT_LON, None),
            P(LAT_LON),
            P(LAT_LON, None),
            P(LAT_LON),
            P(),
            P(),
            P(),
            P(),
            P(),
            P(),
        ),
        out_specs=(P(LAT_LON, None), P("lat", "lon", None)),
        check_vma=False,
    )
```

```python
import jax
import jax.numpy as jnp
from jax import lax
from jax.experimental import pallas as pl
from jax.experimental.pallas import tpu as pltpu
from jax.sharding import PartitionSpec as P

CH = 192
HEADS = 3
HEAD_DIM = 64
ROWS = 32
COLS = 128
FINE = 4 * (COLS - 1)
CAP = 4
N = 128
N_LAT = 4
N_LON = 32
SLOTS = N * CAP
STATIONS = 256
TAPS = 9 * CH
DEPTH = TAPS + 2 * ROWS
EPS = 1e-06
F32 = jnp.float32
BF16 = jnp.bfloat16
LAT_LON = ("lat", "lon")


def nn(a, b):
    return lax.dot_general(a, b, (((1,), (0,)), ((), ())), preferred_element_type=F32)


def nt(a, b):
    return lax.dot_general(a, b, (((1,), (1,)), ((), ())), preferred_element_type=F32)


def lane_iota(shape):
    return lax.broadcasted_iota(jnp.int32, shape, len(shape) - 1)


def row_iota(shape):
    return lax.broadcasted_iota(jnp.int32, shape, len(shape) - 2)


def as_columns(row):
    return jnp.transpose(jnp.broadcast_to(row, (128, row.shape[1])))


def flipped(value):
    return jnp.transpose(value.astype(F32)).astype(BF16)


def sigmoid(v):
    return 0.5 * (1.0 + jnp.tanh(0.5 * v))


def fill_shifted(shifted, y, value):
    lane = lane_iota((CH, COLS))
    shifted[y, 1] = value.astype(BF16)
    shifted[y, 0] = jnp.where(lane == 0, 0.0, pltpu.roll(value, 1, 1)).astype(BF16)
    shifted[y, 2] = jnp.where(lane == COLS - 1, 0.0, pltpu.roll(value, COLS - 1, 1)).astype(BF16)


def around(shifted, y):
    ends_at = row_iota((2 * ROWS, COLS))
    lane = lane_iota((2 * ROWS, COLS))
    hit = ((ends_at == y) & (lane == 0)) | ((ends_at == y + ROWS) & (lane == COLS - 1))
    return jnp.concatenate([shifted[pl.ds(y, 3)].reshape(TAPS, COLS), hit.astype(F32).astype(BF16)], axis=0)


def poles(lat):
    return jnp.where(lat > 0, 1.0, 0.0), jnp.where(lat < N_LAT - 1, 1.0, 0.0)


def side_terms(side_in, corner_in, conv_ref, taps, keep, backward):
    total = []
    for side in range(2):
        above = corner_in[side].astype(F32)[15:16, 0:CH] * keep[0]
        below = corner_in[2 + side].astype(F32)[0:1, 0:CH] * keep[1]
        column = jnp.concatenate([above, side_in[side].astype(F32)[:, 0:CH], below], axis=0)
        sums = None
        for i in range(3):
            piece = column[i : i + ROWS].astype(BF16)
            if backward:
                term = nt(piece, conv_ref[8 - (3 * i + 2 * side)])
            else:
                term = nn(piece, conv_ref[3 * i + 2 * side])
            sums = term if sums is None else sums + term
        total.append(sums)
    total = jnp.concatenate(total + [jnp.zeros((64, CH), F32)], axis=0)
    taps[:, TAPS:] = jnp.transpose(total)[:, 0 : 2 * ROWS].astype(BF16)


def kernel(*refs):
    inputs = refs[0:16]
    (predicted_hbm, dpre_hbm, dfield_hbm, taps_hbm, rows_hbm, sides_hbm, corners_hbm) = refs[16:23]
    refs = refs[3:]
    (x_ref, conv_ref, observed_ref, mask_ref, tile_ref, spot_ref, neighbours_ref, count_ref) = refs[20:28]
    (bias_ref, live_ref, in_ref, gain1_ref, qkv_ref, out_ref, gain2_ref, head_ref) = refs[28:36]
    (shifted, taps_f, taps_b, field, slope, spread, dpre, dfield, pick) = refs[36:45]
    (answer_out, answer_in, grads_out, grads_in, ask_out, ask_in, wide) = refs[45:52]
    (row_in, side_out, side_in, corner_in, select, select_t, scores_bias, grads_t) = refs[52:60]
    (embedded0, gain1, gain2, in_low, in_low_t, qkv_t, out_t, head_t, mask_t, observed_t) = refs[60:70]
    (ends_spread, slope_ends, predicted_out) = refs[70:73]
    (halo_send, halo_recv, a2a_send, a2a_recv, load_sem, store_sem) = refs[73:79]

    loads = [pltpu.make_async_copy(inputs[k], refs[20 + k], load_sem.at[k]) for k in range(16)]
    for k in (4, 5, 0, 1, 2, 3, 6, 7, 8, 9, 10, 11, 12, 13, 14, 15):
        loads[k].start()
    lat = lax.axis_index("lat")
    lon = lax.axis_index("lon")
    me = lat * N_LON + lon
    barrier = pltpu.get_barrier_semaphore()

    def coords(peer):
        return (lax.div(peer, N_LON), lax.rem(peer, N_LON))

    def greet(i, carry):
        pl.semaphore_signal(
            barrier, inc=1, device_id=coords(lax.rem(me + i, N)), device_id_type=pl.DeviceIdType.MESH
        )
        return carry

    lax.fori_loop(1, N, greet, 0)

    loads[4].wait()
    loads[5].wait()
    tile_row = tile_ref[...].astype(F32)
    tile_cols = as_columns(tile_row)
    tile_cols = jnp.concatenate([tile_cols, tile_cols], axis=1)
    square = (STATIONS, STATIONS)
    same = (tile_cols == tile_row) & (row_iota(square) < lane_iota(square))
    rank = jnp.sum(same.astype(F32), axis=0, keepdims=True)
    slot = tile_row * CAP + rank
    ahead = tile_row - me.astype(F32)
    ahead = jnp.where(ahead < 0.0, ahead + N, ahead)
    spot = spot_ref[...].astype(F32)
    spot_high = jnp.floor(spot * (1.0 / 256.0))
    spot_low = spot - 256.0 * spot_high
    part = row_iota((128, STATIONS))
    wanted = jnp.where(part < CAP, spot_high, spot_low)
    wanted = jnp.where((part & (CAP - 1)).astype(F32) == rank, wanted, 0.0)
    wanted = jnp.where(part < 2 * CAP, wanted, 0.0).astype(BF16)
    is_tile = (row_iota((N, STATIONS)).astype(F32) == ahead).astype(BF16)
    ask_out[...] = nt(is_tile, wanted).reshape(N, 1, 128)

    end = row_iota((2 * ROWS, ROWS * COLS))
    end_cell = jnp.where(end < ROWS, end * COLS, (end - ROWS) * COLS + COLS - 1)
    pick[...] = (lane_iota((2 * ROWS, ROWS * COLS)) == end_cell).astype(F32).astype(BF16)
    side_out[...] = jnp.zeros((2, 2 * ROWS, 256), BF16)
    loads[0].wait()
    side_out[0, :, 0:CH] = nt(pick[...], jnp.concatenate([x_ref[y] for y in range(ROWS)], axis=1)).astype(BF16)

    up, down = lax.rem(lat + N_LAT - 1, N_LAT), lax.rem(lat + 1, N_LAT)
    left, right = lax.rem(lon + N_LON - 1, N_LON), lax.rem(lon + 1, N_LON)

    def halo_copies(turn, first, last, rows_to, sides_to, corners_to):
        mine = side_out.at[turn]
        plan = [
            (mine.at[pl.ds(0, ROWS)], sides_to.at[1], (lat, left)),
            (mine.at[pl.ds(ROWS, ROWS)], sides_to.at[0], (lat, right)),
            (mine.at[pl.ds(0, 16)], corners_to.at[3], (up, left)),
            (mine.at[pl.ds(ROWS, 16)], corners_to.at[2], (up, right)),
            (mine.at[pl.ds(16, 16)], corners_to.at[1], (down, left)),
            (mine.at[pl.ds(ROWS + 16, 16)], corners_to.at[0], (down, right)),
            (first, rows_to.at[1], (up, lon)),
            (last, rows_to.at[0], (down, lon)),
        ]
        return [
            pltpu.make_async_remote_copy(
                src_ref=source,
                dst_ref=target,
                send_sem=halo_send.at[turn, k],
                recv_sem=halo_recv.at[turn, k],
                device_id=where,
                device_id_type=pl.DeviceIdType.MESH,
            )
            for k, (source, target, where) in enumerate(plan)
        ]

    def start_exchange(turn, source, target, by_tile, first=1, last=N):
        def send(i, carry):
            pltpu.make_async_remote_copy(
                src_ref=source.at[i],
                dst_ref=target.at[me if by_tile else N - i],
                send_sem=a2a_send.at[turn],
                recv_sem=a2a_recv.at[turn],
                device_id=coords(lax.rem(me + i, N)),
                device_id_type=pl.DeviceIdType.MESH,
            ).start()
            return carry

        lax.fori_loop(first, last, send, 0)

    def wait_received(turn, target):
        rest = target.at[pl.ds(0, N - 1)]
        pltpu.make_async_copy(rest, rest, a2a_recv.at[turn]).wait()

    def wait_sent(turn, source):
        rest = source.at[pl.ds(0, N - 1)]
        pltpu.make_async_copy(rest, rest, a2a_send.at[turn]).wait()

    pl.semaphore_wait(barrier, N - 1)
    first_halo = halo_copies(0, x_ref.at[0], x_ref.at[ROWS - 1], row_in, side_in, corner_in)
    for copy in first_halo:
        copy.start()
    start_exchange(0, ask_out, ask_in, False)
    ask_in[0] = ask_out[0]

    def fill_row(y, carry):
        fill_shifted(shifted, y + 1, x_ref[y].astype(F32))
        return carry

    lax.fori_loop(0, ROWS, fill_row, 0, unroll=2)
    loads[1].wait()
    for tap in range(9):
        taps_f[:, CH * tap : CH * (tap + 1)] = flipped(conv_ref[tap])

    keep = poles(lat)
    for copy in first_halo:
        copy.wait_recv()
    fill_shifted(shifted, 0, row_in[0].astype(F32) * keep[0])
    fill_shifted(shifted, ROWS + 1, row_in[1].astype(F32) * keep[1])
    side_terms(side_in, corner_in, conv_ref, taps_f, keep, False)

    def forward_rows(pair, carry):
        y = pair * 2
        pre = nn(taps_f[...], jnp.concatenate([around(shifted, y), around(shifted, y + 1)], axis=1))
        gate = sigmoid(pre)
        moved = pre * gate
        tilt = gate * (1.0 + pre * (1.0 - gate))
        for k in range(2):
            cut = slice(COLS * k, COLS * (k + 1))
            field[y + k] = (x_ref[y + k].astype(F32) + moved[:, cut]).astype(BF16)
            slope[y + k] = tilt[:, cut].astype(BF16)
        return carry

    lax.fori_loop(0, ROWS // 2, forward_rows, 0, unroll=4)

    wait_received(0, ask_in)
    asked = ask_in[...].reshape(N, 128).astype(BF16)
    repeat = (row_iota((SLOTS, N)) // CAP == lane_iota((SLOTS, N))).astype(BF16)
    asked = nn(repeat, asked)
    place = lane_iota((SLOTS, 128))
    turn_of = row_iota((SLOTS, 128)) & (CAP - 1)
    spots = jnp.where(place == turn_of, asked * 256.0, 0.0) + jnp.where(place == turn_of + CAP, asked, 0.0)
    spots = jnp.sum(spots, axis=1, keepdims=True)
    fine_row = jnp.floor((spots + 0.5) * (1.0 / FINE))
    fine_col = spots - FINE * fine_row
    at_row = jnp.broadcast_to((fine_row + 0.5) * 0.25, (SLOTS, COLS))
    at_col = jnp.broadcast_to((fine_col + 0.5) * 0.25, (SLOTS, COLS))
    along = jnp.maximum(1.0 - jnp.abs(at_col - place.astype(F32)), 0.0).astype(BF16)
    at_row16 = at_row.astype(BF16)

    def fill_spread(y, carry):
        away = jnp.abs(at_row16 - y.astype(BF16))
        spread[y] = jnp.maximum(1.0 - away, 0.0).astype(BF16) * along
        return carry

    lax.fori_loop(0, ROWS, fill_spread, 0, unroll=4)

    def put_wide(half, rows, out):
        count = SLOTS // 2
        at = half * SLOTS
        wide[pl.ds(at, count, 2)] = rows[:, 0:128]
        wide[pl.ds(at + 1, count, 2)] = jnp.concatenate([rows[:, 128:CH], jnp.zeros((count, 256 - CH), F32)], axis=1)
        out[pl.ds(half * (N // 2), N // 2)] = wide[pl.ds(at, SLOTS)].reshape(N // 2, 2 * CAP, 128).astype(BF16)

    def read_wide(held):
        wide[...] = held[...].astype(F32).reshape(2 * SLOTS, 128)
        return wide[pl.ds(0, SLOTS, 2)], wide[pl.ds(1, SLOTS, 2)]

    for half in range(2):
        of_half = pl.ds(half * (SLOTS // 2), SLOTS // 2)
        sampled = None
        for part in range(4):
            rows = [8 * part + k for k in range(8)]
            term = nt(
                jnp.concatenate([spread[y, of_half] for y in rows], axis=1),
                jnp.concatenate([field[y] for y in rows], axis=1),
            )
            sampled = term if sampled is None else sampled + term
        put_wide(half, sampled, answer_out)
        start_exchange(1, answer_out, answer_in, True, max(1, half * (N // 2)), (half + 1) * (N // 2))
    answer_in[me] = answer_out[0]

    for k in (2, 3, 6, 7, 8, 9, 10, 11, 12, 13, 14, 15):
        loads[k].wait()
    select_t[...] = (row_iota((SLOTS, STATIONS)).astype(F32) == ahead * CAP + rank).astype(BF16)
    slot_cols = as_columns(slot)
    slot_cols = jnp.concatenate([slot_cols] * (SLOTS // 128), axis=1)
    select[...] = (lane_iota((STATIONS, SLOTS)).astype(F32) == slot_cols).astype(BF16)
    for wide_gain, gain in ((gain1, gain1_ref), (gain2, gain2_ref)):
        cols = as_columns(gain[...])
        wide_gain[...] = jnp.concatenate([cols, cols], axis=1)
    observed_t[...] = jnp.transpose(observed_ref[...])
    mask_t[...] = jnp.transpose(mask_ref[...].astype(F32))
    shown = (observed_t[...] * (1.0 - mask_t[...])).astype(BF16)
    embedded0[...] = nn(in_ref[:, 0:128], shown) + nn(in_ref[:, 128:256], mask_t[...].astype(BF16))
    low = in_ref[:, 256:448].astype(F32)
    in_low[...] = jnp.concatenate([low, jnp.zeros((CH, 64), F32)], axis=1).astype(BF16)
    in_low_t[...] = jnp.transpose(low).astype(BF16)
    qkv_t[...] = flipped(qkv_ref[...])
    out_t[...] = flipped(out_ref[...])
    head_t[...] = flipped(head_ref[...])

    live = live_ref[...].astype(F32)
    station = lane_iota((1, STATIONS)).astype(F32)
    near = neighbours_ref[...].astype(F32)
    used = (row_iota((16, STATIONS)).astype(F32) < count_ref[...].astype(F32)) & (near < live)
    near = jnp.where(used, near, -1.0)
    near = jnp.concatenate([near, station, jnp.full((7, STATIONS), -1.0, F32)], axis=0)
    bias = jnp.concatenate([bias_ref[...], jnp.zeros((8, STATIONS), F32)], axis=0)
    top = jnp.full((24, STATIONS), -1e30, F32)
    for j in range(17):
        top = jnp.where(near == near[j : j + 1], jnp.maximum(top, bias[j : j + 1]), top)
    together = jnp.zeros((24, STATIONS), F32)
    for j in range(17):
        together = together + jnp.where(near == near[j : j + 1], jnp.exp(bias[j : j + 1] - top), 0.0)
    level = top + jnp.log(together)
    other = row_iota(square).astype(F32)
    dense = jnp.full(square, -1e30, F32)
    for j in range(17):
        dense = jnp.where(other == near[j : j + 1], level[j : j + 1], dense)
    scores_bias[...] = dense

    wait_received(1, answer_in)

    low_part, high_part = read_wide(answer_in)
    answers = jnp.concatenate([low_part, high_part], axis=1).astype(BF16)
    interp = nn(select[...], answers).astype(BF16)
    embedded = embedded0[...] + nt(in_low[...], interp)
    scale1 = lax.rsqrt(jnp.mean(embedded * embedded, axis=0, keepdims=True) + EPS)
    unit1 = embedded * scale1
    projected = nn(qkv_t[...], (unit1 * gain1[...]).astype(BF16)).astype(BF16)
    probs, mixed = [], []
    score_scale = 1.0 / 8.0

    def part_of(kind, head):
        at = kind * CH + head * HEAD_DIM
        return projected[at : at + HEAD_DIM]

    for head in range(HEADS):
        score = nn(flipped(part_of(1, head)), part_of(0, head)) * score_scale + scores_bias[...]
        weight = jnp.exp(score - jnp.max(score, axis=0, keepdims=True))
        prob = (weight * (1.0 / jnp.sum(weight, axis=0, keepdims=True))).astype(BF16)
        probs.append(prob)
        mixed.append(nn(part_of(2, head), prob))
    mixed = jnp.concatenate(mixed, axis=0).astype(BF16)
    residual = embedded + nn(out_t[...], mixed)
    scale2 = lax.rsqrt(jnp.mean(residual * residual, axis=0, keepdims=True) + EPS)
    unit2 = residual * scale2
    final = (unit2 * gain2[...]).astype(BF16)
    alive = (station < live).astype(F32)
    predicted = nn(head_t[...], final) * alive
    d_pred = (2.0 * alive * mask_t[...] * (predicted - observed_t[...])).astype(BF16)

    d_unit2 = nn(head_ref[...], d_pred) * gain2[...]
    d_residual = scale2 * (d_unit2 - unit2 * jnp.mean(d_unit2 * unit2, axis=0, keepdims=True))
    d_mixed = nn(out_ref[...], d_residual.astype(BF16)).astype(BF16)
    d_query, d_key, d_value = [], [], []
    for head in range(HEADS):
        d_here = d_mixed[head * HEAD_DIM : (head + 1) * HEAD_DIM]
        prob = probs[head]
        d_prob = nn(flipped(part_of(2, head)), d_here)
        wide_prob = prob.astype(F32)
        d_score = d_prob - jnp.sum(d_prob * wide_prob, axis=0, keepdims=True)
        d_score = (wide_prob * d_score * score_scale).astype(BF16)
        d_query.append(nn(part_of(1, head), d_score))
        d_key.append(nt(part_of(0, head), d_score))
        d_value.append(nt(d_here, prob))
    d_projected = jnp.concatenate(d_query + d_key + d_value, axis=0).astype(BF16)
    d_unit1 = nn(qkv_ref[...], d_projected) * gain1[...]
    d_embedded = d_residual + scale1 * (d_unit1 - unit1 * jnp.mean(d_unit1 * unit1, axis=0, keepdims=True))
    d_interp = nn(in_low_t[...], d_embedded.astype(BF16)).astype(BF16)
    for half in range(2):
        put_wide(half, nt(select_t[pl.ds(half * (SLOTS // 2), SLOTS // 2)], d_interp), grads_out)
        start_exchange(2, grads_out, grads_in, False, max(1, half * (N // 2)), (half + 1) * (N // 2))
    grads_in[0] = grads_out[0]

    predicted_out[...] = jnp.transpose(predicted)
    stores = [pltpu.make_async_copy(predicted_out, predicted_hbm, store_sem.at[0])]
    stores[0].start()
    for tap in range(9):
        taps_b[:, CH * tap : CH * (tap + 1)] = conv_ref[8 - tap]
    taps_b[:, TAPS:] = jnp.zeros((CH, 2 * ROWS), BF16)
    stores.append(pltpu.make_async_copy(taps_b, taps_hbm, store_sem.at[1]))
    stores[1].start()
    slope_ends[...] = nt(pick[...], jnp.concatenate([slope[y] for y in range(ROWS)], axis=1))
    end_row = (place & (ROWS - 1)).astype(F32)
    end_col = jnp.where(place < ROWS, 0.0, COLS - 1.0)
    on_end = jnp.maximum(1.0 - jnp.abs(at_row - end_row), 0.0) * jnp.maximum(1.0 - jnp.abs(at_col - end_col), 0.0)
    ends_spread[...] = jnp.transpose(on_end)[0 : 2 * ROWS].astype(BF16)
    for copy in first_halo:
        copy.wait_send()
    wait_received(2, grads_in)

    low_part, high_part = read_wide(grads_in)
    arrived = jnp.concatenate([low_part, high_part], axis=1)
    at_ends = nn(ends_spread[...], arrived.astype(BF16))[:, 0:CH] * slope_ends[...]
    side_out[1, :, 0:CH] = at_ends.astype(BF16)
    grads_t[...] = jnp.transpose(arrived)[0:CH].astype(BF16)

    def scatter_pair(y0, y1):
        both = nn(grads_t[...], jnp.concatenate([spread[y0], spread[y1]], axis=1))
        for k, y in enumerate((y0, y1)):
            value = both[:, COLS * k : COLS * (k + 1)]
            dfield[y] = value
            dpre[y] = (value * slope[y].astype(F32)).astype(BF16)

    scatter_pair(0, ROWS - 1)
    second_halo = halo_copies(1, dpre.at[0], dpre.at[ROWS - 1], rows_hbm, sides_hbm, corners_hbm)
    for copy in second_halo:
        copy.start()

    def store(source, target):
        copy = pltpu.make_async_copy(source, target, store_sem.at[len(stores)])
        copy.start()
        stores.append(copy)

    store(dfield.at[pl.ds(0, 1)], dfield_hbm.at[pl.ds(0, 1)])
    store(dfield.at[pl.ds(ROWS - 1, 1)], dfield_hbm.at[pl.ds(ROWS - 1, 1)])
    store(dpre.at[pl.ds(0, 1)], dpre_hbm.at[pl.ds(0, 1)])
    store(dpre.at[pl.ds(ROWS - 1, 1)], dpre_hbm.at[pl.ds(ROWS - 1, 1)])
    for third in range(3):

        def scatter_rows(pair, carry):
            y = 1 + 10 * third + 2 * pair
            scatter_pair(y, y + 1)
            return carry

        lax.fori_loop(0, 5, scatter_rows, 0, unroll=True)
        at = pl.ds(1 + 10 * third, 10)
        store(dfield.at[at], dfield_hbm.at[at])
        store(dpre.at[at], dpre_hbm.at[at])
    for copy in second_halo:
        copy.wait_recv()
    for copy in second_halo:
        copy.wait_send()
    wait_sent(0, ask_out)
    wait_sent(1, answer_out)
    wait_sent(2, grads_out)
    for copy in stores:
        copy.wait()


PARTS = ((0, 4), (4, 10), (14, 10), (24, 8))


def back_kernel(*refs):
    (dpre_hbm, dfield_hbm, predicted_hbm, grad_hbm, predicted_to) = refs[0:2] + refs[7:10]
    (dpre, dfield, taps, row_in, side_in, corner_in, conv_ref, shifted, grad, sem) = refs[10:20]
    keep = poles(lax.axis_index("lat"))
    small = [pltpu.make_async_copy(refs[k], refs[10 + k], sem.at[k]) for k in range(2, 7)]
    load_taps, load_rows, load_sides, load_corners, load_conv = small
    through = pltpu.make_async_copy(predicted_hbm, predicted_to, sem.at[7])

    def load(part):
        first, count = PARTS[part]
        begin = first + 1 if part else 0
        end = min(first + count + 1, ROWS)
        at, fields = pl.ds(begin, end - begin), pl.ds(first, count)
        return (
            pltpu.make_async_copy(dpre_hbm.at[at], dpre.at[at], sem.at[8 + part]),
            pltpu.make_async_copy(dfield_hbm.at[fields], dfield.at[fields], sem.at[12 + part]),
        )

    def store(part):
        fields = pl.ds(*PARTS[part])
        return pltpu.make_async_copy(grad.at[fields], grad_hbm.at[fields], sem.at[16 + part])

    loads = [load(part) for part in range(4)]
    for copy in (load_sides, load_corners, load_conv, load_rows, loads[0][0], load_taps, loads[0][1]):
        copy.start()
    for part in range(1, 4):
        for copy in loads[part]:
            copy.start()
    through.start()

    def shift_part(part):
        first, count = PARTS[part]
        loads[part][0].wait()
        if part == 0:
            fill_shifted(shifted, 0, row_in[0].astype(F32) * keep[0])
        for y in range(first + 1 if part else 0, min(first + count + 1, ROWS)):
            fill_shifted(shifted, y + 1, dpre[y].astype(F32))
        if part == 3:
            fill_shifted(shifted, ROWS + 1, row_in[1].astype(F32) * keep[1])

    load_rows.wait()
    shift_part(0)
    for copy in (load_taps, load_sides, load_corners, load_conv):
        copy.wait()
    side_terms(side_in, corner_in, conv_ref, taps, keep, True)
    for part in range(4):
        loads[part][1].wait()
        first, count = PARTS[part]
        for pair in range(count // 2):
            y = first + pair * 2
            back = nn(taps[...], jnp.concatenate([around(shifted, y), around(shifted, y + 1)], axis=1))
            for k in range(2):
                grad[y + k] = dfield[y + k] + back[:, COLS * k : COLS * (k + 1)]
        store(part).start()
        if part < 3:
            shift_part(part + 1)
    for part in range(4):
        store(part).wait()
    through.wait()


def on_device(
    grid_field,
    conv_weight,
    observed,
    hidden_mask,
    tile_route,
    station_spot,
    neighbours,
    neighbour_count,
    edge_bias,
    live_count,
    in_weight,
    norm_gain,
    qkv_weight,
    out_weight,
    final_gain,
    head_weight,
):
    operands = (
        jnp.transpose(grid_field, (0, 2, 1)),
        conv_weight,
        observed,
        hidden_mask,
        tile_route.reshape(1, STATIONS),
        station_spot.reshape(1, STATIONS),
        neighbours.T,
        neighbour_count.reshape(1, STATIONS),
        edge_bias.T,
        live_count.reshape(1, 1),
        in_weight.T,
        norm_gain.reshape(1, CH),
        qkv_weight,
        out_weight,
        final_gain.reshape(1, CH),
        head_weight,
    )
    anywhere = pl.BlockSpec(memory_space=pl.ANY)

    def vmem(*shape, kind=BF16):
        return pltpu.VMEM(shape, kind)

    predicted, dpre, dfield, taps, rows, sides, corners = pl.pallas_call(
        kernel,
        out_shape=(
            jax.ShapeDtypeStruct((STATIONS, 128), F32),
            jax.ShapeDtypeStruct((ROWS, CH, COLS), BF16),
            jax.ShapeDtypeStruct((ROWS, CH, COLS), F32),
            jax.ShapeDtypeStruct((CH, DEPTH), BF16),
            jax.ShapeDtypeStruct((2, CH, COLS), BF16),
            jax.ShapeDtypeStruct((2, ROWS, 256), BF16),
            jax.ShapeDtypeStruct((4, 16, 256), BF16),
        ),
        in_specs=[anywhere] * len(operands),
        out_specs=(anywhere,) * 7,
        scratch_shapes=[pltpu.VMEM(o.shape, o.dtype) for o in operands]
        + [
            vmem(ROWS + 2, 3, CH, COLS),
            vmem(CH, DEPTH),
            vmem(CH, DEPTH),
            vmem(ROWS, CH, COLS),
            vmem(ROWS, CH, COLS),
            vmem(ROWS, SLOTS, COLS),
            vmem(ROWS, CH, COLS),
            vmem(ROWS, CH, COLS, kind=F32),
            vmem(2 * ROWS, ROWS * COLS),
            vmem(N, 2 * CAP, 128),
            vmem(N, 2 * CAP, 128),
            vmem(N, 2 * CAP, 128),
            vmem(N, 2 * CAP, 128),
            vmem(N, 1, 128, kind=F32),
            vmem(N, 1, 128, kind=F32),
            vmem(2 * SLOTS, 128, kind=F32),
            vmem(2, CH, COLS),
            vmem(2, 2 * ROWS, 256),
            vmem(2, ROWS, 256),
            vmem(4, 16, 256),
            vmem(STATIONS, SLOTS),
            vmem(SLOTS, STATIONS),
            vmem(STATIONS, STATIONS, kind=F32),
            vmem(CH, SLOTS),
            vmem(CH, STATIONS, kind=F32),
            vmem(CH, STATIONS, kind=F32),
            vmem(CH, STATIONS, kind=F32),
            vmem(CH, 256),
            vmem(CH, CH),
            vmem(3 * CH, CH),
            vmem(CH, CH),
            vmem(128, CH),
            vmem(128, STATIONS, kind=F32),
            vmem(128, STATIONS, kind=F32),
            vmem(2 * ROWS, SLOTS),
            vmem(2 * ROWS, CH, kind=F32),
            vmem(STATIONS, 128, kind=F32),
            pltpu.SemaphoreType.DMA((2, 8)),
            pltpu.SemaphoreType.DMA((2, 8)),
            pltpu.SemaphoreType.DMA((3,)),
            pltpu.SemaphoreType.DMA((3,)),
            pltpu.SemaphoreType.DMA((16,)),
            pltpu.SemaphoreType.DMA((16,)),
        ],
        compiler_params=pltpu.CompilerParams(
            collective_id=0, has_side_effects=True, vmem_limit_bytes=56 << 20
        ),
        name="whole",
    )(*operands)
    gradient, predicted = pl.pallas_call(
        back_kernel,
        out_shape=(
            jax.ShapeDtypeStruct((ROWS, CH, COLS), F32),
            jax.ShapeDtypeStruct((STATIONS, 128), F32),
        ),
        in_specs=[anywhere] * 8,
        out_specs=(anywhere, anywhere),
        scratch_shapes=[
            vmem(ROWS, CH, COLS),
            vmem(ROWS, CH, COLS, kind=F32),
            vmem(CH, DEPTH),
            vmem(2, CH, COLS),
            vmem(2, ROWS, 256),
            vmem(4, 16, 256),
            vmem(9, CH, CH),
            vmem(ROWS + 2, 3, CH, COLS),
            vmem(ROWS, CH, COLS, kind=F32),
            pltpu.SemaphoreType.DMA((20,)),
        ],
        compiler_params=pltpu.CompilerParams(vmem_limit_bytes=60 << 20),
        name="back",
    )(dpre, dfield, taps, rows, sides, corners, conv_weight, predicted)
    return predicted, jnp.transpose(gradient, (0, 2, 1))


def solution(mesh):
    return jax.shard_map(
        on_device,
        mesh=mesh,
        in_specs=(
            P("lat", "lon", None),
            P(),
            P(LAT_LON, None),
            P(LAT_LON, None),
            P(LAT_LON, None),
            P(LAT_LON),
            P(LAT_LON, None),
            P(LAT_LON),
            P(LAT_LON, None),
            P(LAT_LON),
            P(),
            P(),
            P(),
            P(),
            P(),
            P(),
        ),
        out_specs=(P(LAT_LON, None), P("lat", "lon", None)),
        check_vma=False,
    )
```

```python
import jax
import jax.numpy as jnp
from jax import lax
from jax.experimental import pallas as pl
from jax.experimental.pallas import tpu as pltpu
from jax.sharding import PartitionSpec as P

CH = 192
HEADS = 3
HEAD_DIM = 64
ROWS = 32
COLS = 128
FINE = 4 * (COLS - 1)
CAP = 4
N = 128
N_LAT = 4
N_LON = 32
SLOTS = N * CAP
STATIONS = 256
TAPS = 9 * CH
DEPTH = TAPS + 2 * ROWS
EPS = 1e-06
F32 = jnp.float32
BF16 = jnp.bfloat16
LAT_LON = ("lat", "lon")
HOPS = (0, 1, 2, 1)
GROUPS = sorted(((dx, dz) for dx in range(4) for dz in range(4)), key=lambda d: -HOPS[d[0]] - HOPS[d[1]])
OWN = 8 * GROUPS.index((0, 0)) + 5


def nn(a, b):
    return lax.dot_general(a, b, (((1,), (0,)), ((), ())), preferred_element_type=F32)


def nt(a, b):
    return lax.dot_general(a, b, (((1,), (1,)), ((), ())), preferred_element_type=F32)


def lane_iota(shape):
    return lax.broadcasted_iota(jnp.int32, shape, len(shape) - 1)


def row_iota(shape):
    return lax.broadcasted_iota(jnp.int32, shape, len(shape) - 2)


def as_columns(row):
    return jnp.transpose(jnp.broadcast_to(row, (128, row.shape[1])))


def flipped(value):
    return jnp.transpose(value.astype(F32)).astype(BF16)


def sigmoid(v):
    return 0.5 * (1.0 + jnp.tanh(0.5 * v))


def fill_shifted(shifted, y, value):
    lane = lane_iota((CH, COLS))
    shifted[y, 1] = value.astype(BF16)
    shifted[y, 0] = jnp.where(lane == 0, 0.0, pltpu.roll(value, 1, 1)).astype(BF16)
    shifted[y, 2] = jnp.where(lane == COLS - 1, 0.0, pltpu.roll(value, COLS - 1, 1)).astype(BF16)


def around(shifted, y):
    ends_at = row_iota((2 * ROWS, COLS))
    lane = lane_iota((2 * ROWS, COLS))
    hit = ((ends_at == y) & (lane == 0)) | ((ends_at == y + ROWS) & (lane == COLS - 1))
    return jnp.concatenate([shifted[pl.ds(y, 3)].reshape(TAPS, COLS), hit.astype(F32).astype(BF16)], axis=0)


def poles(lat):
    return jnp.where(lat > 0, 1.0, 0.0), jnp.where(lat < N_LAT - 1, 1.0, 0.0)


def side_terms(side_in, corner_in, conv_ref, taps, keep, backward):
    total = []
    for side in range(2):
        above = corner_in[side].astype(F32)[15:16, 0:CH] * keep[0]
        below = corner_in[2 + side].astype(F32)[0:1, 0:CH] * keep[1]
        column = jnp.concatenate([above, side_in[side].astype(F32)[:, 0:CH], below], axis=0)
        sums = None
        for i in range(3):
            piece = column[i : i + ROWS].astype(BF16)
            if backward:
                term = nt(piece, conv_ref[8 - (3 * i + 2 * side)])
            else:
                term = nn(piece, conv_ref[3 * i + 2 * side])
            sums = term if sums is None else sums + term
        total.append(sums)
    total = jnp.concatenate(total + [jnp.zeros((64, CH), F32)], axis=0)
    taps[:, TAPS:] = jnp.transpose(total)[:, 0 : 2 * ROWS].astype(BF16)


def kernel(*refs):
    inputs = refs[0:16]
    (predicted_hbm, dpre_hbm, dfield_hbm, taps_hbm, rows_hbm, sides_hbm, corners_hbm) = refs[16:23]
    refs = refs[3:]
    (x_ref, conv_ref, observed_ref, mask_ref, tile_ref, spot_ref, neighbours_ref, count_ref) = refs[20:28]
    (bias_ref, live_ref, in_ref, gain1_ref, qkv_ref, out_ref, gain2_ref, head_ref) = refs[28:36]
    (shifted, taps_f, taps_b, field, slope, spread, dpre, dfield, pick) = refs[36:45]
    (answer_out, answer_in, grads_out, grads_in, ask_out, ask_in, wide) = refs[45:52]
    (row_in, side_out, side_in, corner_in, select, select_t, scores_bias, grads_t) = refs[52:60]
    (embedded0, gain1, gain2, in_low, in_low_t, qkv_t, out_t, head_t, mask_t, observed_t) = refs[60:70]
    (ends_spread, slope_ends, predicted_out, before) = refs[70:74]
    (halo_send, halo_recv, a2a_send, a2a_recv, load_sem, store_sem) = refs[74:80]

    loads = [pltpu.make_async_copy(inputs[k], refs[20 + k], load_sem.at[k]) for k in range(16)]
    for k in (4, 5, 0, 1, 2, 3, 6, 7, 8, 9, 10, 11, 12, 13, 14, 15):
        loads[k].start()
    lat = lax.axis_index("lat")
    lon = lax.axis_index("lon")
    me = lat * N_LON + lon
    at_z, at_core = lax.div(lon, 8), lax.rem(lon, 2)
    at_y = lax.rem(lax.div(lon, 2), 4)
    barrier = pltpu.get_barrier_semaphore()

    def coords(peer):
        return (lax.div(peer, N_LON), lax.rem(peer, N_LON))

    def greet(i, carry):
        pl.semaphore_signal(
            barrier, inc=1, device_id=coords(lax.rem(me + i, N)), device_id_type=pl.DeviceIdType.MESH
        )
        return carry

    lax.fori_loop(1, N, greet, 0)

    loads[4].wait()
    loads[5].wait()
    tile_row = tile_ref[...].astype(F32)
    tile_cols = as_columns(tile_row)
    tile_cols = jnp.concatenate([tile_cols, tile_cols], axis=1)
    square = (STATIONS, STATIONS)
    same = (tile_cols == tile_row) & (row_iota(square) < lane_iota(square))
    rank = jnp.sum(same.astype(F32), axis=0, keepdims=True)
    slot = tile_row * CAP + rank

    def ring(value, here):
        ahead = value - here.astype(F32)
        return jnp.where(ahead < 0.0, ahead + 4.0, ahead)

    tile_x = jnp.floor(tile_row * (1.0 / 32.0))
    tile_z = jnp.floor((tile_row - 32.0 * tile_x) * (1.0 / 8.0))
    tile_pair = jnp.floor(tile_row * 0.5)
    tile_y = tile_pair - 4.0 * jnp.floor(tile_pair * 0.25)
    step = 4.0 * ring(tile_x, lat) + ring(tile_z, at_z)
    group = jnp.zeros_like(step)
    for index, (dx, dz) in enumerate(GROUPS):
        group = jnp.where(step == 4.0 * dx + dz, float(index), group)
    back_y = ring(2.0 - ring(tile_y, at_y), jnp.int32(0))
    same_core = 1.0 - jnp.abs(tile_row - 2.0 * tile_pair - at_core.astype(F32))
    ahead = 8.0 * group + 2.0 * back_y + same_core
    spot = spot_ref[...].astype(F32)
    spot_high = jnp.floor(spot * (1.0 / 256.0))
    spot_low = spot - 256.0 * spot_high
    part = row_iota((128, STATIONS))
    wanted = jnp.where(part < CAP, spot_high, spot_low)
    wanted = jnp.where((part & (CAP - 1)).astype(F32) == rank, wanted, 0.0)
    wanted = jnp.where(part < 2 * CAP, wanted, 0.0).astype(BF16)
    is_tile = (row_iota((N, STATIONS)).astype(F32) == ahead).astype(BF16)
    ask_out[...] = nt(is_tile, wanted).reshape(N, 1, 128)

    end = row_iota((2 * ROWS, ROWS * COLS))
    end_cell = jnp.where(end < ROWS, end * COLS, (end - ROWS) * COLS + COLS - 1)
    pick[...] = (lane_iota((2 * ROWS, ROWS * COLS)) == end_cell).astype(F32).astype(BF16)
    side_out[...] = jnp.zeros((2, 2 * ROWS, 256), BF16)
    loads[0].wait()
    side_out[0, :, 0:CH] = nt(pick[...], jnp.concatenate([x_ref[y] for y in range(ROWS)], axis=1)).astype(BF16)

    up, down = lax.rem(lat + N_LAT - 1, N_LAT), lax.rem(lat + 1, N_LAT)
    left, right = lax.rem(lon + N_LON - 1, N_LON), lax.rem(lon + 1, N_LON)

    def halo_copies(turn, first, last, rows_to, sides_to, corners_to):
        mine = side_out.at[turn]
        plan = [
            (mine.at[pl.ds(0, ROWS)], sides_to.at[1], (lat, left)),
            (mine.at[pl.ds(ROWS, ROWS)], sides_to.at[0], (lat, right)),
            (mine.at[pl.ds(0, 16)], corners_to.at[3], (up, left)),
            (mine.at[pl.ds(ROWS, 16)], corners_to.at[2], (up, right)),
            (mine.at[pl.ds(16, 16)], corners_to.at[1], (down, left)),
            (mine.at[pl.ds(ROWS + 16, 16)], corners_to.at[0], (down, right)),
            (first, rows_to.at[1], (up, lon)),
            (last, rows_to.at[0], (down, lon)),
        ]
        return [
            pltpu.make_async_remote_copy(
                src_ref=source,
                dst_ref=target,
                send_sem=halo_send.at[turn, k],
                recv_sem=halo_recv.at[turn, k],
                device_id=where,
                device_id_type=pl.DeviceIdType.MESH,
            )
            for k, (source, target, where) in enumerate(plan)
        ]

    def start_exchange(turn, source, target, by_tile, first=0, last=16):
        for group in range(first, last):
            dx, dz = GROUPS[group]
            opposite = GROUPS.index((-dx % 4, -dz % 4))

            def send(k, carry):
                d = lax.div(k, 2)
                e = k - 2 * d
                x, z = lax.rem(lat + dx, 4), lax.rem(at_z + dz, 4)
                y, core = lax.rem(at_y + 6 - d, 4), lax.rem(at_core + 1 - e, 2)
                pltpu.make_async_remote_copy(
                    src_ref=source.at[8 * group + k],
                    dst_ref=target.at[me if by_tile else 8 * opposite + 2 * lax.rem(4 - d, 4) + e],
                    send_sem=a2a_send.at[turn],
                    recv_sem=a2a_recv.at[turn],
                    device_id=(x, (z * 4 + y) * 2 + core),
                    device_id_type=pl.DeviceIdType.MESH,
                ).start()
                return carry

            if OWN // 8 == group:
                lax.fori_loop(0, OWN % 8, send, 0)
                lax.fori_loop(OWN % 8 + 1, 8, send, 0)
            else:
                lax.fori_loop(0, 8, send, 0)

    def wait_received(turn, target):
        rest = target.at[pl.ds(0, N - 1)]
        pltpu.make_async_copy(rest, rest, a2a_recv.at[turn]).wait()

    def wait_sent(turn, source):
        rest = source.at[pl.ds(0, N - 1)]
        pltpu.make_async_copy(rest, rest, a2a_send.at[turn]).wait()

    pl.semaphore_wait(barrier, N - 1)
    first_halo = halo_copies(0, x_ref.at[0], x_ref.at[ROWS - 1], row_in, side_in, corner_in)
    for copy in first_halo:
        copy.start()
    start_exchange(0, ask_out, ask_in, False)
    ask_in[OWN] = ask_out[OWN]

    def fill_row(y, carry):
        fill_shifted(shifted, y + 1, x_ref[y].astype(F32))
        return carry

    lax.fori_loop(0, ROWS, fill_row, 0, unroll=2)
    loads[1].wait()
    for tap in range(9):
        taps_f[:, CH * tap : CH * (tap + 1)] = flipped(conv_ref[tap])

    keep = poles(lat)
    for copy in first_halo:
        copy.wait_recv()
    fill_shifted(shifted, 0, row_in[0].astype(F32) * keep[0])
    fill_shifted(shifted, ROWS + 1, row_in[1].astype(F32) * keep[1])
    side_terms(side_in, corner_in, conv_ref, taps_f, keep, False)

    def forward_rows(pair, carry):
        y = pair * 2
        pre = nn(taps_f[...], jnp.concatenate([around(shifted, y), around(shifted, y + 1)], axis=1))
        gate = sigmoid(pre)
        moved = pre * gate
        for k in range(2):
            cut = slice(COLS * k, COLS * (k + 1))
            field[y + k] = (x_ref[y + k].astype(F32) + moved[:, cut]).astype(BF16)
            before[y + k] = pre[:, cut]
        return carry

    lax.fori_loop(0, ROWS // 2, forward_rows, 0, unroll=4)

    wait_received(0, ask_in)
    asked = ask_in[...].reshape(N, 128).astype(BF16)
    repeat = (row_iota((SLOTS, N)) // CAP == lane_iota((SLOTS, N))).astype(BF16)
    asked = nn(repeat, asked)
    place = lane_iota((SLOTS, 128))
    turn_of = row_iota((SLOTS, 128)) & (CAP - 1)
    spots = jnp.where(place == turn_of, asked * 256.0, 0.0) + jnp.where(place == turn_of + CAP, asked, 0.0)
    spots = jnp.sum(spots, axis=1, keepdims=True)
    fine_row = jnp.floor((spots + 0.5) * (1.0 / FINE))
    fine_col = spots - FINE * fine_row
    at_row = jnp.broadcast_to((fine_row + 0.5) * 0.25, (SLOTS, COLS))
    at_col = jnp.broadcast_to((fine_col + 0.5) * 0.25, (SLOTS, COLS))
    along = jnp.maximum(1.0 - jnp.abs(at_col - place.astype(F32)), 0.0).astype(BF16)
    at_row16 = at_row.astype(BF16)

    def fill_spread(y, carry):
        away = jnp.abs(at_row16 - y.astype(BF16))
        spread[y] = jnp.maximum(1.0 - away, 0.0).astype(BF16) * along
        return carry

    lax.fori_loop(0, ROWS, fill_spread, 0, unroll=4)

    def put_wide(half, rows, out):
        count = SLOTS // 2
        at = half * SLOTS
        wide[pl.ds(at, count, 2)] = rows[:, 0:128]
        wide[pl.ds(at + 1, count, 2)] = jnp.concatenate([rows[:, 128:CH], jnp.zeros((count, 256 - CH), F32)], axis=1)
        out[pl.ds(half * (N // 2), N // 2)] = wide[pl.ds(at, SLOTS)].reshape(N // 2, 2 * CAP, 128).astype(BF16)

    def read_wide(held):
        wide[...] = held[...].astype(F32).reshape(2 * SLOTS, 128)
        return wide[pl.ds(0, SLOTS, 2)], wide[pl.ds(1, SLOTS, 2)]

    for half in range(2):
        of_half = pl.ds(half * (SLOTS // 2), SLOTS // 2)
        sampled = None
        for part in range(4):
            rows = [8 * part + k for k in range(8)]
            term = nt(
                jnp.concatenate([spread[y, of_half] for y in rows], axis=1),
                jnp.concatenate([field[y] for y in rows], axis=1),
            )
            sampled = term if sampled is None else sampled + term
        put_wide(half, sampled, answer_out)
        start_exchange(1, answer_out, answer_in, True, half * 8, half * 8 + 8)
    answer_in[me] = answer_out[OWN]

    for k in (2, 3, 6, 7, 8, 9, 10, 11, 12, 13, 14, 15):
        loads[k].wait()
    select_t[...] = (row_iota((SLOTS, STATIONS)).astype(F32) == ahead * CAP + rank).astype(BF16)
    slot_cols = as_columns(slot)
    slot_cols = jnp.concatenate([slot_cols] * (SLOTS // 128), axis=1)
    select[...] = (lane_iota((STATIONS, SLOTS)).astype(F32) == slot_cols).astype(BF16)
    for wide_gain, gain in ((gain1, gain1_ref), (gain2, gain2_ref)):
        cols = as_columns(gain[...])
        wide_gain[...] = jnp.concatenate([cols, cols], axis=1)
    observed_t[...] = jnp.transpose(observed_ref[...])
    mask_t[...] = jnp.transpose(mask_ref[...].astype(F32))
    shown = (observed_t[...] * (1.0 - mask_t[...])).astype(BF16)
    embedded0[...] = nn(in_ref[:, 0:128], shown) + nn(in_ref[:, 128:256], mask_t[...].astype(BF16))
    low = in_ref[:, 256:448].astype(F32)
    in_low[...] = jnp.concatenate([low, jnp.zeros((CH, 64), F32)], axis=1).astype(BF16)
    in_low_t[...] = jnp.transpose(low).astype(BF16)
    qkv_t[...] = flipped(qkv_ref[...])
    out_t[...] = flipped(out_ref[...])
    head_t[...] = flipped(head_ref[...])

    live = live_ref[...].astype(F32)
    station = lane_iota((1, STATIONS)).astype(F32)
    near = neighbours_ref[...].astype(F32)
    used = (row_iota((16, STATIONS)).astype(F32) < count_ref[...].astype(F32)) & (near < live)
    near = jnp.where(used, near, -1.0)
    near = jnp.concatenate([near, station, jnp.full((7, STATIONS), -1.0, F32)], axis=0)
    bias = jnp.concatenate([bias_ref[...], jnp.zeros((8, STATIONS), F32)], axis=0)
    top = jnp.full((24, STATIONS), -1e30, F32)
    for j in range(17):
        top = jnp.where(near == near[j : j + 1], jnp.maximum(top, bias[j : j + 1]), top)
    together = jnp.zeros((24, STATIONS), F32)
    for j in range(17):
        together = together + jnp.where(near == near[j : j + 1], jnp.exp(bias[j : j + 1] - top), 0.0)
    level = top + jnp.log(together)
    other = row_iota(square).astype(F32)
    dense = jnp.full(square, -1e30, F32)
    for j in range(17):
        dense = jnp.where(other == near[j : j + 1], level[j : j + 1], dense)
    scores_bias[...] = dense

    wait_received(1, answer_in)

    low_part, high_part = read_wide(answer_in)
    answers = jnp.concatenate([low_part, high_part], axis=1).astype(BF16)
    interp = nn(select[...], answers).astype(BF16)
    embedded = embedded0[...] + nt(in_low[...], interp)
    scale1 = lax.rsqrt(jnp.mean(embedded * embedded, axis=0, keepdims=True) + EPS)
    unit1 = embedded * scale1
    projected = nn(qkv_t[...], (unit1 * gain1[...]).astype(BF16)).astype(BF16)
    probs, mixed = [], []
    score_scale = 1.0 / 8.0

    def part_of(kind, head):
        at = kind * CH + head * HEAD_DIM
        return projected[at : at + HEAD_DIM]

    for head in range(HEADS):
        score = nn(flipped(part_of(1, head)), part_of(0, head)) * score_scale + scores_bias[...]
        weight = jnp.exp(score - jnp.max(score, axis=0, keepdims=True))
        prob = (weight * (1.0 / jnp.sum(weight, axis=0, keepdims=True))).astype(BF16)
        probs.append(prob)
        mixed.append(nn(part_of(2, head), prob))
    mixed = jnp.concatenate(mixed, axis=0).astype(BF16)
    residual = embedded + nn(out_t[...], mixed)
    scale2 = lax.rsqrt(jnp.mean(residual * residual, axis=0, keepdims=True) + EPS)
    unit2 = residual * scale2
    final = (unit2 * gain2[...]).astype(BF16)
    alive = (station < live).astype(F32)
    predicted = nn(head_t[...], final) * alive
    d_pred = (2.0 * alive * mask_t[...] * (predicted - observed_t[...])).astype(BF16)

    d_unit2 = nn(head_ref[...], d_pred) * gain2[...]
    d_residual = scale2 * (d_unit2 - unit2 * jnp.mean(d_unit2 * unit2, axis=0, keepdims=True))
    d_mixed = nn(out_ref[...], d_residual.astype(BF16)).astype(BF16)
    d_query, d_key, d_value = [], [], []
    for head in range(HEADS):
        d_here = d_mixed[head * HEAD_DIM : (head + 1) * HEAD_DIM]
        prob = probs[head]
        d_prob = nn(flipped(part_of(2, head)), d_here)
        wide_prob = prob.astype(F32)
        d_score = d_prob - jnp.sum(d_prob * wide_prob, axis=0, keepdims=True)
        d_score = (wide_prob * d_score * score_scale).astype(BF16)
        d_query.append(nn(part_of(1, head), d_score))
        d_key.append(nt(part_of(0, head), d_score))
        d_value.append(nt(d_here, prob))
    d_projected = jnp.concatenate(d_query + d_key + d_value, axis=0).astype(BF16)
    d_unit1 = nn(qkv_ref[...], d_projected) * gain1[...]
    d_embedded = d_residual + scale1 * (d_unit1 - unit1 * jnp.mean(d_unit1 * unit1, axis=0, keepdims=True))
    d_interp = nn(in_low_t[...], d_embedded.astype(BF16)).astype(BF16)
    for half in range(2):
        put_wide(half, nt(select_t[pl.ds(half * (SLOTS // 2), SLOTS // 2)], d_interp), grads_out)
        start_exchange(2, grads_out, grads_in, False, half * 8, half * 8 + 8)
    grads_in[OWN] = grads_out[OWN]

    predicted_out[...] = jnp.transpose(predicted)
    stores = [pltpu.make_async_copy(predicted_out, predicted_hbm, store_sem.at[0])]
    stores[0].start()
    for tap in range(9):
        taps_b[:, CH * tap : CH * (tap + 1)] = conv_ref[8 - tap]
    taps_b[:, TAPS:] = jnp.zeros((CH, 2 * ROWS), BF16)
    stores.append(pltpu.make_async_copy(taps_b, taps_hbm, store_sem.at[1]))
    stores[1].start()

    def fill_slope(y, carry):
        pre = before[y]
        gate = sigmoid(pre)
        slope[y] = (gate * (1.0 + pre * (1.0 - gate))).astype(BF16)
        return carry

    lax.fori_loop(0, ROWS, fill_slope, 0, unroll=2)
    slope_ends[...] = nt(pick[...], jnp.concatenate([slope[y] for y in range(ROWS)], axis=1))
    end_row = (place & (ROWS - 1)).astype(F32)
    end_col = jnp.where(place < ROWS, 0.0, COLS - 1.0)
    on_end = jnp.maximum(1.0 - jnp.abs(at_row - end_row), 0.0) * jnp.maximum(1.0 - jnp.abs(at_col - end_col), 0.0)
    ends_spread[...] = jnp.transpose(on_end)[0 : 2 * ROWS].astype(BF16)
    for copy in first_halo:
        copy.wait_send()
    wait_received(2, grads_in)

    low_part, high_part = read_wide(grads_in)
    arrived = jnp.concatenate([low_part, high_part], axis=1)
    at_ends = nn(ends_spread[...], arrived.astype(BF16))[:, 0:CH] * slope_ends[...]
    side_out[1, :, 0:CH] = at_ends.astype(BF16)
    grads_t[...] = jnp.transpose(arrived)[0:CH].astype(BF16)

    def scatter_pair(y0, y1):
        both = nn(grads_t[...], jnp.concatenate([spread[y0], spread[y1]], axis=1))
        for k, y in enumerate((y0, y1)):
            value = both[:, COLS * k : COLS * (k + 1)]
            dfield[y] = value
            dpre[y] = (value * slope[y].astype(F32)).astype(BF16)

    scatter_pair(0, ROWS - 1)
    second_halo = halo_copies(1, dpre.at[0], dpre.at[ROWS - 1], rows_hbm, sides_hbm, corners_hbm)
    for copy in second_halo:
        copy.start()

    def store(source, target):
        copy = pltpu.make_async_copy(source, target, store_sem.at[len(stores)])
        copy.start()
        stores.append(copy)

    store(dfield.at[pl.ds(0, 1)], dfield_hbm.at[pl.ds(0, 1)])
    store(dfield.at[pl.ds(ROWS - 1, 1)], dfield_hbm.at[pl.ds(ROWS - 1, 1)])
    store(dpre.at[pl.ds(0, 1)], dpre_hbm.at[pl.ds(0, 1)])
    store(dpre.at[pl.ds(ROWS - 1, 1)], dpre_hbm.at[pl.ds(ROWS - 1, 1)])
    for third in range(3):

        def scatter_rows(pair, carry):
            y = 1 + 10 * third + 2 * pair
            scatter_pair(y, y + 1)
            return carry

        lax.fori_loop(0, 5, scatter_rows, 0, unroll=True)
        at = pl.ds(1 + 10 * third, 10)
        store(dfield.at[at], dfield_hbm.at[at])
        store(dpre.at[at], dpre_hbm.at[at])
    for copy in second_halo:
        copy.wait_recv()
    for copy in second_halo:
        copy.wait_send()
    wait_sent(0, ask_out)
    wait_sent(1, answer_out)
    wait_sent(2, grads_out)
    for copy in stores:
        copy.wait()


PARTS = ((0, 4), (4, 10), (14, 10), (24, 8))


def back_kernel(*refs):
    (dpre_hbm, dfield_hbm, predicted_hbm, grad_hbm, predicted_to) = refs[0:2] + refs[7:10]
    (dpre, dfield, taps, row_in, side_in, corner_in, conv_ref, shifted, grad, sem) = refs[10:20]
    keep = poles(lax.axis_index("lat"))
    small = [pltpu.make_async_copy(refs[k], refs[10 + k], sem.at[k]) for k in range(2, 7)]
    load_taps, load_rows, load_sides, load_corners, load_conv = small
    through = pltpu.make_async_copy(predicted_hbm, predicted_to, sem.at[7])

    def load(part):
        first, count = PARTS[part]
        begin = first + 1 if part else 0
        end = min(first + count + 1, ROWS)
        at, fields = pl.ds(begin, end - begin), pl.ds(first, count)
        return (
            pltpu.make_async_copy(dpre_hbm.at[at], dpre.at[at], sem.at[8 + part]),
            pltpu.make_async_copy(dfield_hbm.at[fields], dfield.at[fields], sem.at[12 + part]),
        )

    def store(part):
        fields = pl.ds(*PARTS[part])
        return pltpu.make_async_copy(grad.at[fields], grad_hbm.at[fields], sem.at[16 + part])

    loads = [load(part) for part in range(4)]
    for copy in (load_sides, load_corners, load_conv, load_rows, loads[0][0], load_taps, loads[0][1]):
        copy.start()
    for part in range(1, 4):
        for copy in loads[part]:
            copy.start()
    through.start()

    def rows_of(part):
        first, count = PARTS[part]
        return list(range(first + 1 if part else -1, min(first + count + 1, ROWS))) + ([ROWS] if part == 3 else [])

    def shift_row(y):
        if y < 0:
            fill_shifted(shifted, 0, row_in[0].astype(F32) * keep[0])
        elif y == ROWS:
            fill_shifted(shifted, ROWS + 1, row_in[1].astype(F32) * keep[1])
        else:
            fill_shifted(shifted, y + 1, dpre[y].astype(F32))

    for copy in (load_sides, load_corners, load_conv, load_taps):
        copy.wait()
    side_terms(side_in, corner_in, conv_ref, taps, keep, True)
    load_rows.wait()
    loads[0][0].wait()
    for y in rows_of(0):
        shift_row(y)
    for part in range(4):
        loads[part][1].wait()
        first, count = PARTS[part]
        coming = []
        if part < 3:
            loads[part + 1][0].wait()
            coming = rows_of(part + 1)
        for pair in range(count // 2):
            y = first + pair * 2
            back = nn(taps[...], jnp.concatenate([around(shifted, y), around(shifted, y + 1)], axis=1))
            for k in range(2):
                grad[y + k] = dfield[y + k] + back[:, COLS * k : COLS * (k + 1)]
            share = -(-len(coming) // (count // 2 - pair))
            for row in coming[:share]:
                shift_row(row)
            coming = coming[share:]
        store(part).start()
    for part in range(4):
        store(part).wait()
    through.wait()


def on_device(
    grid_field,
    conv_weight,
    observed,
    hidden_mask,
    tile_route,
    station_spot,
    neighbours,
    neighbour_count,
    edge_bias,
    live_count,
    in_weight,
    norm_gain,
    qkv_weight,
    out_weight,
    final_gain,
    head_weight,
):
    operands = (
        jnp.transpose(grid_field, (0, 2, 1)),
        conv_weight,
        observed,
        hidden_mask,
        tile_route.reshape(1, STATIONS),
        station_spot.reshape(1, STATIONS),
        neighbours.T,
        neighbour_count.reshape(1, STATIONS),
        edge_bias.T,
        live_count.reshape(1, 1),
        in_weight.T,
        norm_gain.reshape(1, CH),
        qkv_weight,
        out_weight,
        final_gain.reshape(1, CH),
        head_weight,
    )
    anywhere = pl.BlockSpec(memory_space=pl.ANY)

    def vmem(*shape, kind=BF16):
        return pltpu.VMEM(shape, kind)

    predicted, dpre, dfield, taps, rows, sides, corners = pl.pallas_call(
        kernel,
        out_shape=(
            jax.ShapeDtypeStruct((STATIONS, 128), F32),
            jax.ShapeDtypeStruct((ROWS, CH, COLS), BF16),
            jax.ShapeDtypeStruct((ROWS, CH, COLS), F32),
            jax.ShapeDtypeStruct((CH, DEPTH), BF16),
            jax.ShapeDtypeStruct((2, CH, COLS), BF16),
            jax.ShapeDtypeStruct((2, ROWS, 256), BF16),
            jax.ShapeDtypeStruct((4, 16, 256), BF16),
        ),
        in_specs=[anywhere] * len(operands),
        out_specs=(anywhere,) * 7,
        scratch_shapes=[pltpu.VMEM(o.shape, o.dtype) for o in operands]
        + [
            vmem(ROWS + 2, 3, CH, COLS),
            vmem(CH, DEPTH),
            vmem(CH, DEPTH),
            vmem(ROWS, CH, COLS),
            vmem(ROWS, CH, COLS),
            vmem(ROWS, SLOTS, COLS),
            vmem(ROWS, CH, COLS),
            vmem(ROWS, CH, COLS, kind=F32),
            vmem(2 * ROWS, ROWS * COLS),
            vmem(N, 2 * CAP, 128),
            vmem(N, 2 * CAP, 128),
            vmem(N, 2 * CAP, 128),
            vmem(N, 2 * CAP, 128),
            vmem(N, 1, 128, kind=F32),
            vmem(N, 1, 128, kind=F32),
            vmem(2 * SLOTS, 128, kind=F32),
            vmem(2, CH, COLS),
            vmem(2, 2 * ROWS, 256),
            vmem(2, ROWS, 256),
            vmem(4, 16, 256),
            vmem(STATIONS, SLOTS),
            vmem(SLOTS, STATIONS),
            vmem(STATIONS, STATIONS, kind=F32),
            vmem(CH, SLOTS),
            vmem(CH, STATIONS, kind=F32),
            vmem(CH, STATIONS, kind=F32),
            vmem(CH, STATIONS, kind=F32),
            vmem(CH, 256),
            vmem(CH, CH),
            vmem(3 * CH, CH),
            vmem(CH, CH),
            vmem(128, CH),
            vmem(128, STATIONS, kind=F32),
            vmem(128, STATIONS, kind=F32),
            vmem(2 * ROWS, SLOTS),
            vmem(2 * ROWS, CH, kind=F32),
            vmem(STATIONS, 128, kind=F32),
            vmem(ROWS, CH, COLS, kind=F32),
            pltpu.SemaphoreType.DMA((2, 8)),
            pltpu.SemaphoreType.DMA((2, 8)),
            pltpu.SemaphoreType.DMA((3,)),
            pltpu.SemaphoreType.DMA((3,)),
            pltpu.SemaphoreType.DMA((16,)),
            pltpu.SemaphoreType.DMA((16,)),
        ],
        compiler_params=pltpu.CompilerParams(
            collective_id=0, has_side_effects=True, vmem_limit_bytes=56 << 20
        ),
        name="whole",
    )(*operands)
    gradient, predicted = pl.pallas_call(
        back_kernel,
        out_shape=(
            jax.ShapeDtypeStruct((ROWS, CH, COLS), F32),
            jax.ShapeDtypeStruct((STATIONS, 128), F32),
        ),
        in_specs=[anywhere] * 8,
        out_specs=(anywhere, anywhere),
        scratch_shapes=[
            vmem(ROWS, CH, COLS),
            vmem(ROWS, CH, COLS, kind=F32),
            vmem(CH, DEPTH),
            vmem(2, CH, COLS),
            vmem(2, ROWS, 256),
            vmem(4, 16, 256),
            vmem(9, CH, CH),
            vmem(ROWS + 2, 3, CH, COLS),
            vmem(ROWS, CH, COLS, kind=F32),
            pltpu.SemaphoreType.DMA((20,)),
        ],
        compiler_params=pltpu.CompilerParams(vmem_limit_bytes=60 << 20),
        name="back",
    )(dpre, dfield, taps, rows, sides, corners, conv_weight, predicted)
    return predicted, jnp.transpose(gradient, (0, 2, 1))


def solution(mesh):
    return jax.shard_map(
        on_device,
        mesh=mesh,
        in_specs=(
            P("lat", "lon", None),
            P(),
            P(LAT_LON, None),
            P(LAT_LON, None),
            P(LAT_LON, None),
            P(LAT_LON),
            P(LAT_LON, None),
            P(LAT_LON),
            P(LAT_LON, None),
            P(LAT_LON),
            P(),
            P(),
            P(),
            P(),
            P(),
            P(),
        ),
        out_specs=(P(LAT_LON, None), P("lat", "lon", None)),
        check_vma=False,
    )
```

```python
import jax
import jax.numpy as jnp
from jax import lax
from jax.experimental import pallas as pl
from jax.experimental.pallas import tpu as pltpu
from jax.sharding import PartitionSpec as P

CH = 192
HEADS = 3
HEAD_DIM = 64
ROWS = 32
COLS = 128
FINE = 4 * (COLS - 1)
CAP = 4
N = 128
N_LAT = 4
N_LON = 32
SLOTS = N * CAP
STATIONS = 256
TAPS = 9 * CH
DEPTH = TAPS + 2 * ROWS
EPS = 1e-06
F32 = jnp.float32
BF16 = jnp.bfloat16
LAT_LON = ("lat", "lon")
HOPS = (0, 1, 2, 1)
GROUPS = sorted(((dx, dz) for dx in range(4) for dz in range(4)), key=lambda d: -HOPS[d[0]] - HOPS[d[1]])
OWN = 8 * GROUPS.index((0, 0)) + 5


def nn(a, b):
    return lax.dot_general(a, b, (((1,), (0,)), ((), ())), preferred_element_type=F32)


def nt(a, b):
    return lax.dot_general(a, b, (((1,), (1,)), ((), ())), preferred_element_type=F32)


def lane_iota(shape):
    return lax.broadcasted_iota(jnp.int32, shape, len(shape) - 1)


def row_iota(shape):
    return lax.broadcasted_iota(jnp.int32, shape, len(shape) - 2)


def as_columns(row):
    return jnp.transpose(jnp.broadcast_to(row, (128, row.shape[1])))


def flipped(value):
    return jnp.transpose(value.astype(F32)).astype(BF16)


def sigmoid(v):
    return 0.5 * (1.0 + jnp.tanh(0.5 * v))


def fill_shifted(shifted, y, value):
    lane = lane_iota((CH, COLS))
    shifted[y, 1] = value.astype(BF16)
    shifted[y, 0] = jnp.where(lane == 0, 0.0, pltpu.roll(value, 1, 1)).astype(BF16)
    shifted[y, 2] = jnp.where(lane == COLS - 1, 0.0, pltpu.roll(value, COLS - 1, 1)).astype(BF16)


def end_hits(y):
    ends_at = row_iota((2 * ROWS, COLS))
    lane = lane_iota((2 * ROWS, COLS))
    hit = ((ends_at == y) & (lane == 0)) | ((ends_at == y + ROWS) & (lane == COLS - 1))
    return hit.astype(F32).astype(BF16)


def around(shifted, y):
    return jnp.concatenate([shifted[pl.ds(y, 3)].reshape(TAPS, COLS), end_hits(y)], axis=0)


PARTS = ((0, 4), (4, 10), (14, 10), (24, 8))
EARLY = 2
COMING = (tuple(range(0, 5)), tuple(range(5, 15)), (), tuple(range(23, 32)))


def poles(lat):
    return jnp.where(lat > 0, 1.0, 0.0), jnp.where(lat < N_LAT - 1, 1.0, 0.0)


def side_terms(side_in, corner_in, conv_ref, taps, keep, backward):
    total = []
    for side in range(2):
        above = corner_in[side].astype(F32)[15:16, 0:CH] * keep[0]
        below = corner_in[2 + side].astype(F32)[0:1, 0:CH] * keep[1]
        column = jnp.concatenate([above, side_in[side].astype(F32)[:, 0:CH], below], axis=0)
        sums = None
        for i in range(3):
            piece = column[i : i + ROWS].astype(BF16)
            if backward:
                term = nt(piece, conv_ref[8 - (3 * i + 2 * side)])
            else:
                term = nn(piece, conv_ref[3 * i + 2 * side])
            sums = term if sums is None else sums + term
        total.append(sums)
    total = jnp.concatenate(total + [jnp.zeros((64, CH), F32)], axis=0)
    taps[:, TAPS:] = jnp.transpose(total)[:, 0 : 2 * ROWS].astype(BF16)


def kernel(*refs):
    inputs = refs[0:16]
    (predicted_hbm, dpre_hbm, dfield_hbm, taps_hbm, rows_hbm, sides_hbm, corners_hbm) = refs[16:23]
    refs = refs[3:]
    (x_ref, conv_ref, observed_ref, mask_ref, tile_ref, spot_ref, neighbours_ref, count_ref) = refs[20:28]
    (bias_ref, live_ref, in_ref, gain1_ref, qkv_ref, out_ref, gain2_ref, head_ref) = refs[28:36]
    (shifted, taps_f, taps_b, field, slope, spread, dpre, dfield, pick) = refs[36:45]
    (answer_out, answer_in, grads_out, grads_in, ask_out, ask_in, wide) = refs[45:52]
    (row_in, side_out, side_in, corner_in, select, select_t, scores_bias, grads_t) = refs[52:60]
    (embedded0, gain1, gain2, in_low, in_low_t, qkv_t, out_t, head_t, mask_t, observed_t) = refs[60:70]
    (ends_spread, slope_ends, predicted_out, before) = refs[70:74]
    (halo_send, halo_recv, a2a_send, a2a_recv, load_sem, store_sem) = refs[74:80]

    loads = [pltpu.make_async_copy(inputs[k], refs[20 + k], load_sem.at[k]) for k in range(16)]
    for k in (4, 5, 0, 1, 2, 3, 6, 7, 8, 9, 10, 11, 12, 13, 14, 15):
        loads[k].start()
    lat = lax.axis_index("lat")
    lon = lax.axis_index("lon")
    me = lat * N_LON + lon
    at_z, at_core = lax.div(lon, 8), lax.rem(lon, 2)
    at_y = lax.rem(lax.div(lon, 2), 4)
    barrier = pltpu.get_barrier_semaphore()

    def coords(peer):
        return (lax.div(peer, N_LON), lax.rem(peer, N_LON))

    def greet(i, carry):
        pl.semaphore_signal(
            barrier, inc=1, device_id=coords(lax.rem(me + i, N)), device_id_type=pl.DeviceIdType.MESH
        )
        return carry

    lax.fori_loop(1, N, greet, 0)

    loads[4].wait()
    loads[5].wait()
    tile_row = tile_ref[...].astype(F32)
    tile_cols = as_columns(tile_row)
    tile_cols = jnp.concatenate([tile_cols, tile_cols], axis=1)
    square = (STATIONS, STATIONS)
    same = (tile_cols == tile_row) & (row_iota(square) < lane_iota(square))
    rank = jnp.sum(same.astype(F32), axis=0, keepdims=True)
    slot = tile_row * CAP + rank

    def ring(value, here):
        ahead = value - here.astype(F32)
        return jnp.where(ahead < 0.0, ahead + 4.0, ahead)

    tile_x = jnp.floor(tile_row * (1.0 / 32.0))
    tile_z = jnp.floor((tile_row - 32.0 * tile_x) * (1.0 / 8.0))
    tile_pair = jnp.floor(tile_row * 0.5)
    tile_y = tile_pair - 4.0 * jnp.floor(tile_pair * 0.25)
    step = 4.0 * ring(tile_x, lat) + ring(tile_z, at_z)
    group = jnp.zeros_like(step)
    for index, (dx, dz) in enumerate(GROUPS):
        group = jnp.where(step == 4.0 * dx + dz, float(index), group)
    back_y = ring(2.0 - ring(tile_y, at_y), jnp.int32(0))
    same_core = 1.0 - jnp.abs(tile_row - 2.0 * tile_pair - at_core.astype(F32))
    ahead = 8.0 * group + 2.0 * back_y + same_core
    spot = spot_ref[...].astype(F32)
    spot_high = jnp.floor(spot * (1.0 / 256.0))
    spot_low = spot - 256.0 * spot_high
    part = row_iota((128, STATIONS))
    wanted = jnp.where(part < CAP, spot_high, spot_low)
    wanted = jnp.where((part & (CAP - 1)).astype(F32) == rank, wanted, 0.0)
    wanted = jnp.where(part < 2 * CAP, wanted, 0.0).astype(BF16)
    is_tile = (row_iota((N, STATIONS)).astype(F32) == ahead).astype(BF16)
    ask_out[...] = nt(is_tile, wanted).reshape(N, 1, 128)

    end = row_iota((2 * ROWS, ROWS * COLS))
    end_cell = jnp.where(end < ROWS, end * COLS, (end - ROWS) * COLS + COLS - 1)
    pick[...] = (lane_iota((2 * ROWS, ROWS * COLS)) == end_cell).astype(F32).astype(BF16)
    side_out[...] = jnp.zeros((2, 2 * ROWS, 256), BF16)
    loads[0].wait()
    side_out[0, :, 0:CH] = nt(pick[...], jnp.concatenate([x_ref[y] for y in range(ROWS)], axis=1)).astype(BF16)

    up, down = lax.rem(lat + N_LAT - 1, N_LAT), lax.rem(lat + 1, N_LAT)
    left, right = lax.rem(lon + N_LON - 1, N_LON), lax.rem(lon + 1, N_LON)

    def halo_copies(turn, first, last, rows_to, sides_to, corners_to):
        mine = side_out.at[turn]
        plan = [
            (mine.at[pl.ds(0, ROWS)], sides_to.at[1], (lat, left)),
            (mine.at[pl.ds(ROWS, ROWS)], sides_to.at[0], (lat, right)),
            (mine.at[pl.ds(0, 16)], corners_to.at[3], (up, left)),
            (mine.at[pl.ds(ROWS, 16)], corners_to.at[2], (up, right)),
            (mine.at[pl.ds(16, 16)], corners_to.at[1], (down, left)),
            (mine.at[pl.ds(ROWS + 16, 16)], corners_to.at[0], (down, right)),
            (first, rows_to.at[1], (up, lon)),
            (last, rows_to.at[0], (down, lon)),
        ]
        return [
            pltpu.make_async_remote_copy(
                src_ref=source,
                dst_ref=target,
                send_sem=halo_send.at[turn, k],
                recv_sem=halo_recv.at[turn, k],
                device_id=where,
                device_id_type=pl.DeviceIdType.MESH,
            )
            for k, (source, target, where) in enumerate(plan)
        ]

    def start_exchange(turn, source, target, by_tile, first=0, last=16):
        for group in range(first, last):
            dx, dz = GROUPS[group]
            opposite = GROUPS.index((-dx % 4, -dz % 4))

            def send(k, carry):
                d = lax.div(k, 2)
                e = k - 2 * d
                x, z = lax.rem(lat + dx, 4), lax.rem(at_z + dz, 4)
                y, core = lax.rem(at_y + 6 - d, 4), lax.rem(at_core + 1 - e, 2)
                pltpu.make_async_remote_copy(
                    src_ref=source.at[8 * group + k],
                    dst_ref=target.at[me if by_tile else 8 * opposite + 2 * lax.rem(4 - d, 4) + e],
                    send_sem=a2a_send.at[turn],
                    recv_sem=a2a_recv.at[turn],
                    device_id=(x, (z * 4 + y) * 2 + core),
                    device_id_type=pl.DeviceIdType.MESH,
                ).start()
                return carry

            if OWN // 8 == group:
                lax.fori_loop(0, OWN % 8, send, 0)
                lax.fori_loop(OWN % 8 + 1, 8, send, 0)
            else:
                lax.fori_loop(0, 8, send, 0)

    def wait_received(turn, target):
        rest = target.at[pl.ds(0, N - 1)]
        pltpu.make_async_copy(rest, rest, a2a_recv.at[turn]).wait()

    def wait_sent(turn, source):
        rest = source.at[pl.ds(0, N - 1)]
        pltpu.make_async_copy(rest, rest, a2a_send.at[turn]).wait()

    pl.semaphore_wait(barrier, N - 1)
    first_halo = halo_copies(0, x_ref.at[0], x_ref.at[ROWS - 1], row_in, side_in, corner_in)
    for copy in first_halo:
        copy.start()
    start_exchange(0, ask_out, ask_in, False)
    ask_in[OWN] = ask_out[OWN]

    def fill_row(y, carry):
        fill_shifted(shifted, y + 1, x_ref[y].astype(F32))
        return carry

    lax.fori_loop(0, ROWS, fill_row, 0, unroll=2)
    loads[1].wait()
    for tap in range(9):
        taps_f[:, CH * tap : CH * (tap + 1)] = flipped(conv_ref[tap])

    keep = poles(lat)
    for copy in first_halo:
        copy.wait_recv()
    fill_shifted(shifted, 0, row_in[0].astype(F32) * keep[0])
    fill_shifted(shifted, ROWS + 1, row_in[1].astype(F32) * keep[1])
    side_terms(side_in, corner_in, conv_ref, taps_f, keep, False)

    def forward_rows(pair, carry):
        y = pair * 2
        pre = nn(taps_f[...], jnp.concatenate([around(shifted, y), around(shifted, y + 1)], axis=1))
        gate = sigmoid(pre)
        moved = pre * gate
        for k in range(2):
            cut = slice(COLS * k, COLS * (k + 1))
            field[y + k] = (x_ref[y + k].astype(F32) + moved[:, cut]).astype(BF16)
            before[y + k] = pre[:, cut]
        return carry

    lax.fori_loop(0, ROWS // 2, forward_rows, 0, unroll=4)

    wait_received(0, ask_in)
    asked = ask_in[...].reshape(N, 128).astype(BF16)
    repeat = (row_iota((SLOTS, N)) // CAP == lane_iota((SLOTS, N))).astype(BF16)
    asked = nn(repeat, asked)
    place = lane_iota((SLOTS, 128))
    turn_of = row_iota((SLOTS, 128)) & (CAP - 1)
    spots = jnp.where(place == turn_of, asked * 256.0, 0.0) + jnp.where(place == turn_of + CAP, asked, 0.0)
    spots = jnp.sum(spots, axis=1, keepdims=True)
    fine_row = jnp.floor((spots + 0.5) * (1.0 / FINE))
    fine_col = spots - FINE * fine_row
    at_row = jnp.broadcast_to((fine_row + 0.5) * 0.25, (SLOTS, COLS))
    at_col = jnp.broadcast_to((fine_col + 0.5) * 0.25, (SLOTS, COLS))
    along = jnp.maximum(1.0 - jnp.abs(at_col - place.astype(F32)), 0.0).astype(BF16)
    at_row16 = at_row.astype(BF16)

    def fill_spread(y, carry):
        away = jnp.abs(at_row16 - y.astype(BF16))
        spread[y] = jnp.maximum(1.0 - away, 0.0).astype(BF16) * along
        return carry

    lax.fori_loop(0, ROWS, fill_spread, 0, unroll=4)

    def put_wide(half, rows, out):
        count = SLOTS // 2
        at = half * SLOTS
        wide[pl.ds(at, count, 2)] = rows[:, 0:128]
        wide[pl.ds(at + 1, count, 2)] = jnp.concatenate([rows[:, 128:CH], jnp.zeros((count, 256 - CH), F32)], axis=1)
        out[pl.ds(half * (N // 2), N // 2)] = wide[pl.ds(at, SLOTS)].reshape(N // 2, 2 * CAP, 128).astype(BF16)

    def read_wide(held):
        wide[...] = held[...].astype(F32).reshape(2 * SLOTS, 128)
        return wide[pl.ds(0, SLOTS, 2)], wide[pl.ds(1, SLOTS, 2)]

    for half in range(2):
        of_half = pl.ds(half * (SLOTS // 2), SLOTS // 2)
        sampled = None
        for part in range(4):
            rows = [8 * part + k for k in range(8)]
            term = nt(
                jnp.concatenate([spread[y, of_half] for y in rows], axis=1),
                jnp.concatenate([field[y] for y in rows], axis=1),
            )
            sampled = term if sampled is None else sampled + term
        put_wide(half, sampled, answer_out)
        start_exchange(1, answer_out, answer_in, True, half * 8, half * 8 + 8)
    answer_in[me] = answer_out[OWN]

    for k in (2, 3, 6, 7, 8, 9, 10, 11, 12, 13, 14, 15):
        loads[k].wait()
    select_t[...] = (row_iota((SLOTS, STATIONS)).astype(F32) == ahead * CAP + rank).astype(BF16)
    slot_cols = as_columns(slot)
    slot_cols = jnp.concatenate([slot_cols] * (SLOTS // 128), axis=1)
    select[...] = (lane_iota((STATIONS, SLOTS)).astype(F32) == slot_cols).astype(BF16)
    for wide_gain, gain in ((gain1, gain1_ref), (gain2, gain2_ref)):
        cols = as_columns(gain[...])
        wide_gain[...] = jnp.concatenate([cols, cols], axis=1)
    observed_t[...] = jnp.transpose(observed_ref[...])
    mask_t[...] = jnp.transpose(mask_ref[...].astype(F32))
    shown = (observed_t[...] * (1.0 - mask_t[...])).astype(BF16)
    embedded0[...] = nn(in_ref[:, 0:128], shown) + nn(in_ref[:, 128:256], mask_t[...].astype(BF16))
    low = in_ref[:, 256:448].astype(F32)
    in_low[...] = jnp.concatenate([low, jnp.zeros((CH, 64), F32)], axis=1).astype(BF16)
    in_low_t[...] = jnp.transpose(low).astype(BF16)
    qkv_t[...] = flipped(qkv_ref[...])
    out_t[...] = flipped(out_ref[...])
    head_t[...] = flipped(head_ref[...])

    live = live_ref[...].astype(F32)
    station = lane_iota((1, STATIONS)).astype(F32)
    near = neighbours_ref[...].astype(F32)
    used = (row_iota((16, STATIONS)).astype(F32) < count_ref[...].astype(F32)) & (near < live)
    near = jnp.where(used, near, -1.0)
    near = jnp.concatenate([near, station, jnp.full((7, STATIONS), -1.0, F32)], axis=0)
    bias = jnp.concatenate([bias_ref[...], jnp.zeros((8, STATIONS), F32)], axis=0)
    top = jnp.full((24, STATIONS), -1e30, F32)
    for j in range(17):
        top = jnp.where(near == near[j : j + 1], jnp.maximum(top, bias[j : j + 1]), top)
    together = jnp.zeros((24, STATIONS), F32)
    for j in range(17):
        together = together + jnp.where(near == near[j : j + 1], jnp.exp(bias[j : j + 1] - top), 0.0)
    level = top + jnp.log(together)
    other = row_iota(square).astype(F32)
    dense = jnp.full(square, -1e30, F32)
    for j in range(17):
        dense = jnp.where(other == near[j : j + 1], level[j : j + 1], dense)
    scores_bias[...] = dense

    wait_received(1, answer_in)

    low_part, high_part = read_wide(answer_in)
    answers = jnp.concatenate([low_part, high_part], axis=1).astype(BF16)
    interp = nn(select[...], answers).astype(BF16)
    embedded = embedded0[...] + nt(in_low[...], interp)
    scale1 = lax.rsqrt(jnp.mean(embedded * embedded, axis=0, keepdims=True) + EPS)
    unit1 = embedded * scale1
    projected = nn(qkv_t[...], (unit1 * gain1[...]).astype(BF16)).astype(BF16)
    probs, mixed = [], []
    score_scale = 1.0 / 8.0

    def part_of(kind, head):
        at = kind * CH + head * HEAD_DIM
        return projected[at : at + HEAD_DIM]

    for head in range(HEADS):
        score = nn(flipped(part_of(1, head)), part_of(0, head)) * score_scale + scores_bias[...]
        weight = jnp.exp(score - jnp.max(score, axis=0, keepdims=True))
        prob = (weight * (1.0 / jnp.sum(weight, axis=0, keepdims=True))).astype(BF16)
        probs.append(prob)
        mixed.append(nn(part_of(2, head), prob))
    mixed = jnp.concatenate(mixed, axis=0).astype(BF16)
    residual = embedded + nn(out_t[...], mixed)
    scale2 = lax.rsqrt(jnp.mean(residual * residual, axis=0, keepdims=True) + EPS)
    unit2 = residual * scale2
    final = (unit2 * gain2[...]).astype(BF16)
    alive = (station < live).astype(F32)
    predicted = nn(head_t[...], final) * alive
    d_pred = (2.0 * alive * mask_t[...] * (predicted - observed_t[...])).astype(BF16)

    d_unit2 = nn(head_ref[...], d_pred) * gain2[...]
    d_residual = scale2 * (d_unit2 - unit2 * jnp.mean(d_unit2 * unit2, axis=0, keepdims=True))
    d_mixed = nn(out_ref[...], d_residual.astype(BF16)).astype(BF16)
    d_query, d_key, d_value = [], [], []
    for head in range(HEADS):
        d_here = d_mixed[head * HEAD_DIM : (head + 1) * HEAD_DIM]
        prob = probs[head]
        d_prob = nn(flipped(part_of(2, head)), d_here)
        wide_prob = prob.astype(F32)
        d_score = d_prob - jnp.sum(d_prob * wide_prob, axis=0, keepdims=True)
        d_score = (wide_prob * d_score * score_scale).astype(BF16)
        d_query.append(nn(part_of(1, head), d_score))
        d_key.append(nt(part_of(0, head), d_score))
        d_value.append(nt(d_here, prob))
    d_projected = jnp.concatenate(d_query + d_key + d_value, axis=0).astype(BF16)
    d_unit1 = nn(qkv_ref[...], d_projected) * gain1[...]
    d_embedded = d_residual + scale1 * (d_unit1 - unit1 * jnp.mean(d_unit1 * unit1, axis=0, keepdims=True))
    d_interp = nn(in_low_t[...], d_embedded.astype(BF16)).astype(BF16)
    for half in range(2):
        put_wide(half, nt(select_t[pl.ds(half * (SLOTS // 2), SLOTS // 2)], d_interp), grads_out)
        start_exchange(2, grads_out, grads_in, False, half * 8, half * 8 + 8)
    grads_in[OWN] = grads_out[OWN]

    predicted_out[...] = jnp.transpose(predicted)
    stores = [pltpu.make_async_copy(predicted_out, predicted_hbm, store_sem.at[0])]
    stores[0].start()
    for tap in range(9):
        taps_b[:, CH * tap : CH * (tap + 1)] = conv_ref[8 - tap]
    taps_b[:, TAPS:] = jnp.zeros((CH, 2 * ROWS), BF16)
    stores.append(pltpu.make_async_copy(taps_b, taps_hbm, store_sem.at[1]))
    stores[1].start()

    def fill_slope(y, carry):
        pre = before[y]
        gate = sigmoid(pre)
        slope[y] = (gate * (1.0 + pre * (1.0 - gate))).astype(BF16)
        return carry

    lax.fori_loop(0, ROWS, fill_slope, 0, unroll=2)
    slope_ends[...] = nt(pick[...], jnp.concatenate([slope[y] for y in range(ROWS)], axis=1))
    end_row = (place & (ROWS - 1)).astype(F32)
    end_col = jnp.where(place < ROWS, 0.0, COLS - 1.0)
    on_end = jnp.maximum(1.0 - jnp.abs(at_row - end_row), 0.0) * jnp.maximum(1.0 - jnp.abs(at_col - end_col), 0.0)
    ends_spread[...] = jnp.transpose(on_end)[0 : 2 * ROWS].astype(BF16)
    for copy in first_halo:
        copy.wait_send()
    wait_received(2, grads_in)

    low_part, high_part = read_wide(grads_in)
    arrived = jnp.concatenate([low_part, high_part], axis=1)
    at_ends = nn(ends_spread[...], arrived.astype(BF16))[:, 0:CH] * slope_ends[...]
    side_out[1, :, 0:CH] = at_ends.astype(BF16)
    grads_t[...] = jnp.transpose(arrived)[0:CH].astype(BF16)

    def scatter_pair(y0, y1):
        both = nn(grads_t[...], jnp.concatenate([spread[y0], spread[y1]], axis=1))
        for k, y in enumerate((y0, y1)):
            value = both[:, COLS * k : COLS * (k + 1)]
            dfield[y] = value
            dpre[y] = (value * slope[y].astype(F32)).astype(BF16)

    scatter_pair(0, ROWS - 1)
    second_halo = halo_copies(1, dpre.at[0], dpre.at[ROWS - 1], rows_hbm, sides_hbm, corners_hbm)
    for copy in second_halo:
        copy.start()

    def store(source, target):
        copy = pltpu.make_async_copy(source, target, store_sem.at[len(stores)])
        copy.start()
        stores.append(copy)

    store(dfield.at[pl.ds(0, 1)], dfield_hbm.at[pl.ds(0, 1)])
    store(dfield.at[pl.ds(ROWS - 1, 1)], dfield_hbm.at[pl.ds(ROWS - 1, 1)])
    store(dpre.at[pl.ds(0, 1)], dpre_hbm.at[pl.ds(0, 1)])
    store(dpre.at[pl.ds(ROWS - 1, 1)], dpre_hbm.at[pl.ds(ROWS - 1, 1)])
    for third in range(3):

        def scatter_rows(pair, carry):
            y = 1 + 10 * third + 2 * pair
            scatter_pair(y, y + 1)
            return carry

        lax.fori_loop(0, 5, scatter_rows, 0, unroll=True)
        at = (pl.ds(1, 10), pl.ds(11, 3), pl.ds(24, 7))[third]
        store(dfield.at[at], dfield_hbm.at[at])
        at = pl.ds(1 + 10 * third, 10)
        store(dpre.at[at], dpre_hbm.at[at])
    first, count = PARTS[EARLY]
    for y in range(first - 1, first + 3):
        fill_shifted(shifted, y + 1, dpre[y].astype(F32))
    for y in range(first, first + count, 2):
        back = nn(taps_b[...], jnp.concatenate([around(shifted, y), around(shifted, y + 1)], axis=1))
        for k in range(2):
            dfield[y + k] = dfield[y + k] + back[:, COLS * k : COLS * (k + 1)]
            if y + 2 < first + count:
                fill_shifted(shifted, y + k + 4, dpre[y + k + 3].astype(F32))
    store(dfield.at[pl.ds(first, count)], dfield_hbm.at[pl.ds(first, count)])
    for copy in second_halo:
        copy.wait_recv()
    for copy in second_halo:
        copy.wait_send()
    wait_sent(0, ask_out)
    wait_sent(1, answer_out)
    wait_sent(2, grads_out)
    for copy in stores:
        copy.wait()


def back_kernel(*refs):
    (dpre_hbm, dfield_hbm, predicted_hbm, grad_hbm, predicted_to) = refs[0:2] + refs[7:10]
    (dpre, dfield, taps, row_in, side_in, corner_in, conv_ref, shifted, grad, sem) = refs[10:20]
    keep = poles(lax.axis_index("lat"))
    small = [pltpu.make_async_copy(refs[k], refs[10 + k], sem.at[k]) for k in range(2, 7)]
    load_taps, load_rows, load_sides, load_corners, load_conv = small
    through = pltpu.make_async_copy(predicted_hbm, predicted_to, sem.at[7])

    def load(part):
        fields = pl.ds(*PARTS[part])
        copies = [pltpu.make_async_copy(dfield_hbm.at[fields], dfield.at[fields], sem.at[12 + part])]
        if COMING[part]:
            at = pl.ds(COMING[part][0], len(COMING[part]))
            copies.append(pltpu.make_async_copy(dpre_hbm.at[at], dpre.at[at], sem.at[8 + part]))
        return copies

    def store(part):
        fields = pl.ds(*PARTS[part])
        return pltpu.make_async_copy(grad.at[fields], grad_hbm.at[fields], sem.at[16 + part])

    loads = [load(part) for part in range(4)]
    for copy in (load_sides, load_corners, load_conv, load_rows, loads[0][1], load_taps, loads[0][0]):
        copy.start()
    for part in range(1, 4):
        for copy in reversed(loads[part]):
            copy.start()
    through.start()

    def shift_row(y):
        if y < 0:
            fill_shifted(shifted, 0, row_in[0].astype(F32) * keep[0])
        elif y == ROWS:
            fill_shifted(shifted, ROWS + 1, row_in[1].astype(F32) * keep[1])
        else:
            fill_shifted(shifted, y + 1, dpre[y].astype(F32))

    for copy in (load_sides, load_corners, load_conv, load_taps):
        copy.wait()
    side_terms(side_in, corner_in, conv_ref, taps, keep, True)
    load_rows.wait()
    loads[0][1].wait()
    for y in (-1,) + COMING[0]:
        shift_row(y)
    end_taps = taps[:, TAPS:]
    for part in range(4):
        loads[part][0].wait()
        first, count = PARTS[part]
        coming = []
        if part == 0:
            loads[1][1].wait()
            coming = COMING[1]
        elif part == 1:
            loads[3][1].wait()
            coming = COMING[3] + (ROWS,)
        for pair in range(count // 2):
            y = first + pair * 2
            if part == EARLY:
                back = nn(end_taps, jnp.concatenate([end_hits(y), end_hits(y + 1)], axis=1))
            else:
                back = nn(taps[...], jnp.concatenate([around(shifted, y), around(shifted, y + 1)], axis=1))
            for k in range(2):
                grad[y + k] = dfield[y + k] + back[:, COLS * k : COLS * (k + 1)]
            share = -(-len(coming) // (count // 2 - pair))
            for row in coming[:share]:
                shift_row(row)
            coming = coming[share:]
        store(part).start()
    for part in range(4):
        store(part).wait()
    through.wait()


def on_device(
    grid_field,
    conv_weight,
    observed,
    hidden_mask,
    tile_route,
    station_spot,
    neighbours,
    neighbour_count,
    edge_bias,
    live_count,
    in_weight,
    norm_gain,
    qkv_weight,
    out_weight,
    final_gain,
    head_weight,
):
    operands = (
        jnp.transpose(grid_field, (0, 2, 1)),
        conv_weight,
        observed,
        hidden_mask,
        tile_route.reshape(1, STATIONS),
        station_spot.reshape(1, STATIONS),
        neighbours.T,
        neighbour_count.reshape(1, STATIONS),
        edge_bias.T,
        live_count.reshape(1, 1),
        in_weight.T,
        norm_gain.reshape(1, CH),
        qkv_weight,
        out_weight,
        final_gain.reshape(1, CH),
        head_weight,
    )
    anywhere = pl.BlockSpec(memory_space=pl.ANY)

    def vmem(*shape, kind=BF16):
        return pltpu.VMEM(shape, kind)

    predicted, dpre, dfield, taps, rows, sides, corners = pl.pallas_call(
        kernel,
        out_shape=(
            jax.ShapeDtypeStruct((STATIONS, 128), F32),
            jax.ShapeDtypeStruct((ROWS, CH, COLS), BF16),
            jax.ShapeDtypeStruct((ROWS, CH, COLS), F32),
            jax.ShapeDtypeStruct((CH, DEPTH), BF16),
            jax.ShapeDtypeStruct((2, CH, COLS), BF16),
            jax.ShapeDtypeStruct((2, ROWS, 256), BF16),
            jax.ShapeDtypeStruct((4, 16, 256), BF16),
        ),
        in_specs=[anywhere] * len(operands),
        out_specs=(anywhere,) * 7,
        scratch_shapes=[pltpu.VMEM(o.shape, o.dtype) for o in operands]
        + [
            vmem(ROWS + 2, 3, CH, COLS),
            vmem(CH, DEPTH),
            vmem(CH, DEPTH),
            vmem(ROWS, CH, COLS),
            vmem(ROWS, CH, COLS),
            vmem(ROWS, SLOTS, COLS),
            vmem(ROWS, CH, COLS),
            vmem(ROWS, CH, COLS, kind=F32),
            vmem(2 * ROWS, ROWS * COLS),
            vmem(N, 2 * CAP, 128),
            vmem(N, 2 * CAP, 128),
            vmem(N, 2 * CAP, 128),
            vmem(N, 2 * CAP, 128),
            vmem(N, 1, 128, kind=F32),
            vmem(N, 1, 128, kind=F32),
            vmem(2 * SLOTS, 128, kind=F32),
            vmem(2, CH, COLS),
            vmem(2, 2 * ROWS, 256),
            vmem(2, ROWS, 256),
            vmem(4, 16, 256),
            vmem(STATIONS, SLOTS),
            vmem(SLOTS, STATIONS),
            vmem(STATIONS, STATIONS, kind=F32),
            vmem(CH, SLOTS),
            vmem(CH, STATIONS, kind=F32),
            vmem(CH, STATIONS, kind=F32),
            vmem(CH, STATIONS, kind=F32),
            vmem(CH, 256),
            vmem(CH, CH),
            vmem(3 * CH, CH),
            vmem(CH, CH),
            vmem(128, CH),
            vmem(128, STATIONS, kind=F32),
            vmem(128, STATIONS, kind=F32),
            vmem(2 * ROWS, SLOTS),
            vmem(2 * ROWS, CH, kind=F32),
            vmem(STATIONS, 128, kind=F32),
            vmem(ROWS, CH, COLS, kind=F32),
            pltpu.SemaphoreType.DMA((2, 8)),
            pltpu.SemaphoreType.DMA((2, 8)),
            pltpu.SemaphoreType.DMA((3,)),
            pltpu.SemaphoreType.DMA((3,)),
            pltpu.SemaphoreType.DMA((16,)),
            pltpu.SemaphoreType.DMA((16,)),
        ],
        compiler_params=pltpu.CompilerParams(
            collective_id=0, has_side_effects=True, vmem_limit_bytes=56 << 20
        ),
        name="whole",
    )(*operands)
    gradient, predicted = pl.pallas_call(
        back_kernel,
        out_shape=(
            jax.ShapeDtypeStruct((ROWS, CH, COLS), F32),
            jax.ShapeDtypeStruct((STATIONS, 128), F32),
        ),
        in_specs=[anywhere] * 8,
        out_specs=(anywhere, anywhere),
        scratch_shapes=[
            vmem(ROWS, CH, COLS),
            vmem(ROWS, CH, COLS, kind=F32),
            vmem(CH, DEPTH),
            vmem(2, CH, COLS),
            vmem(2, ROWS, 256),
            vmem(4, 16, 256),
            vmem(9, CH, CH),
            vmem(ROWS + 2, 3, CH, COLS),
            vmem(ROWS, CH, COLS, kind=F32),
            pltpu.SemaphoreType.DMA((20,)),
        ],
        compiler_params=pltpu.CompilerParams(vmem_limit_bytes=60 << 20),
        name="back",
    )(dpre, dfield, taps, rows, sides, corners, conv_weight, predicted)
    return predicted, jnp.transpose(gradient, (0, 2, 1))


def solution(mesh):
    return jax.shard_map(
        on_device,
        mesh=mesh,
        in_specs=(
            P("lat", "lon", None),
            P(),
            P(LAT_LON, None),
            P(LAT_LON, None),
            P(LAT_LON, None),
            P(LAT_LON),
            P(LAT_LON, None),
            P(LAT_LON),
            P(LAT_LON, None),
            P(LAT_LON),
            P(),
            P(),
            P(),
            P(),
            P(),
            P(),
        ),
        out_specs=(P(LAT_LON, None), P("lat", "lon", None)),
        check_vma=False,
    )
```

```python
import jax
import jax.numpy as jnp
from jax import lax
from jax.experimental import pallas as pl
from jax.experimental.pallas import tpu as pltpu
from jax.sharding import PartitionSpec as P

CH = 192
HEADS = 3
HEAD_DIM = 64
ROWS = 32
COLS = 128
FINE = 4 * (COLS - 1)
CAP = 4
N = 128
N_LAT = 4
N_LON = 32
SLOTS = N * CAP
STATIONS = 256
TAPS = 9 * CH
DEPTH = TAPS + 2 * ROWS
EPS = 1e-06
F32 = jnp.float32
BF16 = jnp.bfloat16
LAT_LON = ("lat", "lon")
HOPS = (0, 1, 2, 1)
GROUPS = sorted(((dx, dz) for dx in range(4) for dz in range(4)), key=lambda d: -HOPS[d[0]] - HOPS[d[1]])
OWN = 8 * GROUPS.index((0, 0)) + 5


def nn(a, b):
    return lax.dot_general(a, b, (((1,), (0,)), ((), ())), preferred_element_type=F32)


def nt(a, b):
    return lax.dot_general(a, b, (((1,), (1,)), ((), ())), preferred_element_type=F32)


def lane_iota(shape):
    return lax.broadcasted_iota(jnp.int32, shape, len(shape) - 1)


def row_iota(shape):
    return lax.broadcasted_iota(jnp.int32, shape, len(shape) - 2)


def as_columns(row):
    return jnp.transpose(jnp.broadcast_to(row, (128, row.shape[1])))


def flipped(value):
    return jnp.transpose(value.astype(F32)).astype(BF16)


def sigmoid(v):
    return 0.5 * (1.0 + jnp.tanh(0.5 * v))


def fill_shifted(shifted, y, value):
    lane = lane_iota((CH, COLS))
    shifted[y, 1] = value.astype(BF16)
    shifted[y, 0] = jnp.where(lane == 0, 0.0, pltpu.roll(value, 1, 1)).astype(BF16)
    shifted[y, 2] = jnp.where(lane == COLS - 1, 0.0, pltpu.roll(value, COLS - 1, 1)).astype(BF16)


def end_hits(y):
    ends_at = row_iota((2 * ROWS, COLS))
    lane = lane_iota((2 * ROWS, COLS))
    hit = ((ends_at == y) & (lane == 0)) | ((ends_at == y + ROWS) & (lane == COLS - 1))
    return hit.astype(F32).astype(BF16)


def around(shifted, y):
    return jnp.concatenate([shifted[pl.ds(y, 3)].reshape(TAPS, COLS), end_hits(y)], axis=0)


PARTS = ((0, 4), (4, 6), (10, 14), (24, 8))
EARLY = 2
COMING = (tuple(range(0, 5)), tuple(range(5, 11)), (), tuple(range(23, 32)))


def poles(lat):
    return jnp.where(lat > 0, 1.0, 0.0), jnp.where(lat < N_LAT - 1, 1.0, 0.0)


def side_terms(side_in, corner_in, conv_ref, taps, keep, backward):
    total = []
    for side in range(2):
        above = corner_in[side].astype(F32)[15:16, 0:CH] * keep[0]
        below = corner_in[2 + side].astype(F32)[0:1, 0:CH] * keep[1]
        column = jnp.concatenate([above, side_in[side].astype(F32)[:, 0:CH], below], axis=0)
        sums = None
        for i in range(3):
            piece = column[i : i + ROWS].astype(BF16)
            if backward:
                term = nt(piece, conv_ref[8 - (3 * i + 2 * side)])
            else:
                term = nn(piece, conv_ref[3 * i + 2 * side])
            sums = term if sums is None else sums + term
        total.append(sums)
    total = jnp.concatenate(total + [jnp.zeros((64, CH), F32)], axis=0)
    taps[:, TAPS:] = jnp.transpose(total)[:, 0 : 2 * ROWS].astype(BF16)


def kernel(*refs):
    inputs = refs[0:16]
    (predicted_hbm, dpre_hbm, dfield_hbm, taps_hbm, rows_hbm, sides_hbm, corners_hbm) = refs[16:23]
    refs = refs[3:]
    (x_ref, conv_ref, observed_ref, mask_ref, tile_ref, spot_ref, neighbours_ref, count_ref) = refs[20:28]
    (bias_ref, live_ref, in_ref, gain1_ref, qkv_ref, out_ref, gain2_ref, head_ref) = refs[28:36]
    (shifted, taps_f, taps_b, field, slope, spread, dpre, dfield, pick) = refs[36:45]
    (answer_out, answer_in, grads_out, grads_in, ask_out, ask_in, wide) = refs[45:52]
    (row_in, side_out, side_in, corner_in, select, select_t, scores_bias, grads_t) = refs[52:60]
    (embedded0, gain1, gain2, in_low, in_low_t, qkv_t, out_t, head_t, mask_t, observed_t) = refs[60:70]
    (ends_spread, slope_ends, predicted_out, before) = refs[70:74]
    (halo_send, halo_recv, a2a_send, a2a_recv, load_sem, store_sem) = refs[74:80]

    loads = [pltpu.make_async_copy(inputs[k], refs[20 + k], load_sem.at[k]) for k in range(16)]
    for k in (4, 5, 0, 1, 2, 3, 6, 7, 8, 9, 10, 11, 12, 13, 14, 15):
        loads[k].start()
    lat = lax.axis_index("lat")
    lon = lax.axis_index("lon")
    me = lat * N_LON + lon
    at_z, at_core = lax.div(lon, 8), lax.rem(lon, 2)
    at_y = lax.rem(lax.div(lon, 2), 4)
    barrier = pltpu.get_barrier_semaphore()

    def coords(peer):
        return (lax.div(peer, N_LON), lax.rem(peer, N_LON))

    def greet(i, carry):
        pl.semaphore_signal(
            barrier, inc=1, device_id=coords(lax.rem(me + i, N)), device_id_type=pl.DeviceIdType.MESH
        )
        return carry

    lax.fori_loop(1, N, greet, 0)

    loads[4].wait()
    loads[5].wait()
    tile_row = tile_ref[...].astype(F32)
    tile_cols = as_columns(tile_row)
    tile_cols = jnp.concatenate([tile_cols, tile_cols], axis=1)
    square = (STATIONS, STATIONS)
    same = (tile_cols == tile_row) & (row_iota(square) < lane_iota(square))
    rank = jnp.sum(same.astype(F32), axis=0, keepdims=True)
    slot = tile_row * CAP + rank

    def ring(value, here):
        ahead = value - here.astype(F32)
        return jnp.where(ahead < 0.0, ahead + 4.0, ahead)

    tile_x = jnp.floor(tile_row * (1.0 / 32.0))
    tile_z = jnp.floor((tile_row - 32.0 * tile_x) * (1.0 / 8.0))
    tile_pair = jnp.floor(tile_row * 0.5)
    tile_y = tile_pair - 4.0 * jnp.floor(tile_pair * 0.25)
    step = 4.0 * ring(tile_x, lat) + ring(tile_z, at_z)
    group = jnp.zeros_like(step)
    for index, (dx, dz) in enumerate(GROUPS):
        group = jnp.where(step == 4.0 * dx + dz, float(index), group)
    back_y = ring(2.0 - ring(tile_y, at_y), jnp.int32(0))
    same_core = 1.0 - jnp.abs(tile_row - 2.0 * tile_pair - at_core.astype(F32))
    ahead = 8.0 * group + 2.0 * back_y + same_core
    spot = spot_ref[...].astype(F32)
    spot_high = jnp.floor(spot * (1.0 / 256.0))
    spot_low = spot - 256.0 * spot_high
    part = row_iota((128, STATIONS))
    wanted = jnp.where(part < CAP, spot_high, spot_low)
    wanted = jnp.where((part & (CAP - 1)).astype(F32) == rank, wanted, 0.0)
    wanted = jnp.where(part < 2 * CAP, wanted, 0.0).astype(BF16)
    is_tile = (row_iota((N, STATIONS)).astype(F32) == ahead).astype(BF16)
    ask_out[...] = nt(is_tile, wanted).reshape(N, 1, 128)

    end = row_iota((2 * ROWS, ROWS * COLS))
    end_cell = jnp.where(end < ROWS, end * COLS, (end - ROWS) * COLS + COLS - 1)
    pick[...] = (lane_iota((2 * ROWS, ROWS * COLS)) == end_cell).astype(F32).astype(BF16)
    side_out[...] = jnp.zeros((2, 2 * ROWS, 256), BF16)
    loads[0].wait()
    side_out[0, :, 0:CH] = nt(pick[...], jnp.concatenate([x_ref[y] for y in range(ROWS)], axis=1)).astype(BF16)

    up, down = lax.rem(lat + N_LAT - 1, N_LAT), lax.rem(lat + 1, N_LAT)
    left, right = lax.rem(lon + N_LON - 1, N_LON), lax.rem(lon + 1, N_LON)

    def halo_copies(turn, first, last, rows_to, sides_to, corners_to):
        mine = side_out.at[turn]
        plan = [
            (mine.at[pl.ds(0, ROWS)], sides_to.at[1], (lat, left)),
            (mine.at[pl.ds(ROWS, ROWS)], sides_to.at[0], (lat, right)),
            (mine.at[pl.ds(0, 16)], corners_to.at[3], (up, left)),
            (mine.at[pl.ds(ROWS, 16)], corners_to.at[2], (up, right)),
            (mine.at[pl.ds(16, 16)], corners_to.at[1], (down, left)),
            (mine.at[pl.ds(ROWS + 16, 16)], corners_to.at[0], (down, right)),
            (first, rows_to.at[1], (up, lon)),
            (last, rows_to.at[0], (down, lon)),
        ]
        return [
            pltpu.make_async_remote_copy(
                src_ref=source,
                dst_ref=target,
                send_sem=halo_send.at[turn, k],
                recv_sem=halo_recv.at[turn, k],
                device_id=where,
                device_id_type=pl.DeviceIdType.MESH,
            )
            for k, (source, target, where) in enumerate(plan)
        ]

    def start_exchange(turn, source, target, by_tile, first=0, last=16):
        for group in range(first, last):
            dx, dz = GROUPS[group]
            opposite = GROUPS.index((-dx % 4, -dz % 4))

            def send(k, carry):
                d = lax.div(k, 2)
                e = k - 2 * d
                x, z = lax.rem(lat + dx, 4), lax.rem(at_z + dz, 4)
                y, core = lax.rem(at_y + 6 - d, 4), lax.rem(at_core + 1 - e, 2)
                pltpu.make_async_remote_copy(
                    src_ref=source.at[8 * group + k],
                    dst_ref=target.at[me if by_tile else 8 * opposite + 2 * lax.rem(4 - d, 4) + e],
                    send_sem=a2a_send.at[turn],
                    recv_sem=a2a_recv.at[turn],
                    device_id=(x, (z * 4 + y) * 2 + core),
                    device_id_type=pl.DeviceIdType.MESH,
                ).start()
                return carry

            if OWN // 8 == group:
                lax.fori_loop(0, OWN % 8, send, 0)
                lax.fori_loop(OWN % 8 + 1, 8, send, 0)
            else:
                lax.fori_loop(0, 8, send, 0)

    def wait_received(turn, target):
        rest = target.at[pl.ds(0, N - 1)]
        pltpu.make_async_copy(rest, rest, a2a_recv.at[turn]).wait()

    def wait_sent(turn, source):
        rest = source.at[pl.ds(0, N - 1)]
        pltpu.make_async_copy(rest, rest, a2a_send.at[turn]).wait()

    pl.semaphore_wait(barrier, N - 1)
    first_halo = halo_copies(0, x_ref.at[0], x_ref.at[ROWS - 1], row_in, side_in, corner_in)
    for copy in first_halo:
        copy.start()
    start_exchange(0, ask_out, ask_in, False)
    ask_in[OWN] = ask_out[OWN]

    def fill_row(y, carry):
        fill_shifted(shifted, y + 1, x_ref[y].astype(F32))
        return carry

    lax.fori_loop(0, ROWS, fill_row, 0, unroll=2)
    loads[1].wait()
    for tap in range(9):
        taps_f[:, CH * tap : CH * (tap + 1)] = flipped(conv_ref[tap])

    keep = poles(lat)
    for copy in first_halo:
        copy.wait_recv()
    fill_shifted(shifted, 0, row_in[0].astype(F32) * keep[0])
    fill_shifted(shifted, ROWS + 1, row_in[1].astype(F32) * keep[1])
    side_terms(side_in, corner_in, conv_ref, taps_f, keep, False)

    def forward_rows(pair, carry):
        y = pair * 2
        pre = nn(taps_f[...], jnp.concatenate([around(shifted, y), around(shifted, y + 1)], axis=1))
        gate = sigmoid(pre)
        moved = pre * gate
        for k in range(2):
            cut = slice(COLS * k, COLS * (k + 1))
            field[y + k] = (x_ref[y + k].astype(F32) + moved[:, cut]).astype(BF16)
            before[y + k] = pre[:, cut]
        return carry

    lax.fori_loop(0, ROWS // 2, forward_rows, 0, unroll=4)

    wait_received(0, ask_in)
    asked = ask_in[...].reshape(N, 128).astype(BF16)
    repeat = (row_iota((SLOTS, N)) // CAP == lane_iota((SLOTS, N))).astype(BF16)
    asked = nn(repeat, asked)
    place = lane_iota((SLOTS, 128))
    turn_of = row_iota((SLOTS, 128)) & (CAP - 1)
    spots = jnp.where(place == turn_of, asked * 256.0, 0.0) + jnp.where(place == turn_of + CAP, asked, 0.0)
    spots = jnp.sum(spots, axis=1, keepdims=True)
    fine_row = jnp.floor((spots + 0.5) * (1.0 / FINE))
    fine_col = spots - FINE * fine_row
    at_row = jnp.broadcast_to((fine_row + 0.5) * 0.25, (SLOTS, COLS))
    at_col = jnp.broadcast_to((fine_col + 0.5) * 0.25, (SLOTS, COLS))
    along = jnp.maximum(1.0 - jnp.abs(at_col - place.astype(F32)), 0.0).astype(BF16)
    at_row16 = at_row.astype(BF16)

    def fill_spread(y, carry):
        away = jnp.abs(at_row16 - y.astype(BF16))
        spread[y] = jnp.maximum(1.0 - away, 0.0).astype(BF16) * along
        return carry

    lax.fori_loop(0, ROWS, fill_spread, 0, unroll=4)

    def put_wide(half, rows, out):
        count = SLOTS // 2
        at = half * SLOTS
        wide[pl.ds(at, count, 2)] = rows[:, 0:128]
        wide[pl.ds(at + 1, count, 2)] = jnp.concatenate([rows[:, 128:CH], jnp.zeros((count, 256 - CH), F32)], axis=1)
        out[pl.ds(half * (N // 2), N // 2)] = wide[pl.ds(at, SLOTS)].reshape(N // 2, 2 * CAP, 128).astype(BF16)

    def read_wide(held):
        wide[...] = held[...].astype(F32).reshape(2 * SLOTS, 128)
        return wide[pl.ds(0, SLOTS, 2)], wide[pl.ds(1, SLOTS, 2)]

    for half in range(2):
        of_half = pl.ds(half * (SLOTS // 2), SLOTS // 2)
        sampled = None
        for part in range(4):
            rows = [8 * part + k for k in range(8)]
            term = nt(
                jnp.concatenate([spread[y, of_half] for y in rows], axis=1),
                jnp.concatenate([field[y] for y in rows], axis=1),
            )
            sampled = term if sampled is None else sampled + term
        put_wide(half, sampled, answer_out)
        start_exchange(1, answer_out, answer_in, True, half * 8, half * 8 + 8)
    answer_in[me] = answer_out[OWN]

    for k in (2, 3, 6, 7, 8, 9, 10, 11, 12, 13, 14, 15):
        loads[k].wait()
    select_t[...] = (row_iota((SLOTS, STATIONS)).astype(F32) == ahead * CAP + rank).astype(BF16)
    slot_cols = as_columns(slot)
    slot_cols = jnp.concatenate([slot_cols] * (SLOTS // 128), axis=1)
    select[...] = (lane_iota((STATIONS, SLOTS)).astype(F32) == slot_cols).astype(BF16)
    for wide_gain, gain in ((gain1, gain1_ref), (gain2, gain2_ref)):
        cols = as_columns(gain[...])
        wide_gain[...] = jnp.concatenate([cols, cols], axis=1)
    observed_t[...] = jnp.transpose(observed_ref[...])
    mask_t[...] = jnp.transpose(mask_ref[...].astype(F32))
    shown = (observed_t[...] * (1.0 - mask_t[...])).astype(BF16)
    embedded0[...] = nn(in_ref[:, 0:128], shown) + nn(in_ref[:, 128:256], mask_t[...].astype(BF16))
    low = in_ref[:, 256:448].astype(F32)
    in_low[...] = jnp.concatenate([low, jnp.zeros((CH, 64), F32)], axis=1).astype(BF16)
    in_low_t[...] = jnp.transpose(low).astype(BF16)
    qkv_t[...] = flipped(qkv_ref[...])
    out_t[...] = flipped(out_ref[...])
    head_t[...] = flipped(head_ref[...])

    live = live_ref[...].astype(F32)
    station = lane_iota((1, STATIONS)).astype(F32)
    near = neighbours_ref[...].astype(F32)
    used = (row_iota((16, STATIONS)).astype(F32) < count_ref[...].astype(F32)) & (near < live)
    near = jnp.where(used, near, -1.0)
    near = jnp.concatenate([near, station, jnp.full((7, STATIONS), -1.0, F32)], axis=0)
    bias = jnp.concatenate([bias_ref[...], jnp.zeros((8, STATIONS), F32)], axis=0)
    top = jnp.full((24, STATIONS), -1e30, F32)
    for j in range(17):
        top = jnp.where(near == near[j : j + 1], jnp.maximum(top, bias[j : j + 1]), top)
    together = jnp.zeros((24, STATIONS), F32)
    for j in range(17):
        together = together + jnp.where(near == near[j : j + 1], jnp.exp(bias[j : j + 1] - top), 0.0)
    level = top + jnp.log(together)
    other = row_iota(square).astype(F32)
    dense = jnp.full(square, -1e30, F32)
    for j in range(17):
        dense = jnp.where(other == near[j : j + 1], level[j : j + 1], dense)
    scores_bias[...] = dense

    wait_received(1, answer_in)

    low_part, high_part = read_wide(answer_in)
    answers = jnp.concatenate([low_part, high_part], axis=1).astype(BF16)
    interp = nn(select[...], answers).astype(BF16)
    embedded = embedded0[...] + nt(in_low[...], interp)
    scale1 = lax.rsqrt(jnp.mean(embedded * embedded, axis=0, keepdims=True) + EPS)
    unit1 = embedded * scale1
    projected = nn(qkv_t[...], (unit1 * gain1[...]).astype(BF16)).astype(BF16)
    probs, mixed = [], []
    score_scale = 1.0 / 8.0

    def part_of(kind, head):
        at = kind * CH + head * HEAD_DIM
        return projected[at : at + HEAD_DIM]

    for head in range(HEADS):
        score = nn(flipped(part_of(1, head)), part_of(0, head)) * score_scale + scores_bias[...]
        weight = jnp.exp(score - jnp.max(score, axis=0, keepdims=True))
        prob = (weight * (1.0 / jnp.sum(weight, axis=0, keepdims=True))).astype(BF16)
        probs.append(prob)
        mixed.append(nn(part_of(2, head), prob))
    mixed = jnp.concatenate(mixed, axis=0).astype(BF16)
    residual = embedded + nn(out_t[...], mixed)
    scale2 = lax.rsqrt(jnp.mean(residual * residual, axis=0, keepdims=True) + EPS)
    unit2 = residual * scale2
    final = (unit2 * gain2[...]).astype(BF16)
    alive = (station < live).astype(F32)
    predicted = nn(head_t[...], final) * alive
    d_pred = (2.0 * alive * mask_t[...] * (predicted - observed_t[...])).astype(BF16)

    d_unit2 = nn(head_ref[...], d_pred) * gain2[...]
    d_residual = scale2 * (d_unit2 - unit2 * jnp.mean(d_unit2 * unit2, axis=0, keepdims=True))
    d_mixed = nn(out_ref[...], d_residual.astype(BF16)).astype(BF16)
    d_query, d_key, d_value = [], [], []
    for head in range(HEADS):
        d_here = d_mixed[head * HEAD_DIM : (head + 1) * HEAD_DIM]
        prob = probs[head]
        d_prob = nn(flipped(part_of(2, head)), d_here)
        wide_prob = prob.astype(F32)
        d_score = d_prob - jnp.sum(d_prob * wide_prob, axis=0, keepdims=True)
        d_score = (wide_prob * d_score * score_scale).astype(BF16)
        d_query.append(nn(part_of(1, head), d_score))
        d_key.append(nt(part_of(0, head), d_score))
        d_value.append(nt(d_here, prob))
    d_projected = jnp.concatenate(d_query + d_key + d_value, axis=0).astype(BF16)
    d_unit1 = nn(qkv_ref[...], d_projected) * gain1[...]
    d_embedded = d_residual + scale1 * (d_unit1 - unit1 * jnp.mean(d_unit1 * unit1, axis=0, keepdims=True))
    d_interp = nn(in_low_t[...], d_embedded.astype(BF16)).astype(BF16)
    for half in range(2):
        put_wide(half, nt(select_t[pl.ds(half * (SLOTS // 2), SLOTS // 2)], d_interp), grads_out)
        start_exchange(2, grads_out, grads_in, False, half * 8, half * 8 + 8)
    grads_in[OWN] = grads_out[OWN]

    predicted_out[...] = jnp.transpose(predicted)
    stores = [pltpu.make_async_copy(predicted_out, predicted_hbm, store_sem.at[0])]
    stores[0].start()
    for tap in range(9):
        taps_b[:, CH * tap : CH * (tap + 1)] = conv_ref[8 - tap]
    taps_b[:, TAPS:] = jnp.zeros((CH, 2 * ROWS), BF16)
    stores.append(pltpu.make_async_copy(taps_b, taps_hbm, store_sem.at[1]))
    stores[1].start()

    def fill_slope(y, carry):
        pre = before[y]
        gate = sigmoid(pre)
        slope[y] = (gate * (1.0 + pre * (1.0 - gate))).astype(BF16)
        return carry

    lax.fori_loop(0, ROWS, fill_slope, 0, unroll=2)
    slope_ends[...] = nt(pick[...], jnp.concatenate([slope[y] for y in range(ROWS)], axis=1))
    end_row = (place & (ROWS - 1)).astype(F32)
    end_col = jnp.where(place < ROWS, 0.0, COLS - 1.0)
    on_end = jnp.maximum(1.0 - jnp.abs(at_row - end_row), 0.0) * jnp.maximum(1.0 - jnp.abs(at_col - end_col), 0.0)
    ends_spread[...] = jnp.transpose(on_end)[0 : 2 * ROWS].astype(BF16)
    for copy in first_halo:
        copy.wait_send()
    wait_received(2, grads_in)

    low_part, high_part = read_wide(grads_in)
    arrived = jnp.concatenate([low_part, high_part], axis=1)
    at_ends = nn(ends_spread[...], arrived.astype(BF16))[:, 0:CH] * slope_ends[...]
    side_out[1, :, 0:CH] = at_ends.astype(BF16)
    grads_t[...] = jnp.transpose(arrived)[0:CH].astype(BF16)

    def scatter_pair(y0, y1):
        both = nn(grads_t[...], jnp.concatenate([spread[y0], spread[y1]], axis=1))
        for k, y in enumerate((y0, y1)):
            value = both[:, COLS * k : COLS * (k + 1)]
            dfield[y] = value
            dpre[y] = (value * slope[y].astype(F32)).astype(BF16)

    scatter_pair(0, ROWS - 1)
    second_halo = halo_copies(1, dpre.at[0], dpre.at[ROWS - 1], rows_hbm, sides_hbm, corners_hbm)
    for copy in second_halo:
        copy.start()

    def store(source, target):
        copy = pltpu.make_async_copy(source, target, store_sem.at[len(stores)])
        copy.start()
        stores.append(copy)

    store(dfield.at[pl.ds(0, 1)], dfield_hbm.at[pl.ds(0, 1)])
    store(dfield.at[pl.ds(ROWS - 1, 1)], dfield_hbm.at[pl.ds(ROWS - 1, 1)])
    store(dpre.at[pl.ds(0, 1)], dpre_hbm.at[pl.ds(0, 1)])
    store(dpre.at[pl.ds(ROWS - 1, 1)], dpre_hbm.at[pl.ds(ROWS - 1, 1)])
    for third in range(3):

        def scatter_rows(pair, carry):
            y = 1 + 10 * third + 2 * pair
            scatter_pair(y, y + 1)
            return carry

        lax.fori_loop(0, 5, scatter_rows, 0, unroll=True)
        at = (pl.ds(1, 9), None, pl.ds(24, 7))[third]
        if at is not None:
            store(dfield.at[at], dfield_hbm.at[at])
        at = pl.ds(1 + 10 * third, 10)
        store(dpre.at[at], dpre_hbm.at[at])
    first, count = PARTS[EARLY]
    for y in range(first - 1, first + 3):
        fill_shifted(shifted, y + 1, dpre[y].astype(F32))
    for y in range(first, first + count, 2):
        back = nn(taps_b[...], jnp.concatenate([around(shifted, y), around(shifted, y + 1)], axis=1))
        for k in range(2):
            dfield[y + k] = dfield[y + k] + back[:, COLS * k : COLS * (k + 1)]
            if y + 2 < first + count:
                fill_shifted(shifted, y + k + 4, dpre[y + k + 3].astype(F32))
    store(dfield.at[pl.ds(first, count)], dfield_hbm.at[pl.ds(first, count)])
    for copy in second_halo:
        copy.wait_recv()
    for copy in second_halo:
        copy.wait_send()
    wait_sent(0, ask_out)
    wait_sent(1, answer_out)
    wait_sent(2, grads_out)
    for copy in stores:
        copy.wait()


def back_kernel(*refs):
    (dpre_hbm, dfield_hbm, predicted_hbm, grad_hbm, predicted_to) = refs[0:2] + refs[7:10]
    (dpre, dfield, taps, row_in, side_in, corner_in, conv_ref, shifted, grad, sem) = refs[10:20]
    keep = poles(lax.axis_index("lat"))
    small = [pltpu.make_async_copy(refs[k], refs[10 + k], sem.at[k]) for k in range(2, 7)]
    load_taps, load_rows, load_sides, load_corners, load_conv = small
    through = pltpu.make_async_copy(predicted_hbm, predicted_to, sem.at[7])

    def load(part):
        fields = pl.ds(*PARTS[part])
        copies = [pltpu.make_async_copy(dfield_hbm.at[fields], dfield.at[fields], sem.at[12 + part])]
        if COMING[part]:
            at = pl.ds(COMING[part][0], len(COMING[part]))
            copies.append(pltpu.make_async_copy(dpre_hbm.at[at], dpre.at[at], sem.at[8 + part]))
        return copies

    def store(part):
        fields = pl.ds(*PARTS[part])
        return pltpu.make_async_copy(grad.at[fields], grad_hbm.at[fields], sem.at[16 + part])

    loads = [load(part) for part in range(4)]
    for copy in (load_sides, load_corners, load_conv, load_rows, loads[0][1], load_taps, loads[0][0]):
        copy.start()
    for part in range(1, 4):
        for copy in reversed(loads[part]):
            copy.start()
    through.start()

    def shift_row(y):
        if y < 0:
            fill_shifted(shifted, 0, row_in[0].astype(F32) * keep[0])
        elif y == ROWS:
            fill_shifted(shifted, ROWS + 1, row_in[1].astype(F32) * keep[1])
        else:
            fill_shifted(shifted, y + 1, dpre[y].astype(F32))

    for copy in (load_sides, load_corners, load_conv, load_taps):
        copy.wait()
    side_terms(side_in, corner_in, conv_ref, taps, keep, True)
    load_rows.wait()
    loads[0][1].wait()
    for y in (-1,) + COMING[0]:
        shift_row(y)
    end_taps = taps[:, TAPS:]
    for part in range(4):
        loads[part][0].wait()
        first, count = PARTS[part]
        coming = []
        if part == 0:
            loads[1][1].wait()
            coming = COMING[1]
        elif part == 1:
            loads[3][1].wait()
            coming = COMING[3] + (ROWS,)
        for pair in range(count // 2):
            y = first + pair * 2
            if part == EARLY:
                back = nn(end_taps, jnp.concatenate([end_hits(y), end_hits(y + 1)], axis=1))
            else:
                back = nn(taps[...], jnp.concatenate([around(shifted, y), around(shifted, y + 1)], axis=1))
            for k in range(2):
                grad[y + k] = dfield[y + k] + back[:, COLS * k : COLS * (k + 1)]
            share = -(-len(coming) // (count // 2 - pair))
            for row in coming[:share]:
                shift_row(row)
            coming = coming[share:]
        store(part).start()
    for part in range(4):
        store(part).wait()
    through.wait()


def on_device(
    grid_field,
    conv_weight,
    observed,
    hidden_mask,
    tile_route,
    station_spot,
    neighbours,
    neighbour_count,
    edge_bias,
    live_count,
    in_weight,
    norm_gain,
    qkv_weight,
    out_weight,
    final_gain,
    head_weight,
):
    operands = (
        jnp.transpose(grid_field, (0, 2, 1)),
        conv_weight,
        observed,
        hidden_mask,
        tile_route.reshape(1, STATIONS),
        station_spot.reshape(1, STATIONS),
        neighbours.T,
        neighbour_count.reshape(1, STATIONS),
        edge_bias.T,
        live_count.reshape(1, 1),
        in_weight.T,
        norm_gain.reshape(1, CH),
        qkv_weight,
        out_weight,
        final_gain.reshape(1, CH),
        head_weight,
    )
    anywhere = pl.BlockSpec(memory_space=pl.ANY)

    def vmem(*shape, kind=BF16):
        return pltpu.VMEM(shape, kind)

    predicted, dpre, dfield, taps, rows, sides, corners = pl.pallas_call(
        kernel,
        out_shape=(
            jax.ShapeDtypeStruct((STATIONS, 128), F32),
            jax.ShapeDtypeStruct((ROWS, CH, COLS), BF16),
            jax.ShapeDtypeStruct((ROWS, CH, COLS), F32),
            jax.ShapeDtypeStruct((CH, DEPTH), BF16),
            jax.ShapeDtypeStruct((2, CH, COLS), BF16),
            jax.ShapeDtypeStruct((2, ROWS, 256), BF16),
            jax.ShapeDtypeStruct((4, 16, 256), BF16),
        ),
        in_specs=[anywhere] * len(operands),
        out_specs=(anywhere,) * 7,
        scratch_shapes=[pltpu.VMEM(o.shape, o.dtype) for o in operands]
        + [
            vmem(ROWS + 2, 3, CH, COLS),
            vmem(CH, DEPTH),
            vmem(CH, DEPTH),
            vmem(ROWS, CH, COLS),
            vmem(ROWS, CH, COLS),
            vmem(ROWS, SLOTS, COLS),
            vmem(ROWS, CH, COLS),
            vmem(ROWS, CH, COLS, kind=F32),
            vmem(2 * ROWS, ROWS * COLS),
            vmem(N, 2 * CAP, 128),
            vmem(N, 2 * CAP, 128),
            vmem(N, 2 * CAP, 128),
            vmem(N, 2 * CAP, 128),
            vmem(N, 1, 128, kind=F32),
            vmem(N, 1, 128, kind=F32),
            vmem(2 * SLOTS, 128, kind=F32),
            vmem(2, CH, COLS),
            vmem(2, 2 * ROWS, 256),
            vmem(2, ROWS, 256),
            vmem(4, 16, 256),
            vmem(STATIONS, SLOTS),
            vmem(SLOTS, STATIONS),
            vmem(STATIONS, STATIONS, kind=F32),
            vmem(CH, SLOTS),
            vmem(CH, STATIONS, kind=F32),
            vmem(CH, STATIONS, kind=F32),
            vmem(CH, STATIONS, kind=F32),
            vmem(CH, 256),
            vmem(CH, CH),
            vmem(3 * CH, CH),
            vmem(CH, CH),
            vmem(128, CH),
            vmem(128, STATIONS, kind=F32),
            vmem(128, STATIONS, kind=F32),
            vmem(2 * ROWS, SLOTS),
            vmem(2 * ROWS, CH, kind=F32),
            vmem(STATIONS, 128, kind=F32),
            vmem(ROWS, CH, COLS, kind=F32),
            pltpu.SemaphoreType.DMA((2, 8)),
            pltpu.SemaphoreType.DMA((2, 8)),
            pltpu.SemaphoreType.DMA((3,)),
            pltpu.SemaphoreType.DMA((3,)),
            pltpu.SemaphoreType.DMA((16,)),
            pltpu.SemaphoreType.DMA((16,)),
        ],
        compiler_params=pltpu.CompilerParams(
            collective_id=0, has_side_effects=True, vmem_limit_bytes=56 << 20
        ),
        name="whole",
    )(*operands)
    gradient, predicted = pl.pallas_call(
        back_kernel,
        out_shape=(
            jax.ShapeDtypeStruct((ROWS, CH, COLS), F32),
            jax.ShapeDtypeStruct((STATIONS, 128), F32),
        ),
        in_specs=[anywhere] * 8,
        out_specs=(anywhere, anywhere),
        scratch_shapes=[
            vmem(ROWS, CH, COLS),
            vmem(ROWS, CH, COLS, kind=F32),
            vmem(CH, DEPTH),
            vmem(2, CH, COLS),
            vmem(2, ROWS, 256),
            vmem(4, 16, 256),
            vmem(9, CH, CH),
            vmem(ROWS + 2, 3, CH, COLS),
            vmem(ROWS, CH, COLS, kind=F32),
            pltpu.SemaphoreType.DMA((20,)),
        ],
        compiler_params=pltpu.CompilerParams(vmem_limit_bytes=60 << 20),
        name="back",
    )(dpre, dfield, taps, rows, sides, corners, conv_weight, predicted)
    return predicted, jnp.transpose(gradient, (0, 2, 1))


def solution(mesh):
    return jax.shard_map(
        on_device,
        mesh=mesh,
        in_specs=(
            P("lat", "lon", None),
            P(),
            P(LAT_LON, None),
            P(LAT_LON, None),
            P(LAT_LON, None),
            P(LAT_LON),
            P(LAT_LON, None),
            P(LAT_LON),
            P(LAT_LON, None),
            P(LAT_LON),
            P(),
            P(),
            P(),
            P(),
            P(),
            P(),
        ),
        out_specs=(P(LAT_LON, None), P("lat", "lon", None)),
        check_vma=False,
    )
```
